32 devices in a mesh: group: 2 (over y), seq: 8 (over z, x), tensor: 2 (over core).
Axes of the slice: x: 2, y: 2, z: 4, core: 2. Of those that a mesh axis runs over, the one named last changes fastest.
Arguments:
- streams: bfloat16 [3, 128, 16, 2048], P(None, 'seq', 'group', 'tensor'), parts along dimension 2, may hold values from -6 to 6
- short_taps: float32 [3, 3, 2048], P(None, None, 'tensor'), may hold values from -3 to 3
- long_filters: bfloat16 [2, 128, 8, 2048], P(None, 'seq', None, 'tensor'), may hold values from -0.1875 to 0.1875
- out_grad: bfloat16 [128, 16, 2048], P('seq', 'group', 'tensor'), parts along dimension 1, may hold values from -6 to 6
Outputs:
- layer_out: bfloat16 [128, 16, 2048], P('seq', 'group', 'tensor'), parts along dimension 1
- stream_grads: bfloat16 [3, 128, 16, 2048], P(None, 'seq', 'group', 'tensor'), parts along dimension 2
- tap_grads: float32 [6, 3, 2048], P('group', None, 'tensor'), parts along dimension 0
The draws below stay inside these ranges and needn't reach their ends.
There are 2 independent parts, one for each index of `group`. The reference program is written for one: setup_inputs(seed, part) draws one part's arguments, and reference() takes and returns one part's arrays. A program takes and returns all parts, laid end to end along the dimension named above; an argument that names none is the same for every part. Nothing has to cross between parts.
All inputs are finite; a program needn't handle non-finite values.
Results may differ from the reference program's by a relative error of at most 0.0064.
Values may be sent and summed in bfloat16 or wider, within the bound.
No kernel may reach another device: no remote copies, remote signals or barrier semaphores. Data moves between devices by JAX's collectives and lax.ppermute only.
A program may use at most 64 MiB of HBM per device.

```python
import math
import jax
import jax.numpy as jnp
from jax import lax

DW = 2048
ROWS = 128
STREAMS = 3
TAPS = 3
BLOCKS = 8
SEQ = 1024


def block_scale(stream_key, dims, shards, low, high):
    level = 1.0
    for dim, parts in shards:
        steps = jax.random.uniform(jax.random.fold_in(jax.random.fold_in(stream_key, 6), dim), (parts,), jnp.float32, low / len(shards), high / len(shards))
        level = level * jnp.repeat(jnp.exp(steps), dims[dim] // parts).reshape((-1,) + (1,) * (len(dims) - 1 - dim))
    return level


def normal_values(own_key, extent, scale, reach, shards=(), held_as=jnp.bfloat16):
    values = jax.random.normal(own_key, extent, jnp.float32) * scale
    if len(shards) > 0:
        values = block_scale(own_key, extent, shards, -0.22, 0.18) * values
    return jnp.clip(values, min=-reach, max=reach).astype(held_as)


def setup_inputs(seed: int = 0, part: int = 0) -> dict:
    keys = jax.random.split(jax.random.key(seed), 5)
    own_keys = jax.random.split(jax.random.fold_in(keys[4], part), 5)
    return {
        "streams": normal_values(own_keys[0], (STREAMS, ROWS, BLOCKS, DW), 1.0, 6.0, ((1, 8), (3, 2))),
        "short_taps": normal_values(keys[1], (STREAMS, TAPS, DW), 0.6, 3.0, ((2, 2),), jnp.float32),
        "long_filters": normal_values(keys[2], (2, ROWS, BLOCKS, DW), (SEQ ** -0.5), 0.1875, ((1, 8), (3, 2))),
        "out_grad": normal_values(own_keys[3], (ROWS, BLOCKS, DW), 1.0, 6.0, ((0, 8), (2, 2))),
    }


def to_time(field):
    moved = jnp.swapaxes(field, -3, -2)
    return moved.reshape(moved.shape[:-3] + (-1, moved.shape[-1]))

def to_layout(field):
    blocked = field.reshape(field.shape[:-2] + (BLOCKS, ROWS, field.shape[-1]))
    return jnp.swapaxes(blocked, -3, -2)

def earlier(field, steps):
    padding = jnp.zeros_like(field[..., :steps, :])
    return jnp.concatenate([padding, field[..., :-steps, :]], axis=-2)

def later(field, steps):
    padding = jnp.zeros_like(field[..., :steps, :])
    return jnp.concatenate([field[..., steps:, :], padding], axis=-2)

def causal(kernel, signal):
    length = signal.shape[0]
    padded = 2 * length
    spectrum = jnp.fft.rfft(kernel, n=padded, axis=0) * jnp.fft.rfft(signal, n=padded, axis=0)
    return jnp.fft.irfft(spectrum, n=padded, axis=0)[:length]

def backwards(kernel, signal):
    return jnp.flip(causal(kernel, jnp.flip(signal, 0)), 0)

def reference(streams, short_taps, long_filters, out_grad):
    inputs = to_time(streams).astype(jnp.float32)
    prev_one = earlier(inputs, 1)
    prev_two = earlier(inputs, 2)
    tap_zero = short_taps[:, 0][:, None, :]
    tap_one = short_taps[:, 1][:, None, :]
    tap_two = short_taps[:, 2][:, None, :]
    filtered = (tap_zero * inputs + tap_one * prev_one + tap_two * prev_two).astype(jnp.bfloat16)
    filtered = filtered.astype(jnp.float32)
    value_stream = filtered[0]
    gate_one = filtered[1]
    gate_two = filtered[2]
    filters = to_time(long_filters).astype(jnp.float32)
    first_conv = causal(filters[0], value_stream)
    gated = gate_one * first_conv
    second_conv = causal(filters[1], gated)
    layer_out = (gate_two * second_conv).astype(jnp.bfloat16)
    cotangent = to_time(out_grad).astype(jnp.float32)
    back_two = cotangent * gate_two
    grad_two = cotangent * second_conv
    grad_gated = backwards(filters[1], back_two)
    grad_one = grad_gated * first_conv
    back_one = grad_gated * gate_one
    grad_value = backwards(filters[0], back_one)
    stream_cot = jnp.stack([grad_value, grad_one, grad_two]).astype(jnp.bfloat16).astype(jnp.float32)
    stream_grads = (tap_zero * stream_cot + tap_one * later(stream_cot, 1) + tap_two * later(stream_cot, 2)).astype(jnp.bfloat16)
    tap_terms = jnp.stack([lax.optimization_barrier(jnp.sum(stream_cot * inputs, axis=1)), lax.optimization_barrier(jnp.sum(stream_cot * prev_one, axis=1)), lax.optimization_barrier(jnp.sum(stream_cot * prev_two, axis=1))], axis=1)
    tap_grads = tap_terms * (1.0 / math.sqrt(SEQ))
    return (to_layout(layer_out), to_layout(stream_grads), tap_grads)
```

```python
import functools
import math

import jax
import jax.numpy as jnp
import numpy as np
from jax import lax
from jax.experimental import pallas as pl
from jax.experimental.pallas import tpu as pltpu
from jax.sharding import PartitionSpec as P

HIGHEST_PRECISION = lax.Precision.HIGHEST
BF16 = jnp.bfloat16
F32 = jnp.float32
LANES = 128
TAPS = 3
TAP_ROWS = 32
CHUNK = 16
VMEM_LIMIT = 40 * 1024 * 1024


def split_bf16(value):
    high = value.astype(BF16)
    return high, (value - high.astype(F32)).astype(BF16)


def odd_transform(parts):
    count = len(parts)
    if count == 1:
        return [(parts[0], None)]
    even = odd_transform(parts[0::2])
    odd = odd_transform(parts[1::2])
    low, high = [], []
    for j in range(count // 2):
        angle = math.pi * (2 * j + 1) / (2 * count)
        cos, sin = math.cos(angle), math.sin(angle)
        even_real, even_imag = even[j]
        odd_real, odd_imag = odd[j]
        if odd_imag is None:
            turn_real, turn_imag = odd_real * cos, odd_real * -sin
            low.append((even_real + turn_real, turn_imag))
            high.append((even_real - turn_real, turn_imag))
        else:
            turn_real = odd_real * cos + odd_imag * sin
            turn_imag = odd_imag * cos - odd_real * sin
            low.append((even_real + turn_real, even_imag + turn_imag))
            high.append((even_real - turn_real, turn_imag - even_imag))
    return low + high[::-1]


def odd_transform_back(slots):
    count = len(slots)
    if count == 1:
        return [slots[0][0]]
    even, odd = [], []
    for j in range(count // 2):
        angle = math.pi * (2 * j + 1) / (2 * count)
        cos, sin = math.cos(angle), math.sin(angle)
        low_real, low_imag = slots[j]
        high_real, high_imag = slots[count - 1 - j]
        diff_real = low_real - high_real
        sum_imag = low_imag + high_imag
        if count == 2:
            even.append((low_real + high_real, None))
            odd.append((diff_real * cos - sum_imag * sin, None))
        else:
            even.append((low_real + high_real, low_imag - high_imag))
            odd.append((diff_real * cos - sum_imag * sin, sum_imag * cos + diff_real * sin))
    even_out = odd_transform_back(even)
    odd_out = odd_transform_back(odd)
    return [part for pair in zip(even_out, odd_out) for part in pair]


def transform_tables(blocks, rows):
    length = blocks * rows
    slot = np.arange(blocks)[:, None, None]
    freq = np.arange(rows)[None, :, None]
    pos = np.arange(rows)[None, None, :]
    number = ((2 * slot + 1 + 4 * blocks * freq) * pos) % (4 * length)
    angle = number * (np.pi / (2 * length))
    cos, sin = np.cos(angle), np.sin(angle)
    forward = np.concatenate(
        [np.concatenate([cos, sin], axis=2), np.concatenate([-sin, cos], axis=2)], axis=1
    )
    back = np.swapaxes(forward, 1, 2) / length

    def halves(table):
        high = table.astype(BF16)
        low = (table - high.astype(np.float64)).astype(BF16)
        return np.concatenate([high, low], axis=1)

    return halves(forward), halves(back)


def shift_blocks(edge, blocks, by):
    rolled = pltpu.roll(edge, by % edge.shape[0], 0)
    block = lax.broadcasted_iota(jnp.int32, edge.shape, 0) % blocks
    empty = 0 if by > 0 else blocks - 1
    return jnp.where(block == empty, 0.0, rolled)


def pack_kernel(me_ref, streams_ref, filters_ref, grad_ref, *out_refs):
    slab = grad_ref.shape[0]
    partners = len(out_refs) - 2
    me = me_ref[0]
    for k in range(partners):
        lanes = pl.ds(pl.multiple_of((me ^ k) * LANES, LANES), LANES)
        out_refs[k][0 : 3 * slab] = streams_ref[:, lanes]
        out_refs[k][3 * slab : 5 * slab] = filters_ref[:, lanes]
        out_refs[k][5 * slab : 6 * slab] = grad_ref[:, lanes]
    edge = out_refs[partners].shape[0]
    out_refs[partners][...] = streams_ref[3 * slab - edge : 3 * slab]
    out_refs[partners + 1][...] = grad_ref[0:edge]


def core_kernel(blocks, partners, me_ref, *refs):
    msgs = refs[:partners]
    taps_ref, fwd_ref, back_ref = refs[partners : partners + 3]
    outs = refs[partners + 3 : 2 * partners + 3]
    raw, sig, gate, grad, zh, zl, spec, turned, cot, conv, grads = refs[2 * partners + 3 :]
    me = me_ref[0]
    total = sig.shape[1]
    rows = total // blocks
    slab = total // partners
    halo = (TAPS - 1) * blocks
    lanes = pl.ds(pl.multiple_of(me * LANES, LANES), LANES)
    weights = taps_ref[:, lanes]

    def weight(stream, tap):
        return weights[stream * TAPS + tap : stream * TAPS + tap + 1]

    for k in range(partners):
        start = pl.multiple_of((me ^ k) * slab, slab)
        for s in range(3):
            raw[s, pl.ds(halo + start, slab)] = msgs[k][s * slab : (s + 1) * slab].astype(F32)
        sig[2, pl.ds(start, slab)] = msgs[k][3 * slab : 4 * slab].astype(F32)
        sig[3, pl.ds(start, slab)] = msgs[k][4 * slab : 5 * slab].astype(F32)
        grad[pl.ds(start, slab)] = msgs[k][5 * slab : 6 * slab].astype(F32)
    for s in range(3):
        raw[s, 0:halo] = shift_blocks(raw[s, total : total + halo], blocks, 1)

    @pl.loop(0, total // slab)
    def _(step):
        base = pl.multiple_of(step * slab, slab)

        def filtered(s):
            now = raw[s, pl.ds(base + 2 * blocks, slab)]
            prev_one = raw[s, pl.ds(base + blocks, slab)]
            prev_two = raw[s, pl.ds(base, slab)]
            both = weight(s, 0) * now + weight(s, 1) * prev_one + weight(s, 2) * prev_two
            return both.astype(BF16).astype(F32)

        sig[0, pl.ds(base, slab)] = filtered(0)
        gate[pl.ds(base, slab)] = filtered(1)
        sig[1, pl.ds(base, slab)] = filtered(2) * grad[pl.ds(base, slab)]

    def store_slots(parts, row, col):
        for j, (real, imag) in enumerate(odd_transform(parts)):
            for at, value in ((row, real), (rows + row, imag)):
                high, low = split_bf16(value)
                zh[j, pl.ds(at, CHUNK), col : col + LANES] = high
                zl[j, pl.ds(at, CHUNK), col : col + LANES] = low

    def times(table, j, high, low):
        size = 2 * rows
        main = jnp.dot(table[j, 0:size], high, preferred_element_type=F32)
        main += jnp.dot(table[j, 0:size], low, preferred_element_type=F32)
        return main + jnp.dot(table[j, size : 2 * size], high, preferred_element_type=F32)

    @pl.loop(0, rows // CHUNK)
    def _(step):
        row = pl.multiple_of(step * CHUNK, CHUNK)
        for s in range(4):
            parts = [
                sig[s, pl.ds(row * blocks + b, CHUNK, stride=blocks)] for b in range(blocks)
            ]
            store_slots(parts, row, s * LANES)

    def products(data, first, second):
        real, imag = data[:rows], data[rows:]
        a_real, a_imag = real[:, :LANES], imag[:, :LANES]
        c_real, c_imag = real[:, LANES:], imag[:, LANES:]
        (f_real, f_imag), (s_real, s_imag) = first, second
        left = jnp.concatenate(
            [a_real * f_real - a_imag * f_imag, a_real * f_imag + a_imag * f_real], axis=0
        )
        right = jnp.concatenate(
            [c_real * s_real + c_imag * s_imag, c_imag * s_real - c_real * s_imag], axis=0
        )
        return jnp.concatenate([left, right], axis=1)

    def filter_spec(j, f):
        cols = slice(f * LANES, (f + 1) * LANES)
        return spec[j, 0:rows, cols], spec[j, rows : 2 * rows, cols]

    @pl.loop(0, blocks)
    def _(j):
        data = times(fwd_ref, j, zh[j], zl[j])
        spec[j] = data[:, 2 * LANES :]
        high, low = split_bf16(
            products(data[:, : 2 * LANES], filter_spec(j, 0), filter_spec(j, 1))
        )
        turned[j] = times(back_ref, j, high, low)

    def blocks_of(row, col):
        return odd_transform_back(
            [
                (
                    turned[j, pl.ds(row, CHUNK), col : col + LANES],
                    turned[j, pl.ds(rows + row, CHUNK), col : col + LANES],
                )
                for j in range(blocks)
            ]
        )

    @pl.loop(0, rows // CHUNK)
    def _(step):
        row = pl.multiple_of(step * CHUNK, CHUNK)
        first = blocks_of(row, 0)
        gated_grad = blocks_of(row, LANES)
        forward, backward = [], []
        for b in range(blocks):
            place = pl.ds(row * blocks + b, CHUNK, stride=blocks)
            gate_one = gate[place]
            cot[1, place] = (gated_grad[b] * first[b]).astype(BF16).astype(F32)
            forward.append(gate_one * first[b])
            backward.append(gate_one * gated_grad[b])
        store_slots(forward, row, 0)
        store_slots(backward, row, LANES)

    @pl.loop(0, blocks)
    def _(j):
        data = times(fwd_ref, j, zh[j, :, : 2 * LANES], zl[j, :, : 2 * LANES])
        high, low = split_bf16(products(data, filter_spec(j, 1), filter_spec(j, 0)))
        turned[j] = times(back_ref, j, high, low)

    @pl.loop(0, rows // CHUNK)
    def _(step):
        row = pl.multiple_of(step * CHUNK, CHUNK)
        second = blocks_of(row, 0)
        value_grad = blocks_of(row, LANES)
        for b in range(blocks):
            place = pl.ds(row * blocks + b, CHUNK, stride=blocks)
            conv[place] = second[b]
            cot[0, place] = value_grad[b].astype(BF16).astype(F32)

    conv[total : total + halo] = shift_blocks(conv[0:halo], blocks, -1)
    for s in range(2):
        cot[s, total : total + halo] = shift_blocks(cot[s, 0:halo], blocks, -1)

    def finish(step, sums):
        base = pl.multiple_of(step * slab, slab)
        here = [cot[s, pl.ds(base, slab)] for s in range(2)]
        last = grad[pl.ds(base, slab)] * conv[pl.ds(base, slab)]
        here.append(last.astype(BF16).astype(F32))
        for s in range(2):
            next_one = cot[s, pl.ds(base + blocks, slab)]
            next_two = cot[s, pl.ds(base + 2 * blocks, slab)]
            grads[s, pl.ds(base, slab)] = (
                weight(s, 0) * here[s] + weight(s, 1) * next_one + weight(s, 2) * next_two
            ).astype(BF16)
        added = []
        for s in range(3):
            for tap in range(TAPS):
                term = here[s] * raw[s, pl.ds(base + (TAPS - 1 - tap) * blocks, slab)]
                added.append(jnp.sum(term.reshape(slab // 8, 8, LANES), axis=0))
        return tuple(a + b for a, b in zip(sums, added))

    zeros = tuple(jnp.zeros((8, LANES), F32) for _ in range(3 * TAPS))
    sums = lax.fori_loop(0, total // slab, finish, zeros)
    scale = 1.0 / math.sqrt(total)
    tap_rows = [jnp.sum(part, axis=0, keepdims=True) * scale for part in sums]
    term = jnp.concatenate(tap_rows, axis=0)
    terms = []
    for _ in range(3):
        high, _ = split_bf16(term)
        terms.append(high.astype(F32))
        term = term - terms[-1]
    pad = jnp.zeros((TAP_ROWS - 9 * TAPS, LANES), F32)
    tap_block = jnp.concatenate(terms + [pad], axis=0).astype(BF16)
    for k in range(partners):
        start = pl.multiple_of((me ^ k) * slab, slab)
        outs[k][0 : slab + halo] = conv[pl.ds(start, slab + halo)].astype(BF16)
        for s in range(2):
            at = slab + halo + s * slab
            outs[k][at : at + slab] = grads[s, pl.ds(start, slab)]
        outs[k][3 * slab + halo :] = tap_block


def home_kernel(blocks, partners, me_ref, *refs):
    msgs = refs[:partners]
    stream_ref, grad_ref, prev_ref, next_ref, taps_ref = refs[partners : partners + 5]
    layer_ref, grads_ref, tap_ref = refs[partners + 5 :]
    me = me_ref[0]
    slab = stream_ref.shape[0]
    halo = (TAPS - 1) * blocks
    for k in range(partners):
        lanes = pl.ds(pl.multiple_of((me ^ k) * LANES, LANES), LANES)
        msg = msgs[k]
        conv = msg[0 : slab + halo].astype(F32)
        weights = taps_ref[:, lanes]
        tap = [weights[2 * TAPS + j : 2 * TAPS + j + 1] for j in range(TAPS)]
        before = prev_ref[:, lanes].astype(F32)
        before = jnp.where(me == 0, shift_blocks(before, blocks, 1), before)
        stream = jnp.concatenate([before, stream_ref[:, lanes].astype(F32)], axis=0)
        gate = tap[0] * stream[halo:] + tap[1] * stream[blocks : blocks + slab]
        gate = (gate + tap[2] * stream[:slab]).astype(BF16).astype(F32)
        layer_ref[:, lanes] = (gate * conv[:slab]).astype(BF16)
        after = next_ref[:, lanes].astype(F32)
        after = jnp.where(me == partners - 1, shift_blocks(after, blocks, -1), after)
        cot = jnp.concatenate([grad_ref[:, lanes].astype(F32), after], axis=0) * conv
        cot = cot.astype(BF16).astype(F32)
        last = tap[0] * cot[:slab] + tap[1] * cot[blocks : blocks + slab]
        grads_ref[2 * slab : 3 * slab, lanes] = (last + tap[2] * cot[halo:]).astype(BF16)
        grads_ref[0 : 2 * slab, lanes] = msg[slab + halo : 3 * slab + halo]
        block = msg[3 * slab + halo :].astype(F32)
        size = 3 * TAPS
        tap_ref[:, lanes] = block[:size] + block[size : 2 * size] + block[2 * size : 3 * size]


def traded(messages, count):
    order = sorted(range(1, count), key=lambda k: -k)
    out = {0: messages[0]}
    for k in order:
        pairs = [(i, i ^ k) for i in range(count)]
        out[k] = lax.ppermute(messages[k], "seq", pairs)
    return [out[k] for k in range(count)]


def whole_specs(count):
    return [pl.BlockSpec(memory_space=pltpu.VMEM) for _ in range(count)]


def short_local(streams, short_taps, long_filters, out_grad):
    count = lax.axis_size("seq")
    me = lax.axis_index("seq").astype(jnp.int32)
    place = me[None]
    _, local_rows, blocks, channels = streams.shape
    slab = local_rows * blocks
    total = slab * count
    rows = local_rows * count
    halo = (TAPS - 1) * blocks
    flat_streams = streams.reshape(3 * slab, channels)
    flat_filters = long_filters.reshape(2 * slab, channels)
    flat_grad = out_grad.reshape(slab, channels)
    flat_taps = short_taps.reshape(3 * TAPS, channels)
    scalar = pl.BlockSpec(memory_space=pltpu.SMEM)
    params = pltpu.CompilerParams(vmem_limit_bytes=VMEM_LIMIT)

    def shape(*dims, dtype=BF16):
        return jax.ShapeDtypeStruct(dims, dtype)

    packed = pl.pallas_call(
        pack_kernel,
        out_shape=[shape(6 * slab, LANES)] * count + [shape(halo, channels)] * 2,
        in_specs=[scalar] + whole_specs(3),
        out_specs=whole_specs(count + 2),
        compiler_params=params,
        name="pack",
    )(place, flat_streams, flat_filters, flat_grad)
    arrived = traded(packed[:count], count)
    before = lax.ppermute(packed[count], "seq", [(i, (i + 1) % count) for i in range(count)])
    after = lax.ppermute(packed[count + 1], "seq", [(i, (i - 1) % count) for i in range(count)])

    forward, back = transform_tables(blocks, rows)
    answer_rows = 3 * slab + halo + TAP_ROWS
    answers = pl.pallas_call(
        functools.partial(core_kernel, blocks, count),
        out_shape=[shape(answer_rows, LANES)] * count,
        in_specs=[scalar] + whole_specs(count + 3),
        out_specs=whole_specs(count),
        scratch_shapes=[
            pltpu.VMEM((3, halo + total, LANES), F32),
            pltpu.VMEM((4, total, LANES), F32),
            pltpu.VMEM((total, LANES), F32),
            pltpu.VMEM((total, LANES), F32),
            pltpu.VMEM((blocks, 2 * rows, 4 * LANES), BF16),
            pltpu.VMEM((blocks, 2 * rows, 4 * LANES), BF16),
            pltpu.VMEM((blocks, 2 * rows, 2 * LANES), F32),
            pltpu.VMEM((blocks, 2 * rows, 2 * LANES), F32),
            pltpu.VMEM((2, total + halo, LANES), F32),
            pltpu.VMEM((total + halo, LANES), F32),
            pltpu.VMEM((2, total, LANES), BF16),
        ],
        compiler_params=params,
        name="core",
    )(place, *arrived, flat_taps, jnp.asarray(forward), jnp.asarray(back))
    returned = traded(answers, count)

    layer_out, stream_grads, tap_grads = pl.pallas_call(
        functools.partial(home_kernel, blocks, count),
        out_shape=[
            shape(slab, channels),
            shape(3 * slab, channels),
            shape(3 * TAPS, channels, dtype=F32),
        ],
        in_specs=[scalar] + whole_specs(count + 5),
        out_specs=whole_specs(3),
        compiler_params=params,
        name="home",
    )(place, *returned, flat_streams[2 * slab :], flat_grad, before, after, flat_taps)
    return (
        layer_out.reshape(out_grad.shape),
        stream_grads.reshape(streams.shape),
        tap_grads.reshape(short_taps.shape),
    )


def shifted(value, axis, by):
    count = lax.axis_size(axis)
    return lax.ppermute(value, axis, [(i, (i + by) % count) for i in range(count)])


def complex_product(left_real, left_imag, right_real, right_imag):
    return (
        left_real * right_real - left_imag * right_imag,
        left_real * right_imag + left_imag * right_real,
    )


def conj_product(left_real, left_imag, right_real, right_imag):
    return (
        left_real * right_real + left_imag * right_imag,
        left_real * right_imag - left_imag * right_real,
    )


def long_local(streams, short_taps, long_filters, out_grad):
    seq_count = lax.axis_size("seq")
    seq_place = lax.axis_index("seq")
    local_rows = streams.shape[1]
    channels = streams.shape[3]
    block_rows = local_rows * seq_count
    full_length = 2 * block_rows * seq_count
    angle_unit = math.pi / full_length
    block_pos = jnp.arange(seq_count, dtype=jnp.int32)
    odd_slots = 2 * block_pos + 1
    local_index = seq_place * local_rows + jnp.arange(local_rows, dtype=jnp.int32)
    row_pos = jnp.arange(block_rows, dtype=jnp.int32)
    start_pos = block_pos[None, :, None] * block_rows + local_index[:, None, None]
    fwd_angle = (start_pos * odd_slots[None, None, :] % (2 * full_length)).astype(
        jnp.float32
    ) * angle_unit
    fwd_table = jnp.stack([jnp.cos(fwd_angle), -jnp.sin(fwd_angle)], axis=-1)
    inner_angle = (row_pos[:, None] * row_pos[None, :] % block_rows).astype(jnp.float32) * (
        2.0 * math.pi / block_rows
    )
    inner_cos = jnp.cos(inner_angle)
    inner_sin = jnp.sin(inner_angle)
    inner_table = jnp.stack(
        [jnp.stack([inner_cos, -inner_sin], axis=-1), jnp.stack([inner_sin, inner_cos], axis=-1)],
        axis=0,
    )
    back_num = (
        row_pos[None, :]
        * (4 * seq_count * row_pos[:, None] + 2 * seq_place + 1)
        % (2 * full_length)
    )
    back_angle = back_num.astype(jnp.float32) * angle_unit
    back_cos = jnp.cos(back_angle)
    back_sin = jnp.sin(back_angle)
    back_table = jnp.stack(
        [jnp.stack([back_cos, back_sin], axis=-1), jnp.stack([-back_sin, back_cos], axis=-1)],
        axis=0,
    )
    outer_angle = (block_pos[:, None] * odd_slots[None, :] % (4 * seq_count)).astype(
        jnp.float32
    ) * (math.pi / (2 * seq_count))
    outer_table = jnp.stack([jnp.cos(outer_angle).T, -jnp.sin(outer_angle).T], axis=0)

    def previous_rows(block):
        edge = shifted(block[:, -1:], "seq", 1)
        rolled = jnp.concatenate([jnp.zeros_like(edge[:, :, :1]), edge[:, :, :-1]], axis=2)
        edge = jnp.where(seq_place == 0, rolled, edge)
        return jnp.concatenate([edge, block[:, :-1]], axis=1)

    def next_rows(block):
        edge = shifted(block[:, :1], "seq", -1)
        rolled = jnp.concatenate([edge[:, :, 1:], jnp.zeros_like(edge[:, :, :1])], axis=2)
        edge = jnp.where(seq_place == seq_count - 1, rolled, edge)
        return jnp.concatenate([block[:, 1:], edge], axis=1)

    def spectra(signals):
        count = signals.shape[0]
        twisted = jnp.einsum("simc,imjr->srijc", signals, fwd_table, precision=HIGHEST_PRECISION)
        slotted = lax.all_to_all(twisted, "seq", split_axis=3, concat_axis=2, tiled=True)
        slotted = slotted.reshape(count, 2, block_rows, channels)
        spec = jnp.einsum("sric,rikq->sqkc", slotted, inner_table, precision=HIGHEST_PRECISION)
        return (spec[:, 0], spec[:, 1])

    def signals_back(real_spec, imag_spec):
        count = real_spec.shape[0]
        stacked = jnp.stack([real_spec, imag_spec], axis=1)
        turned = jnp.einsum("srkc,rkiq->sqic", stacked, back_table, precision=HIGHEST_PRECISION)
        turned = turned.reshape(count, 2, block_rows, 1, channels)
        parts = lax.all_to_all(turned, "seq", split_axis=2, concat_axis=3, tiled=True)
        rows_out = jnp.einsum("srijc,rjm->simc", parts, outer_table, precision=HIGHEST_PRECISION)
        return rows_out * (2.0 / full_length)

    def tap_weight(index):
        return short_taps[:, index][:, None, None, :]

    prev_one = previous_rows(streams)
    prev_two = previous_rows(prev_one)
    filtered = (
        tap_weight(0) * streams + tap_weight(1) * prev_one + tap_weight(2) * prev_two
    ).astype(jnp.bfloat16)
    value_stream = filtered[0].astype(jnp.float32)
    gate_one = filtered[1].astype(jnp.float32)
    gate_two = filtered[2].astype(jnp.float32)
    filters = long_filters.astype(jnp.float32)
    real_first, imag_first = spectra(jnp.stack([value_stream, filters[0]]))
    product_one = complex_product(real_first[0], imag_first[0], real_first[1], imag_first[1])
    first_conv = signals_back(product_one[0][None], product_one[1][None])[0]
    gated_first = gate_one * first_conv
    real_second, imag_second = spectra(jnp.stack([gated_first, filters[1]]))
    product_two = complex_product(real_second[0], imag_second[0], real_second[1], imag_second[1])
    second_conv = signals_back(product_two[0][None], product_two[1][None])[0]
    layer_out = (gate_two * second_conv).astype(jnp.bfloat16)
    cotangent = out_grad.astype(jnp.float32)
    back_two = cotangent * gate_two
    grad_two = cotangent * second_conv
    real_third, imag_third = spectra(back_two[None])
    filter_two_real, filter_two_imag = (real_second[1], imag_second[1])
    correlated_two = conj_product(filter_two_real, filter_two_imag, real_third[0], imag_third[0])
    grad_gated = signals_back(correlated_two[0][None], correlated_two[1][None])[0]
    grad_one = grad_gated * first_conv
    back_one = grad_gated * gate_one
    real_fourth, imag_fourth = spectra(back_one[None])
    filter_one_real, filter_one_imag = (real_first[1], imag_first[1])
    correlated_one = conj_product(filter_one_real, filter_one_imag, real_fourth[0], imag_fourth[0])
    grad_value = signals_back(correlated_one[0][None], correlated_one[1][None])[0]
    stream_cot = jnp.stack([grad_value, grad_one, grad_two]).astype(jnp.bfloat16)
    next_one = next_rows(stream_cot)
    next_two = next_rows(next_one)
    stream_grads = (
        tap_weight(0) * stream_cot + tap_weight(1) * next_one + tap_weight(2) * next_two
    ).astype(jnp.bfloat16)
    cot_float = stream_cot.astype(jnp.float32)
    tap_terms = jnp.stack(
        [
            jnp.sum(cot_float * streams, axis=(1, 2)),
            jnp.sum(cot_float * prev_one, axis=(1, 2)),
            jnp.sum(cot_float * prev_two, axis=(1, 2)),
        ],
        axis=1,
    )
    tap_total = lax.psum(tap_terms, "seq")
    return (layer_out, stream_grads, tap_total * (1.0 / math.sqrt(block_rows * seq_count)))


def local(streams, short_taps, long_filters, out_grad):
    count = lax.axis_size("seq")
    _, local_rows, blocks, channels = streams.shape
    rows = local_rows * count
    fits = (
        channels == LANES * count
        and count & (count - 1) == 0
        and blocks == 8
        and rows == LANES
        and local_rows >= TAPS - 1
    )
    work = short_local if fits else long_local
    return work(streams, short_taps, long_filters, out_grad)


def solution(mesh):
    in_specs = (
        P(None, "seq", "group", "tensor"),
        P(None, None, "tensor"),
        P(None, "seq", None, "tensor"),
        P("seq", "group", "tensor"),
    )
    out_specs = (
        P("seq", "group", "tensor"),
        P(None, "seq", "group", "tensor"),
        P("group", None, "tensor"),
    )
    return jax.shard_map(local, mesh=mesh, in_specs=in_specs, out_specs=out_specs, check_vma=False)
```

```python
import functools
import math

import jax
import jax.numpy as jnp
import numpy as np
from jax import lax
from jax.experimental import pallas as pl
from jax.experimental.pallas import tpu as pltpu
from jax.sharding import PartitionSpec as P

HIGHEST_PRECISION = lax.Precision.HIGHEST
BF16 = jnp.bfloat16
F32 = jnp.float32
LANES = 128
TAPS = 3
TAP_ROWS = 16
CHUNK = 16
VMEM_LIMIT = 40 * 1024 * 1024


def split_bf16(value):
    high = value.astype(BF16)
    return high, (value - high.astype(F32)).astype(BF16)


def odd_transform(parts):
    count = len(parts)
    if count == 1:
        return [(parts[0], None)]
    even = odd_transform(parts[0::2])
    odd = odd_transform(parts[1::2])
    low, high = [], []
    for j in range(count // 2):
        angle = math.pi * (2 * j + 1) / (2 * count)
        cos, sin = math.cos(angle), math.sin(angle)
        even_real, even_imag = even[j]
        odd_real, odd_imag = odd[j]
        if odd_imag is None:
            turn_real, turn_imag = odd_real * cos, odd_real * -sin
            low.append((even_real + turn_real, turn_imag))
            high.append((even_real - turn_real, turn_imag))
        else:
            turn_real = odd_real * cos + odd_imag * sin
            turn_imag = odd_imag * cos - odd_real * sin
            low.append((even_real + turn_real, even_imag + turn_imag))
            high.append((even_real - turn_real, turn_imag - even_imag))
    return low + high[::-1]


def odd_transform_back(slots):
    count = len(slots)
    if count == 1:
        return [slots[0][0]]
    even, odd = [], []
    for j in range(count // 2):
        angle = math.pi * (2 * j + 1) / (2 * count)
        cos, sin = math.cos(angle), math.sin(angle)
        low_real, low_imag = slots[j]
        high_real, high_imag = slots[count - 1 - j]
        diff_real = low_real - high_real
        sum_imag = low_imag + high_imag
        if count == 2:
            even.append((low_real + high_real, None))
            odd.append((diff_real * cos - sum_imag * sin, None))
        else:
            even.append((low_real + high_real, low_imag - high_imag))
            odd.append((diff_real * cos - sum_imag * sin, sum_imag * cos + diff_real * sin))
    even_out = odd_transform_back(even)
    odd_out = odd_transform_back(odd)
    return [part for pair in zip(even_out, odd_out) for part in pair]


def transform_tables(blocks, rows):
    length = blocks * rows
    slot = np.arange(blocks)[:, None, None]
    freq = np.arange(rows)[None, :, None]
    pos = np.arange(rows)[None, None, :]
    number = ((2 * slot + 1 + 4 * blocks * freq) * pos) % (4 * length)
    angle = number * (np.pi / (2 * length))
    cos, sin = np.cos(angle), np.sin(angle)
    forward = np.concatenate(
        [np.concatenate([cos, sin], axis=2), np.concatenate([-sin, cos], axis=2)], axis=1
    )
    back = np.swapaxes(forward, 1, 2) / length

    def halves(table):
        high = table.astype(BF16)
        low = (table - high.astype(np.float64)).astype(BF16)
        return np.concatenate([high, low], axis=1)

    return halves(forward), halves(back)


def shift_blocks(edge, blocks, by):
    rolled = pltpu.roll(edge, by % edge.shape[0], 0)
    block = lax.broadcasted_iota(jnp.int32, edge.shape, 0) % blocks
    empty = 0 if by > 0 else blocks - 1
    return jnp.where(block == empty, 0.0, rolled)


def pack_kernel(me_ref, streams_ref, filters_ref, grad_ref, *refs):
    outs, sems = refs[:-1], refs[-1]
    slab = grad_ref.shape[0]
    me = me_ref[0]
    copies = []
    for k, out in enumerate(outs):
        lanes = pl.ds(pl.multiple_of((me ^ k) * LANES, LANES), LANES)
        at = 0
        for part, source in enumerate((streams_ref, filters_ref, grad_ref)):
            size = source.shape[0]
            copies.append(
                pltpu.make_async_copy(
                    source.at[:, lanes], out.at[pl.ds(at, size)], sems.at[k, part]
                )
            )
            at += size
    for copy in copies:
        copy.start()
    for copy in copies:
        copy.wait()


def core_kernel(blocks, partners, me_ref, *refs):
    msgs = refs[:partners]
    taps_ref, fwd_hbm, back_hbm = refs[partners : partners + 3]
    outs = refs[partners + 3 : 2 * partners + 3]
    scratch = refs[2 * partners + 3 :]
    raw, sig, gate, grad, zh, zl, spec, turned, cot, conv, grads = scratch[:11]
    fwd_ref, back_ref, sems = scratch[11:]
    fetches = [
        pltpu.make_async_copy(fwd_hbm, fwd_ref, sems.at[0]),
        pltpu.make_async_copy(back_hbm, back_ref, sems.at[1]),
    ]
    for fetch in fetches:
        fetch.start()
    me = me_ref[0]
    total = sig.shape[1]
    rows = total // blocks
    slab = total // partners
    halo = (TAPS - 1) * blocks
    lanes = pl.ds(pl.multiple_of(me * LANES, LANES), LANES)

    def weight(stream, tap):
        return taps_ref[stream, tap : tap + 1, lanes]

    for k in range(partners):
        start = pl.multiple_of((me ^ k) * slab, slab)
        for s in range(3):
            raw[s, pl.ds(halo + start, slab)] = msgs[k][s * slab : (s + 1) * slab].astype(F32)
        sig[2, pl.ds(start, slab)] = msgs[k][3 * slab : 4 * slab].astype(F32)
        sig[3, pl.ds(start, slab)] = msgs[k][4 * slab : 5 * slab].astype(F32)
        grad[pl.ds(start, slab)] = msgs[k][5 * slab : 6 * slab].astype(F32)
    for s in range(3):
        raw[s, 0:halo] = shift_blocks(raw[s, total : total + halo], blocks, 1)

    @pl.loop(0, total // slab)
    def _(step):
        base = pl.multiple_of(step * slab, slab)

        def filtered(s):
            now = raw[s, pl.ds(base + 2 * blocks, slab)]
            prev_one = raw[s, pl.ds(base + blocks, slab)]
            prev_two = raw[s, pl.ds(base, slab)]
            both = weight(s, 0) * now + weight(s, 1) * prev_one + weight(s, 2) * prev_two
            return both.astype(BF16).astype(F32)

        sig[0, pl.ds(base, slab)] = filtered(0)
        gate[pl.ds(base, slab)] = filtered(1)
        sig[1, pl.ds(base, slab)] = filtered(2) * grad[pl.ds(base, slab)]

    def store_slots(parts, row, col):
        for j, (real, imag) in enumerate(odd_transform(parts)):
            for at, value in ((row, real), (rows + row, imag)):
                high, low = split_bf16(value)
                zh[j, pl.ds(at, CHUNK), col : col + LANES] = high
                zl[j, pl.ds(at, CHUNK), col : col + LANES] = low

    def times(table, j, high, low):
        size = 2 * rows
        main = jnp.dot(table[j, 0:size], high, preferred_element_type=F32)
        main += jnp.dot(table[j, 0:size], low, preferred_element_type=F32)
        return main + jnp.dot(table[j, size : 2 * size], high, preferred_element_type=F32)

    @pl.loop(0, rows // CHUNK)
    def _(step):
        row = pl.multiple_of(step * CHUNK, CHUNK)
        for s in range(4):
            parts = [
                sig[s, pl.ds(row * blocks + b, CHUNK, stride=blocks)] for b in range(blocks)
            ]
            store_slots(parts, row, s * LANES)

    def products(data, first, second):
        real, imag = data[:rows], data[rows:]
        a_real, a_imag = real[:, :LANES], imag[:, :LANES]
        c_real, c_imag = real[:, LANES:], imag[:, LANES:]
        (f_real, f_imag), (s_real, s_imag) = first, second
        left = jnp.concatenate(
            [a_real * f_real - a_imag * f_imag, a_real * f_imag + a_imag * f_real], axis=0
        )
        right = jnp.concatenate(
            [c_real * s_real + c_imag * s_imag, c_imag * s_real - c_real * s_imag], axis=0
        )
        return jnp.concatenate([left, right], axis=1)

    def filter_spec(j, f):
        cols = slice(f * LANES, (f + 1) * LANES)
        return spec[j, 0:rows, cols], spec[j, rows : 2 * rows, cols]

    for fetch in fetches:
        fetch.wait()

    @pl.loop(0, blocks)
    def _(j):
        data = times(fwd_ref, j, zh[j], zl[j])
        spec[j] = data[:, 2 * LANES :]
        high, low = split_bf16(
            products(data[:, : 2 * LANES], filter_spec(j, 0), filter_spec(j, 1))
        )
        turned[j] = times(back_ref, j, high, low)

    def blocks_of(row, col):
        return odd_transform_back(
            [
                (
                    turned[j, pl.ds(row, CHUNK), col : col + LANES],
                    turned[j, pl.ds(rows + row, CHUNK), col : col + LANES],
                )
                for j in range(blocks)
            ]
        )

    @pl.loop(0, rows // CHUNK)
    def _(step):
        row = pl.multiple_of(step * CHUNK, CHUNK)
        first = blocks_of(row, 0)
        gated_grad = blocks_of(row, LANES)
        forward, backward = [], []
        for b in range(blocks):
            place = pl.ds(row * blocks + b, CHUNK, stride=blocks)
            gate_one = gate[place]
            cot[1, place] = (gated_grad[b] * first[b]).astype(BF16).astype(F32)
            forward.append(gate_one * first[b])
            backward.append(gate_one * gated_grad[b])
        store_slots(forward, row, 0)
        store_slots(backward, row, LANES)

    @pl.loop(0, blocks)
    def _(j):
        data = times(fwd_ref, j, zh[j, :, : 2 * LANES], zl[j, :, : 2 * LANES])
        high, low = split_bf16(products(data, filter_spec(j, 1), filter_spec(j, 0)))
        turned[j] = times(back_ref, j, high, low)

    @pl.loop(0, rows // CHUNK)
    def _(step):
        row = pl.multiple_of(step * CHUNK, CHUNK)
        second = blocks_of(row, 0)
        value_grad = blocks_of(row, LANES)
        for b in range(blocks):
            place = pl.ds(row * blocks + b, CHUNK, stride=blocks)
            conv[place] = second[b]
            cot[0, place] = value_grad[b].astype(BF16).astype(F32)

    for s in range(2):
        cot[s, total : total + halo] = shift_blocks(cot[s, 0:halo], blocks, -1)

    def finish(step, sums):
        base = pl.multiple_of(step * slab, slab)
        here = [cot[s, pl.ds(base, slab)] for s in range(2)]
        last = (grad[pl.ds(base, slab)] * conv[pl.ds(base, slab)]).astype(BF16).astype(F32)
        cot[2, pl.ds(base, slab)] = last
        here.append(last)
        for s in range(2):
            next_one = cot[s, pl.ds(base + blocks, slab)]
            next_two = cot[s, pl.ds(base + 2 * blocks, slab)]
            grads[s, pl.ds(base, slab)] = (
                weight(s, 0) * here[s] + weight(s, 1) * next_one + weight(s, 2) * next_two
            ).astype(BF16)
        added = []
        for s in range(3):
            for tap in range(TAPS):
                term = here[s] * raw[s, pl.ds(base + (TAPS - 1 - tap) * blocks, slab)]
                added.append(jnp.sum(term.reshape(slab // 8, 8, LANES), axis=0))
        return tuple(a + b for a, b in zip(sums, added))

    zeros = tuple(jnp.zeros((8, LANES), F32) for _ in range(3 * TAPS))
    sums = lax.fori_loop(0, total // slab, finish, zeros)
    cot[2, total : total + halo] = shift_blocks(cot[2, 0:halo], blocks, -1)
    scale = 1.0 / math.sqrt(total)
    tap_rows = [jnp.sum(part, axis=0, keepdims=True) * scale for part in sums]
    pad = jnp.zeros((TAP_ROWS - 3 * TAPS, LANES), F32)
    tap_block = jnp.concatenate(tap_rows + [pad], axis=0).astype(BF16)
    for k in range(partners):
        start = pl.multiple_of((me ^ k) * slab, slab)
        outs[k][0:slab] = conv[pl.ds(start, slab)].astype(BF16)
        for s in range(2):
            at = (s + 1) * slab
            outs[k][at : at + slab] = grads[s, pl.ds(start, slab)]
        at = 3 * slab
        now, prev_one, prev_two = (raw[2, pl.ds(start + j * blocks, halo)] for j in (2, 1, 0))
        gate_two = weight(2, 0) * now + weight(2, 1) * prev_one + weight(2, 2) * prev_two
        first = gate_two.astype(BF16).astype(F32) * conv[pl.ds(start, halo)]
        outs[k][at : at + halo] = first.astype(BF16)
        at += halo
        begin = start + slab - halo
        now, next_one, next_two = (cot[2, pl.ds(begin + j * blocks, halo)] for j in range(TAPS))
        end = weight(2, 0) * now + weight(2, 1) * next_one + weight(2, 2) * next_two
        outs[k][at : at + halo] = end.astype(BF16)
        at += halo
        outs[k][at:] = tap_block


def home_kernel(blocks, partners, me_ref, *refs):
    msgs = refs[:partners]
    stream_ref, grad_ref, taps_ref = refs[partners : partners + 3]
    layer_ref, grads_ref, tap_ref = refs[partners + 3 :]
    me = me_ref[0]
    slab = stream_ref.shape[0]
    halo = (TAPS - 1) * blocks
    rest = slab - halo
    for k in range(partners):
        lanes = pl.ds(pl.multiple_of((me ^ k) * LANES, LANES), LANES)
        msg = msgs[k]
        conv = msg[0:slab].astype(F32)
        tap = [taps_ref[2, j : j + 1, lanes] for j in range(TAPS)]
        stream = stream_ref[:, lanes].astype(F32)
        gate = tap[0] * stream[halo:] + tap[1] * stream[blocks : blocks + rest]
        gate = (gate + tap[2] * stream[:rest]).astype(BF16).astype(F32)
        layer_ref[0:halo, lanes] = msg[3 * slab : 3 * slab + halo]
        layer_ref[halo:slab, lanes] = (gate * conv[halo:]).astype(BF16)
        cot = (grad_ref[:, lanes].astype(F32) * conv).astype(BF16).astype(F32)
        last = tap[0] * cot[:rest] + tap[1] * cot[blocks : blocks + rest] + tap[2] * cot[halo:]
        grads_ref[0 : 2 * slab, lanes] = msg[slab : 3 * slab]
        grads_ref[2 * slab : 3 * slab - halo, lanes] = last.astype(BF16)
        grads_ref[3 * slab - halo : 3 * slab, lanes] = msg[3 * slab + halo : 3 * slab + 2 * halo]
        block = msg[3 * slab + 2 * halo :].astype(F32)
        for s in range(3):
            tap_ref[s, :, lanes] = block[s * TAPS : (s + 1) * TAPS]


def traded(messages, count):
    order = range(1, count)
    out = {0: messages[0]}
    for k in order:
        pairs = [(i, i ^ k) for i in range(count)]
        out[k] = lax.ppermute(messages[k], "seq", pairs)
    return [out[k] for k in range(count)]


def whole_specs(count):
    return [pl.BlockSpec(memory_space=pltpu.VMEM) for _ in range(count)]


def short_local(streams, short_taps, long_filters, out_grad):
    count = lax.axis_size("seq")
    me = lax.axis_index("seq").astype(jnp.int32)
    place = me[None]
    _, local_rows, blocks, channels = streams.shape
    slab = local_rows * blocks
    total = slab * count
    rows = local_rows * count
    halo = (TAPS - 1) * blocks
    flat_streams = streams.reshape(3 * slab, channels)
    flat_filters = long_filters.reshape(2 * slab, channels)
    flat_grad = out_grad.reshape(slab, channels)
    scalar = pl.BlockSpec(memory_space=pltpu.SMEM)
    anywhere = pl.BlockSpec(memory_space=pl.ANY)
    params = pltpu.CompilerParams(vmem_limit_bytes=VMEM_LIMIT)

    def shape(*dims, dtype=BF16):
        return jax.ShapeDtypeStruct(dims, dtype)

    messages = pl.pallas_call(
        pack_kernel,
        out_shape=[shape(6 * slab, LANES)] * count,
        in_specs=[scalar] + [anywhere] * 3,
        out_specs=whole_specs(count),
        scratch_shapes=[pltpu.SemaphoreType.DMA((count, 3))],
        compiler_params=params,
        name="pack",
    )(place, flat_streams, flat_filters, flat_grad)
    arrived = traded(messages, count)

    forward, back = transform_tables(blocks, rows)
    answer_rows = 3 * slab + 2 * halo + TAP_ROWS
    answers = pl.pallas_call(
        functools.partial(core_kernel, blocks, count),
        out_shape=[shape(answer_rows, LANES)] * count,
        in_specs=[scalar] + whole_specs(count + 1) + [anywhere] * 2,
        out_specs=whole_specs(count),
        scratch_shapes=[
            pltpu.VMEM((3, halo + total, LANES), F32),
            pltpu.VMEM((4, total, LANES), F32),
            pltpu.VMEM((total, LANES), F32),
            pltpu.VMEM((total, LANES), F32),
            pltpu.VMEM((blocks, 2 * rows, 4 * LANES), BF16),
            pltpu.VMEM((blocks, 2 * rows, 4 * LANES), BF16),
            pltpu.VMEM((blocks, 2 * rows, 2 * LANES), F32),
            pltpu.VMEM((blocks, 2 * rows, 2 * LANES), F32),
            pltpu.VMEM((3, total + halo, LANES), F32),
            pltpu.VMEM((total, LANES), F32),
            pltpu.VMEM((2, total, LANES), BF16),
            pltpu.VMEM(forward.shape, BF16),
            pltpu.VMEM(back.shape, BF16),
            pltpu.SemaphoreType.DMA((2,)),
        ],
        compiler_params=params,
        name="core",
    )(place, *arrived, short_taps, jnp.asarray(forward), jnp.asarray(back))
    returned = traded(answers, count)

    layer_out, stream_grads, tap_grads = pl.pallas_call(
        functools.partial(home_kernel, blocks, count),
        out_shape=[
            shape(slab, channels),
            shape(3 * slab, channels),
            shape(3, TAPS, channels, dtype=F32),
        ],
        in_specs=[scalar] + whole_specs(count + 3),
        out_specs=whole_specs(3),
        compiler_params=params,
        name="home",
    )(place, *returned, flat_streams[2 * slab :], flat_grad, short_taps)
    return (
        layer_out.reshape(out_grad.shape),
        stream_grads.reshape(streams.shape),
        tap_grads,
    )


def shifted(value, axis, by):
    count = lax.axis_size(axis)
    return lax.ppermute(value, axis, [(i, (i + by) % count) for i in range(count)])


def complex_product(left_real, left_imag, right_real, right_imag):
    return (
        left_real * right_real - left_imag * right_imag,
        left_real * right_imag + left_imag * right_real,
    )


def conj_product(left_real, left_imag, right_real, right_imag):
    return (
        left_real * right_real + left_imag * right_imag,
        left_real * right_imag - left_imag * right_real,
    )


def long_local(streams, short_taps, long_filters, out_grad):
    seq_count = lax.axis_size("seq")
    seq_place = lax.axis_index("seq")
    local_rows = streams.shape[1]
    channels = streams.shape[3]
    block_rows = local_rows * seq_count
    full_length = 2 * block_rows * seq_count
    angle_unit = math.pi / full_length
    block_pos = jnp.arange(seq_count, dtype=jnp.int32)
    odd_slots = 2 * block_pos + 1
    local_index = seq_place * local_rows + jnp.arange(local_rows, dtype=jnp.int32)
    row_pos = jnp.arange(block_rows, dtype=jnp.int32)
    start_pos = block_pos[None, :, None] * block_rows + local_index[:, None, None]
    fwd_angle = (start_pos * odd_slots[None, None, :] % (2 * full_length)).astype(
        jnp.float32
    ) * angle_unit
    fwd_table = jnp.stack([jnp.cos(fwd_angle), -jnp.sin(fwd_angle)], axis=-1)
    inner_angle = (row_pos[:, None] * row_pos[None, :] % block_rows).astype(jnp.float32) * (
        2.0 * math.pi / block_rows
    )
    inner_cos = jnp.cos(inner_angle)
    inner_sin = jnp.sin(inner_angle)
    inner_table = jnp.stack(
        [jnp.stack([inner_cos, -inner_sin], axis=-1), jnp.stack([inner_sin, inner_cos], axis=-1)],
        axis=0,
    )
    back_num = (
        row_pos[None, :]
        * (4 * seq_count * row_pos[:, None] + 2 * seq_place + 1)
        % (2 * full_length)
    )
    back_angle = back_num.astype(jnp.float32) * angle_unit
    back_cos = jnp.cos(back_angle)
    back_sin = jnp.sin(back_angle)
    back_table = jnp.stack(
        [jnp.stack([back_cos, back_sin], axis=-1), jnp.stack([-back_sin, back_cos], axis=-1)],
        axis=0,
    )
    outer_angle = (block_pos[:, None] * odd_slots[None, :] % (4 * seq_count)).astype(
        jnp.float32
    ) * (math.pi / (2 * seq_count))
    outer_table = jnp.stack([jnp.cos(outer_angle).T, -jnp.sin(outer_angle).T], axis=0)

    def previous_rows(block):
        edge = shifted(block[:, -1:], "seq", 1)
        rolled = jnp.concatenate([jnp.zeros_like(edge[:, :, :1]), edge[:, :, :-1]], axis=2)
        edge = jnp.where(seq_place == 0, rolled, edge)
        return jnp.concatenate([edge, block[:, :-1]], axis=1)

    def next_rows(block):
        edge = shifted(block[:, :1], "seq", -1)
        rolled = jnp.concatenate([edge[:, :, 1:], jnp.zeros_like(edge[:, :, :1])], axis=2)
        edge = jnp.where(seq_place == seq_count - 1, rolled, edge)
        return jnp.concatenate([block[:, 1:], edge], axis=1)

    def spectra(signals):
        count = signals.shape[0]
        twisted = jnp.einsum("simc,imjr->srijc", signals, fwd_table, precision=HIGHEST_PRECISION)
        slotted = lax.all_to_all(twisted, "seq", split_axis=3, concat_axis=2, tiled=True)
        slotted = slotted.reshape(count, 2, block_rows, channels)
        spec = jnp.einsum("sric,rikq->sqkc", slotted, inner_table, precision=HIGHEST_PRECISION)
        return (spec[:, 0], spec[:, 1])

    def signals_back(real_spec, imag_spec):
        count = real_spec.shape[0]
        stacked = jnp.stack([real_spec, imag_spec], axis=1)
        turned = jnp.einsum("srkc,rkiq->sqic", stacked, back_table, precision=HIGHEST_PRECISION)
        turned = turned.reshape(count, 2, block_rows, 1, channels)
        parts = lax.all_to_all(turned, "seq", split_axis=2, concat_axis=3, tiled=True)
        rows_out = jnp.einsum("srijc,rjm->simc", parts, outer_table, precision=HIGHEST_PRECISION)
        return rows_out * (2.0 / full_length)

    def tap_weight(index):
        return short_taps[:, index][:, None, None, :]

    prev_one = previous_rows(streams)
    prev_two = previous_rows(prev_one)
    filtered = (
        tap_weight(0) * streams + tap_weight(1) * prev_one + tap_weight(2) * prev_two
    ).astype(jnp.bfloat16)
    value_stream = filtered[0].astype(jnp.float32)
    gate_one = filtered[1].astype(jnp.float32)
    gate_two = filtered[2].astype(jnp.float32)
    filters = long_filters.astype(jnp.float32)
    real_first, imag_first = spectra(jnp.stack([value_stream, filters[0]]))
    product_one = complex_product(real_first[0], imag_first[0], real_first[1], imag_first[1])
    first_conv = signals_back(product_one[0][None], product_one[1][None])[0]
    gated_first = gate_one * first_conv
    real_second, imag_second = spectra(jnp.stack([gated_first, filters[1]]))
    product_two = complex_product(real_second[0], imag_second[0], real_second[1], imag_second[1])
    second_conv = signals_back(product_two[0][None], product_two[1][None])[0]
    layer_out = (gate_two * second_conv).astype(jnp.bfloat16)
    cotangent = out_grad.astype(jnp.float32)
    back_two = cotangent * gate_two
    grad_two = cotangent * second_conv
    real_third, imag_third = spectra(back_two[None])
    filter_two_real, filter_two_imag = (real_second[1], imag_second[1])
    correlated_two = conj_product(filter_two_real, filter_two_imag, real_third[0], imag_third[0])
    grad_gated = signals_back(correlated_two[0][None], correlated_two[1][None])[0]
    grad_one = grad_gated * first_conv
    back_one = grad_gated * gate_one
    real_fourth, imag_fourth = spectra(back_one[None])
    filter_one_real, filter_one_imag = (real_first[1], imag_first[1])
    correlated_one = conj_product(filter_one_real, filter_one_imag, real_fourth[0], imag_fourth[0])
    grad_value = signals_back(correlated_one[0][None], correlated_one[1][None])[0]
    stream_cot = jnp.stack([grad_value, grad_one, grad_two]).astype(jnp.bfloat16)
    next_one = next_rows(stream_cot)
    next_two = next_rows(next_one)
    stream_grads = (
        tap_weight(0) * stream_cot + tap_weight(1) * next_one + tap_weight(2) * next_two
    ).astype(jnp.bfloat16)
    cot_float = stream_cot.astype(jnp.float32)
    tap_terms = jnp.stack(
        [
            jnp.sum(cot_float * streams, axis=(1, 2)),
            jnp.sum(cot_float * prev_one, axis=(1, 2)),
            jnp.sum(cot_float * prev_two, axis=(1, 2)),
        ],
        axis=1,
    )
    tap_total = lax.psum(tap_terms, "seq")
    return (layer_out, stream_grads, tap_total * (1.0 / math.sqrt(block_rows * seq_count)))


def local(streams, short_taps, long_filters, out_grad):
    count = lax.axis_size("seq")
    _, local_rows, blocks, channels = streams.shape
    rows = local_rows * count
    fits = (
        channels == LANES * count
        and count & (count - 1) == 0
        and blocks == 8
        and rows == LANES
        and local_rows >= TAPS - 1
    )
    work = short_local if fits else long_local
    return work(streams, short_taps, long_filters, out_grad)


def solution(mesh):
    in_specs = (
        P(None, "seq", "group", "tensor"),
        P(None, None, "tensor"),
        P(None, "seq", None, "tensor"),
        P("seq", "group", "tensor"),
    )
    out_specs = (
        P("seq", "group", "tensor"),
        P(None, "seq", "group", "tensor"),
        P("group", None, "tensor"),
    )
    return jax.shard_map(local, mesh=mesh, in_specs=in_specs, out_specs=out_specs, check_vma=False)
```

```python
import functools
import math

import jax
import jax.numpy as jnp
import numpy as np
from jax import lax
from jax.experimental import pallas as pl
from jax.experimental.pallas import tpu as pltpu
from jax.sharding import PartitionSpec as P

HIGHEST_PRECISION = lax.Precision.HIGHEST
BF16 = jnp.bfloat16
F32 = jnp.float32
LANES = 128
TAPS = 3
TAP_ROWS = 16
CHUNK = 16
VMEM_LIMIT = 40 * 1024 * 1024


def split_bf16(value):
    high = value.astype(BF16)
    return high, (value - high.astype(F32)).astype(BF16)


def odd_transform(parts):
    count = len(parts)
    if count == 1:
        return [(parts[0], None)]
    even = odd_transform(parts[0::2])
    odd = odd_transform(parts[1::2])
    low, high = [], []
    for j in range(count // 2):
        angle = math.pi * (2 * j + 1) / (2 * count)
        cos, sin = math.cos(angle), math.sin(angle)
        even_real, even_imag = even[j]
        odd_real, odd_imag = odd[j]
        if odd_imag is None:
            turn_real, turn_imag = odd_real * cos, odd_real * -sin
            low.append((even_real + turn_real, turn_imag))
            high.append((even_real - turn_real, turn_imag))
        else:
            turn_real = odd_real * cos + odd_imag * sin
            turn_imag = odd_imag * cos - odd_real * sin
            low.append((even_real + turn_real, even_imag + turn_imag))
            high.append((even_real - turn_real, turn_imag - even_imag))
    return low + high[::-1]


def odd_transform_back(slots):
    count = len(slots)
    if count == 1:
        return [slots[0][0]]
    even, odd = [], []
    for j in range(count // 2):
        angle = math.pi * (2 * j + 1) / (2 * count)
        cos, sin = math.cos(angle), math.sin(angle)
        low_real, low_imag = slots[j]
        high_real, high_imag = slots[count - 1 - j]
        diff_real = low_real - high_real
        sum_imag = low_imag + high_imag
        if count == 2:
            even.append((low_real + high_real, None))
            odd.append((diff_real * cos - sum_imag * sin, None))
        else:
            even.append((low_real + high_real, low_imag - high_imag))
            odd.append((diff_real * cos - sum_imag * sin, sum_imag * cos + diff_real * sin))
    even_out = odd_transform_back(even)
    odd_out = odd_transform_back(odd)
    return [part for pair in zip(even_out, odd_out) for part in pair]


def transform_tables(blocks, rows):
    length = blocks * rows
    slot = np.arange(blocks)[:, None, None]
    freq = np.arange(rows)[None, :, None]
    pos = np.arange(rows)[None, None, :]
    number = ((2 * slot + 1 + 4 * blocks * freq) * pos) % (4 * length)
    angle = number * (np.pi / (2 * length))
    cos, sin = np.cos(angle), np.sin(angle)
    forward = np.concatenate(
        [np.concatenate([cos, sin], axis=2), np.concatenate([-sin, cos], axis=2)], axis=1
    )
    back = np.swapaxes(forward, 1, 2) / length

    def halves(table):
        high = table.astype(BF16)
        low = (table - high.astype(np.float64)).astype(BF16)
        return np.concatenate([high, low], axis=1)

    return halves(forward), halves(back)


def shift_blocks(edge, blocks, by):
    rolled = pltpu.roll(edge, by % edge.shape[0], 0)
    block = lax.broadcasted_iota(jnp.int32, edge.shape, 0) % blocks
    empty = 0 if by > 0 else blocks - 1
    return jnp.where(block == empty, 0.0, rolled)


def pack_kernel(me_ref, streams_ref, filters_ref, grad_ref, *refs):
    outs, sems = refs[:-1], refs[-1]
    slab = grad_ref.shape[0]
    me = me_ref[0]
    copies = []
    for k, (by, out) in enumerate(zip(sending_order(len(outs)), outs)):
        lanes = pl.ds(pl.multiple_of((me ^ by) * LANES, LANES), LANES)
        at = 0
        for part, source in enumerate((streams_ref, filters_ref, grad_ref)):
            size = source.shape[0]
            copies.append(
                pltpu.make_async_copy(
                    source.at[:, lanes], out.at[pl.ds(at, size)], sems.at[k, part]
                )
            )
            at += size
    for copy in copies:
        copy.start()
    for copy in copies:
        copy.wait()


def core_kernel(blocks, partners, me_ref, *refs):
    msgs = refs[:partners]
    taps_hbm, fwd_hbm, back_hbm = refs[partners : partners + 3]
    outs = refs[partners + 3 : 2 * partners + 3]
    scratch = refs[2 * partners + 3 :]
    raw, sig, gate, grad, zh, zl, spec, turned, cot, conv, grads = scratch[:11]
    fwd_ref, back_ref, weights, sems = scratch[11:]
    me = me_ref[0]
    lanes = pl.ds(pl.multiple_of(me * LANES, LANES), LANES)
    fetches = [
        pltpu.make_async_copy(taps_hbm.at[:, :, lanes], weights, sems.at[2]),
        pltpu.make_async_copy(fwd_hbm, fwd_ref, sems.at[0]),
        pltpu.make_async_copy(back_hbm, back_ref, sems.at[1]),
    ]
    for fetch in fetches:
        fetch.start()
    total = sig.shape[1]
    rows = total // blocks
    slab = total // partners
    halo = (TAPS - 1) * blocks

    def weight(stream, tap):
        return weights[stream, tap : tap + 1]

    for k, by in enumerate(sending_order(partners)):
        start = pl.multiple_of((me ^ by) * slab, slab)
        for s in range(3):
            raw[s, pl.ds(halo + start, slab)] = msgs[k][s * slab : (s + 1) * slab].astype(F32)
        sig[2, pl.ds(start, slab)] = msgs[k][3 * slab : 4 * slab].astype(F32)
        sig[3, pl.ds(start, slab)] = msgs[k][4 * slab : 5 * slab].astype(F32)
        grad[pl.ds(start, slab)] = msgs[k][5 * slab : 6 * slab].astype(F32)
    for s in range(3):
        raw[s, 0:halo] = shift_blocks(raw[s, total : total + halo], blocks, 1)

    fetches[0].wait()

    @pl.loop(0, total // slab)
    def _(step):
        base = pl.multiple_of(step * slab, slab)

        def filtered(s):
            now = raw[s, pl.ds(base + 2 * blocks, slab)]
            prev_one = raw[s, pl.ds(base + blocks, slab)]
            prev_two = raw[s, pl.ds(base, slab)]
            both = weight(s, 0) * now + weight(s, 1) * prev_one + weight(s, 2) * prev_two
            return both.astype(BF16).astype(F32)

        sig[0, pl.ds(base, slab)] = filtered(0)
        gate[pl.ds(base, slab)] = filtered(1)
        sig[1, pl.ds(base, slab)] = filtered(2) * grad[pl.ds(base, slab)]

    def store_slots(parts, row, col):
        for j, (real, imag) in enumerate(odd_transform(parts)):
            for at, value in ((row, real), (rows + row, imag)):
                high, low = split_bf16(value)
                zh[j, pl.ds(at, CHUNK), col : col + LANES] = high
                zl[j, pl.ds(at, CHUNK), col : col + LANES] = low

    def times(table, j, high, low):
        size = 2 * rows
        main = jnp.dot(table[j, 0:size], high, preferred_element_type=F32)
        main += jnp.dot(table[j, 0:size], low, preferred_element_type=F32)
        return main + jnp.dot(table[j, size : 2 * size], high, preferred_element_type=F32)

    @pl.loop(0, rows // CHUNK)
    def _(step):
        row = pl.multiple_of(step * CHUNK, CHUNK)
        for s in range(4):
            parts = [
                sig[s, pl.ds(row * blocks + b, CHUNK, stride=blocks)] for b in range(blocks)
            ]
            store_slots(parts, row, s * LANES)

    def products(data, first, second):
        real, imag = data[:rows], data[rows:]
        a_real, a_imag = real[:, :LANES], imag[:, :LANES]
        c_real, c_imag = real[:, LANES:], imag[:, LANES:]
        (f_real, f_imag), (s_real, s_imag) = first, second
        left = jnp.concatenate(
            [a_real * f_real - a_imag * f_imag, a_real * f_imag + a_imag * f_real], axis=0
        )
        right = jnp.concatenate(
            [c_real * s_real + c_imag * s_imag, c_imag * s_real - c_real * s_imag], axis=0
        )
        return jnp.concatenate([left, right], axis=1)

    def filter_spec(j, f):
        cols = slice(f * LANES, (f + 1) * LANES)
        return spec[j, 0:rows, cols], spec[j, rows : 2 * rows, cols]

    for fetch in fetches[1:]:
        fetch.wait()

    @pl.loop(0, blocks)
    def _(j):
        data = times(fwd_ref, j, zh[j], zl[j])
        spec[j] = data[:, 2 * LANES :]
        high, low = split_bf16(
            products(data[:, : 2 * LANES], filter_spec(j, 0), filter_spec(j, 1))
        )
        turned[j] = times(back_ref, j, high, low)

    def blocks_of(row, col):
        return odd_transform_back(
            [
                (
                    turned[j, pl.ds(row, CHUNK), col : col + LANES],
                    turned[j, pl.ds(rows + row, CHUNK), col : col + LANES],
                )
                for j in range(blocks)
            ]
        )

    @pl.loop(0, rows // CHUNK)
    def _(step):
        row = pl.multiple_of(step * CHUNK, CHUNK)
        first = blocks_of(row, 0)
        gated_grad = blocks_of(row, LANES)
        forward, backward = [], []
        for b in range(blocks):
            place = pl.ds(row * blocks + b, CHUNK, stride=blocks)
            gate_one = gate[place]
            cot[1, place] = (gated_grad[b] * first[b]).astype(BF16).astype(F32)
            forward.append(gate_one * first[b])
            backward.append(gate_one * gated_grad[b])
        store_slots(forward, row, 0)
        store_slots(backward, row, LANES)

    @pl.loop(0, blocks)
    def _(j):
        data = times(fwd_ref, j, zh[j, :, : 2 * LANES], zl[j, :, : 2 * LANES])
        high, low = split_bf16(products(data, filter_spec(j, 1), filter_spec(j, 0)))
        turned[j] = times(back_ref, j, high, low)

    @pl.loop(0, rows // CHUNK)
    def _(step):
        row = pl.multiple_of(step * CHUNK, CHUNK)
        second = blocks_of(row, 0)
        value_grad = blocks_of(row, LANES)
        for b in range(blocks):
            place = pl.ds(row * blocks + b, CHUNK, stride=blocks)
            conv[place] = second[b]
            cot[0, place] = value_grad[b].astype(BF16).astype(F32)

    for s in range(2):
        cot[s, total : total + halo] = shift_blocks(cot[s, 0:halo], blocks, -1)

    def finish(step, sums):
        base = pl.multiple_of(step * slab, slab)
        here = [cot[s, pl.ds(base, slab)] for s in range(2)]
        last = (grad[pl.ds(base, slab)] * conv[pl.ds(base, slab)]).astype(BF16).astype(F32)
        cot[2, pl.ds(base, slab)] = last
        here.append(last)
        for s in range(2):
            next_one = cot[s, pl.ds(base + blocks, slab)]
            next_two = cot[s, pl.ds(base + 2 * blocks, slab)]
            grads[s, pl.ds(base, slab)] = (
                weight(s, 0) * here[s] + weight(s, 1) * next_one + weight(s, 2) * next_two
            ).astype(BF16)
        added = []
        for s in range(3):
            for tap in range(TAPS):
                term = here[s] * raw[s, pl.ds(base + (TAPS - 1 - tap) * blocks, slab)]
                added.append(jnp.sum(term.reshape(slab // 8, 8, LANES), axis=0))
        return tuple(a + b for a, b in zip(sums, added))

    zeros = tuple(jnp.zeros((8, LANES), F32) for _ in range(3 * TAPS))
    sums = lax.fori_loop(0, total // slab, finish, zeros)
    cot[2, total : total + halo] = shift_blocks(cot[2, 0:halo], blocks, -1)
    scale = 1.0 / math.sqrt(total)
    tap_rows = [jnp.sum(part, axis=0, keepdims=True) * scale for part in sums]
    pad = jnp.zeros((TAP_ROWS - 3 * TAPS, LANES), F32)
    tap_block = jnp.concatenate(tap_rows + [pad], axis=0).astype(BF16)
    for k, by in enumerate(sending_order(partners)):
        start = pl.multiple_of((me ^ by) * slab, slab)
        outs[k][0:slab] = conv[pl.ds(start, slab)].astype(BF16)
        for s in range(2):
            at = (s + 1) * slab
            outs[k][at : at + slab] = grads[s, pl.ds(start, slab)]
        at = 3 * slab
        now, prev_one, prev_two = (raw[2, pl.ds(start + j * blocks, halo)] for j in (2, 1, 0))
        gate_two = weight(2, 0) * now + weight(2, 1) * prev_one + weight(2, 2) * prev_two
        first = gate_two.astype(BF16).astype(F32) * conv[pl.ds(start, halo)]
        outs[k][at : at + halo] = first.astype(BF16)
        at += halo
        begin = start + slab - halo
        now, next_one, next_two = (cot[2, pl.ds(begin + j * blocks, halo)] for j in range(TAPS))
        end = weight(2, 0) * now + weight(2, 1) * next_one + weight(2, 2) * next_two
        outs[k][at : at + halo] = end.astype(BF16)
        at += halo
        outs[k][at:] = tap_block


def home_kernel(blocks, partners, me_ref, *refs):
    msgs = refs[:partners]
    stream_ref, grad_ref, taps_ref = refs[partners : partners + 3]
    layer_ref, grads_ref, tap_ref = refs[partners + 3 :]
    me = me_ref[0]
    slab = stream_ref.shape[0]
    halo = (TAPS - 1) * blocks
    rest = slab - halo
    for k, by in enumerate(sending_order(partners)):
        lanes = pl.ds(pl.multiple_of((me ^ by) * LANES, LANES), LANES)
        msg = msgs[k]
        conv = msg[0:slab].astype(F32)
        tap = [taps_ref[2, j : j + 1, lanes] for j in range(TAPS)]
        stream = stream_ref[:, lanes].astype(F32)
        gate = tap[0] * stream[halo:] + tap[1] * stream[blocks : blocks + rest]
        gate = (gate + tap[2] * stream[:rest]).astype(BF16).astype(F32)
        layer_ref[0:halo, lanes] = msg[3 * slab : 3 * slab + halo]
        layer_ref[halo:slab, lanes] = (gate * conv[halo:]).astype(BF16)
        cot = (grad_ref[:, lanes].astype(F32) * conv).astype(BF16).astype(F32)
        last = tap[0] * cot[:rest] + tap[1] * cot[blocks : blocks + rest] + tap[2] * cot[halo:]
        grads_ref[0 : 2 * slab, lanes] = msg[slab : 3 * slab]
        grads_ref[2 * slab : 3 * slab - halo, lanes] = last.astype(BF16)
        grads_ref[3 * slab - halo : 3 * slab, lanes] = msg[3 * slab + halo : 3 * slab + 2 * halo]
        block = msg[3 * slab + 2 * halo :].astype(F32)
        for s in range(3):
            tap_ref[s, :, lanes] = block[s * TAPS : (s + 1) * TAPS]


def sending_order(count):
    far = [k for k in range(1, count) if k > 2]
    return [0] + far + [k for k in (2, 1) if k < count]


def traded(messages, count):
    out = [messages[0]]
    for k, message in zip(sending_order(count)[1:], messages[1:]):
        out.append(lax.ppermute(message, "seq", [(i, i ^ k) for i in range(count)]))
    return out


def whole_specs(count):
    return [pl.BlockSpec(memory_space=pltpu.VMEM) for _ in range(count)]


def in_hbm(array):
    return pltpu.with_memory_space_constraint(array, pltpu.HBM)


def shape(*dims, dtype=BF16):
    return jax.ShapeDtypeStruct(dims, dtype)


def core_call(place, arrived, short_taps, blocks):
    count = len(arrived)
    slab = arrived[0].shape[0] // 6
    total = slab * count
    rows = total // blocks
    halo = (TAPS - 1) * blocks
    anywhere = pl.BlockSpec(memory_space=pl.ANY)
    scalar = pl.BlockSpec(memory_space=pltpu.SMEM)
    params = pltpu.CompilerParams(vmem_limit_bytes=VMEM_LIMIT)
    forward, back = transform_tables(blocks, rows)
    answer_rows = 3 * slab + 2 * halo + TAP_ROWS
    return pl.pallas_call(
        functools.partial(core_kernel, blocks, count),
        out_shape=[shape(answer_rows, LANES)] * count,
        in_specs=[scalar] + whole_specs(count) + [anywhere] * 3,
        out_specs=whole_specs(count),
        scratch_shapes=[
            pltpu.VMEM((3, halo + total, LANES), F32),
            pltpu.VMEM((4, total, LANES), F32),
            pltpu.VMEM((total, LANES), F32),
            pltpu.VMEM((total, LANES), F32),
            pltpu.VMEM((blocks, 2 * rows, 4 * LANES), BF16),
            pltpu.VMEM((blocks, 2 * rows, 4 * LANES), BF16),
            pltpu.VMEM((blocks, 2 * rows, 2 * LANES), F32),
            pltpu.VMEM((blocks, 2 * rows, 2 * LANES), F32),
            pltpu.VMEM((3, total + halo, LANES), F32),
            pltpu.VMEM((total, LANES), F32),
            pltpu.VMEM((2, total, LANES), BF16),
            pltpu.VMEM(forward.shape, BF16),
            pltpu.VMEM(back.shape, BF16),
            pltpu.VMEM((3, TAPS, LANES), F32),
            pltpu.SemaphoreType.DMA((3,)),
        ],
        compiler_params=params,
        name="core",
    )(place, *arrived, in_hbm(short_taps), in_hbm(jnp.asarray(forward)), in_hbm(jnp.asarray(back)))


def short_local(streams, short_taps, long_filters, out_grad):
    count = lax.axis_size("seq")
    me = lax.axis_index("seq").astype(jnp.int32)
    place = me[None]
    _, local_rows, blocks, channels = streams.shape
    slab = local_rows * blocks
    flat_streams = streams.reshape(3 * slab, channels)
    flat_filters = long_filters.reshape(2 * slab, channels)
    flat_grad = out_grad.reshape(slab, channels)
    scalar = pl.BlockSpec(memory_space=pltpu.SMEM)
    anywhere = pl.BlockSpec(memory_space=pl.ANY)
    params = pltpu.CompilerParams(vmem_limit_bytes=VMEM_LIMIT)

    messages = pl.pallas_call(
        pack_kernel,
        out_shape=[shape(6 * slab, LANES)] * count,
        in_specs=[scalar] + [anywhere] * 3,
        out_specs=whole_specs(count),
        scratch_shapes=[pltpu.SemaphoreType.DMA((count, 3))],
        compiler_params=params,
        name="pack",
    )(place, in_hbm(flat_streams), in_hbm(flat_filters), in_hbm(flat_grad))
    arrived = traded(messages, count)

    answers = core_call(place, arrived, short_taps, blocks)
    returned = traded(answers, count)

    layer_out, stream_grads, tap_grads = pl.pallas_call(
        functools.partial(home_kernel, blocks, count),
        out_shape=[
            shape(slab, channels),
            shape(3 * slab, channels),
            shape(3, TAPS, channels, dtype=F32),
        ],
        in_specs=[scalar] + whole_specs(count + 3),
        out_specs=whole_specs(3),
        compiler_params=params,
        name="home",
    )(place, *returned, flat_streams[2 * slab :], flat_grad, short_taps)
    return (
        layer_out.reshape(out_grad.shape),
        stream_grads.reshape(streams.shape),
        tap_grads,
    )


def shifted(value, axis, by):
    count = lax.axis_size(axis)
    return lax.ppermute(value, axis, [(i, (i + by) % count) for i in range(count)])


def complex_product(left_real, left_imag, right_real, right_imag):
    return (
        left_real * right_real - left_imag * right_imag,
        left_real * right_imag + left_imag * right_real,
    )


def conj_product(left_real, left_imag, right_real, right_imag):
    return (
        left_real * right_real + left_imag * right_imag,
        left_real * right_imag - left_imag * right_real,
    )


def long_local(streams, short_taps, long_filters, out_grad):
    seq_count = lax.axis_size("seq")
    seq_place = lax.axis_index("seq")
    local_rows = streams.shape[1]
    channels = streams.shape[3]
    block_rows = local_rows * seq_count
    full_length = 2 * block_rows * seq_count
    angle_unit = math.pi / full_length
    block_pos = jnp.arange(seq_count, dtype=jnp.int32)
    odd_slots = 2 * block_pos + 1
    local_index = seq_place * local_rows + jnp.arange(local_rows, dtype=jnp.int32)
    row_pos = jnp.arange(block_rows, dtype=jnp.int32)
    start_pos = block_pos[None, :, None] * block_rows + local_index[:, None, None]
    fwd_angle = (start_pos * odd_slots[None, None, :] % (2 * full_length)).astype(
        jnp.float32
    ) * angle_unit
    fwd_table = jnp.stack([jnp.cos(fwd_angle), -jnp.sin(fwd_angle)], axis=-1)
    inner_angle = (row_pos[:, None] * row_pos[None, :] % block_rows).astype(jnp.float32) * (
        2.0 * math.pi / block_rows
    )
    inner_cos = jnp.cos(inner_angle)
    inner_sin = jnp.sin(inner_angle)
    inner_table = jnp.stack(
        [jnp.stack([inner_cos, -inner_sin], axis=-1), jnp.stack([inner_sin, inner_cos], axis=-1)],
        axis=0,
    )
    back_num = (
        row_pos[None, :]
        * (4 * seq_count * row_pos[:, None] + 2 * seq_place + 1)
        % (2 * full_length)
    )
    back_angle = back_num.astype(jnp.float32) * angle_unit
    back_cos = jnp.cos(back_angle)
    back_sin = jnp.sin(back_angle)
    back_table = jnp.stack(
        [jnp.stack([back_cos, back_sin], axis=-1), jnp.stack([-back_sin, back_cos], axis=-1)],
        axis=0,
    )
    outer_angle = (block_pos[:, None] * odd_slots[None, :] % (4 * seq_count)).astype(
        jnp.float32
    ) * (math.pi / (2 * seq_count))
    outer_table = jnp.stack([jnp.cos(outer_angle).T, -jnp.sin(outer_angle).T], axis=0)

    def previous_rows(block):
        edge = shifted(block[:, -1:], "seq", 1)
        rolled = jnp.concatenate([jnp.zeros_like(edge[:, :, :1]), edge[:, :, :-1]], axis=2)
        edge = jnp.where(seq_place == 0, rolled, edge)
        return jnp.concatenate([edge, block[:, :-1]], axis=1)

    def next_rows(block):
        edge = shifted(block[:, :1], "seq", -1)
        rolled = jnp.concatenate([edge[:, :, 1:], jnp.zeros_like(edge[:, :, :1])], axis=2)
        edge = jnp.where(seq_place == seq_count - 1, rolled, edge)
        return jnp.concatenate([block[:, 1:], edge], axis=1)

    def spectra(signals):
        count = signals.shape[0]
        twisted = jnp.einsum("simc,imjr->srijc", signals, fwd_table, precision=HIGHEST_PRECISION)
        slotted = lax.all_to_all(twisted, "seq", split_axis=3, concat_axis=2, tiled=True)
        slotted = slotted.reshape(count, 2, block_rows, channels)
        spec = jnp.einsum("sric,rikq->sqkc", slotted, inner_table, precision=HIGHEST_PRECISION)
        return (spec[:, 0], spec[:, 1])

    def signals_back(real_spec, imag_spec):
        count = real_spec.shape[0]
        stacked = jnp.stack([real_spec, imag_spec], axis=1)
        turned = jnp.einsum("srkc,rkiq->sqic", stacked, back_table, precision=HIGHEST_PRECISION)
        turned = turned.reshape(count, 2, block_rows, 1, channels)
        parts = lax.all_to_all(turned, "seq", split_axis=2, concat_axis=3, tiled=True)
        rows_out = jnp.einsum("srijc,rjm->simc", parts, outer_table, precision=HIGHEST_PRECISION)
        return rows_out * (2.0 / full_length)

    def tap_weight(index):
        return short_taps[:, index][:, None, None, :]

    prev_one = previous_rows(streams)
    prev_two = previous_rows(prev_one)
    filtered = (
        tap_weight(0) * streams + tap_weight(1) * prev_one + tap_weight(2) * prev_two
    ).astype(jnp.bfloat16)
    value_stream = filtered[0].astype(jnp.float32)
    gate_one = filtered[1].astype(jnp.float32)
    gate_two = filtered[2].astype(jnp.float32)
    filters = long_filters.astype(jnp.float32)
    real_first, imag_first = spectra(jnp.stack([value_stream, filters[0]]))
    product_one = complex_product(real_first[0], imag_first[0], real_first[1], imag_first[1])
    first_conv = signals_back(product_one[0][None], product_one[1][None])[0]
    gated_first = gate_one * first_conv
    real_second, imag_second = spectra(jnp.stack([gated_first, filters[1]]))
    product_two = complex_product(real_second[0], imag_second[0], real_second[1], imag_second[1])
    second_conv = signals_back(product_two[0][None], product_two[1][None])[0]
    layer_out = (gate_two * second_conv).astype(jnp.bfloat16)
    cotangent = out_grad.astype(jnp.float32)
    back_two = cotangent * gate_two
    grad_two = cotangent * second_conv
    real_third, imag_third = spectra(back_two[None])
    filter_two_real, filter_two_imag = (real_second[1], imag_second[1])
    correlated_two = conj_product(filter_two_real, filter_two_imag, real_third[0], imag_third[0])
    grad_gated = signals_back(correlated_two[0][None], correlated_two[1][None])[0]
    grad_one = grad_gated * first_conv
    back_one = grad_gated * gate_one
    real_fourth, imag_fourth = spectra(back_one[None])
    filter_one_real, filter_one_imag = (real_first[1], imag_first[1])
    correlated_one = conj_product(filter_one_real, filter_one_imag, real_fourth[0], imag_fourth[0])
    grad_value = signals_back(correlated_one[0][None], correlated_one[1][None])[0]
    stream_cot = jnp.stack([grad_value, grad_one, grad_two]).astype(jnp.bfloat16)
    next_one = next_rows(stream_cot)
    next_two = next_rows(next_one)
    stream_grads = (
        tap_weight(0) * stream_cot + tap_weight(1) * next_one + tap_weight(2) * next_two
    ).astype(jnp.bfloat16)
    cot_float = stream_cot.astype(jnp.float32)
    tap_terms = jnp.stack(
        [
            jnp.sum(cot_float * streams, axis=(1, 2)),
            jnp.sum(cot_float * prev_one, axis=(1, 2)),
            jnp.sum(cot_float * prev_two, axis=(1, 2)),
        ],
        axis=1,
    )
    tap_total = lax.psum(tap_terms, "seq")
    return (layer_out, stream_grads, tap_total * (1.0 / math.sqrt(block_rows * seq_count)))


def local(streams, short_taps, long_filters, out_grad):
    count = lax.axis_size("seq")
    _, local_rows, blocks, channels = streams.shape
    rows = local_rows * count
    fits = (
        channels == LANES * count
        and count & (count - 1) == 0
        and blocks == 8
        and rows == LANES
        and local_rows >= TAPS - 1
    )
    work = short_local if fits else long_local
    return work(streams, short_taps, long_filters, out_grad)


def solution(mesh):
    in_specs = (
        P(None, "seq", "group", "tensor"),
        P(None, None, "tensor"),
        P(None, "seq", None, "tensor"),
        P("seq", "group", "tensor"),
    )
    out_specs = (
        P("seq", "group", "tensor"),
        P(None, "seq", "group", "tensor"),
        P("group", None, "tensor"),
    )
    return jax.shard_map(local, mesh=mesh, in_specs=in_specs, out_specs=out_specs, check_vma=False)
```

```python
import functools
import math

import jax
import jax.numpy as jnp
import numpy as np
from jax import lax
from jax.experimental import pallas as pl
from jax.experimental.pallas import tpu as pltpu
from jax.sharding import PartitionSpec as P

HIGHEST_PRECISION = lax.Precision.HIGHEST
BF16 = jnp.bfloat16
F32 = jnp.float32
LANES = 128
TAPS = 3
TAP_ROWS = 16
CHUNK = 16
VMEM_LIMIT = 40 * 1024 * 1024


def split_bf16(value):
    high = value.astype(BF16)
    return high, (value - high.astype(F32)).astype(BF16)


def odd_transform(parts):
    count = len(parts)
    if count == 1:
        return [(parts[0], None)]
    even = odd_transform(parts[0::2])
    odd = odd_transform(parts[1::2])
    low, high = [], []
    for j in range(count // 2):
        angle = math.pi * (2 * j + 1) / (2 * count)
        cos, sin = math.cos(angle), math.sin(angle)
        even_real, even_imag = even[j]
        odd_real, odd_imag = odd[j]
        if odd_imag is None:
            turn_real, turn_imag = odd_real * cos, odd_real * -sin
            low.append((even_real + turn_real, turn_imag))
            high.append((even_real - turn_real, turn_imag))
        else:
            turn_real = odd_real * cos + odd_imag * sin
            turn_imag = odd_imag * cos - odd_real * sin
            low.append((even_real + turn_real, even_imag + turn_imag))
            high.append((even_real - turn_real, turn_imag - even_imag))
    return low + high[::-1]


def odd_transform_back(slots):
    count = len(slots)
    if count == 1:
        return [slots[0][0]]
    even, odd = [], []
    for j in range(count // 2):
        angle = math.pi * (2 * j + 1) / (2 * count)
        cos, sin = math.cos(angle), math.sin(angle)
        low_real, low_imag = slots[j]
        high_real, high_imag = slots[count - 1 - j]
        diff_real = low_real - high_real
        sum_imag = low_imag + high_imag
        if count == 2:
            even.append((low_real + high_real, None))
            odd.append((diff_real * cos - sum_imag * sin, None))
        else:
            even.append((low_real + high_real, low_imag - high_imag))
            odd.append((diff_real * cos - sum_imag * sin, sum_imag * cos + diff_real * sin))
    even_out = odd_transform_back(even)
    odd_out = odd_transform_back(odd)
    return [part for pair in zip(even_out, odd_out) for part in pair]


def transform_tables(blocks, rows):
    length = blocks * rows
    slot = np.arange(blocks)[:, None, None]
    freq = np.arange(rows)[None, :, None]
    pos = np.arange(rows)[None, None, :]
    number = ((2 * slot + 1 + 4 * blocks * freq) * pos) % (4 * length)
    angle = number * (np.pi / (2 * length))
    cos, sin = np.cos(angle), np.sin(angle)
    forward = np.concatenate(
        [np.concatenate([cos, sin], axis=2), np.concatenate([-sin, cos], axis=2)], axis=1
    )
    back = np.swapaxes(forward, 1, 2) / length

    def halves(table):
        high = table.astype(BF16)
        low = (table - high.astype(np.float64)).astype(BF16)
        return np.concatenate([high, low], axis=1)

    return halves(forward), halves(back)


def shift_blocks(edge, blocks, by):
    rolled = pltpu.roll(edge, by % edge.shape[0], 0)
    block = lax.broadcasted_iota(jnp.int32, edge.shape, 0) % blocks
    empty = 0 if by > 0 else blocks - 1
    return jnp.where(block == empty, 0.0, rolled)


def pack_kernel(me_ref, streams_ref, filters_ref, grad_ref, *refs):
    outs, sems = refs[:-1], refs[-1]
    slab = grad_ref.shape[0]
    me = me_ref[0]
    copies = []
    for k, (by, out) in enumerate(zip(sending_order(len(outs)), outs)):
        lanes = pl.ds(pl.multiple_of((me ^ by) * LANES, LANES), LANES)
        at = 0
        for part, source in enumerate((streams_ref, filters_ref, grad_ref)):
            size = source.shape[0]
            copies.append(
                pltpu.make_async_copy(
                    source.at[:, lanes], out.at[pl.ds(at, size)], sems.at[k, part]
                )
            )
            at += size
    for copy in copies:
        copy.start()
    for copy in copies:
        copy.wait()


def tables_kernel(me_ref, packed_ref, taps_ref, forward_ref, back_ref, *refs):
    del packed_ref
    outs, sems = refs[:-1], refs[-1]
    lanes = pl.ds(pl.multiple_of(me_ref[0] * LANES, LANES), LANES)
    sources = (taps_ref.at[:, :, lanes], forward_ref, back_ref)
    copies = [
        pltpu.make_async_copy(source, out, sems.at[n])
        for n, (source, out) in enumerate(zip(sources, outs))
    ]
    for copy in copies:
        copy.start()
    for copy in copies:
        copy.wait()


def core_kernel(blocks, partners, me_ref, *refs):
    msgs = refs[:partners]
    weights, fwd_ref, back_ref = refs[partners : partners + 3]
    outs = refs[partners + 3 : 2 * partners + 3]
    scratch = refs[2 * partners + 3 :]
    raw, sig, gate, grad, zh, zl, spec, turned, cot, conv, grads = scratch
    me = me_ref[0]
    total = sig.shape[1]
    rows = total // blocks
    slab = total // partners
    halo = (TAPS - 1) * blocks

    def weight(stream, tap):
        return weights[stream, tap : tap + 1]

    for k, by in enumerate(sending_order(partners)):
        start = pl.multiple_of((me ^ by) * slab, slab)
        for s in range(3):
            raw[s, pl.ds(halo + start, slab)] = msgs[k][s * slab : (s + 1) * slab].astype(F32)
        sig[2, pl.ds(start, slab)] = msgs[k][3 * slab : 4 * slab].astype(F32)
        sig[3, pl.ds(start, slab)] = msgs[k][4 * slab : 5 * slab].astype(F32)
        grad[pl.ds(start, slab)] = msgs[k][5 * slab : 6 * slab].astype(F32)
    for s in range(3):
        raw[s, 0:halo] = shift_blocks(raw[s, total : total + halo], blocks, 1)

    @pl.loop(0, total // slab)
    def _(step):
        base = pl.multiple_of(step * slab, slab)

        def filtered(s):
            now = raw[s, pl.ds(base + 2 * blocks, slab)]
            prev_one = raw[s, pl.ds(base + blocks, slab)]
            prev_two = raw[s, pl.ds(base, slab)]
            both = weight(s, 0) * now + weight(s, 1) * prev_one + weight(s, 2) * prev_two
            return both.astype(BF16).astype(F32)

        sig[0, pl.ds(base, slab)] = filtered(0)
        gate[pl.ds(base, slab)] = filtered(1)
        sig[1, pl.ds(base, slab)] = filtered(2) * grad[pl.ds(base, slab)]

    def store_slots(parts, row, col):
        for j, (real, imag) in enumerate(odd_transform(parts)):
            for at, value in ((row, real), (rows + row, imag)):
                high, low = split_bf16(value)
                zh[j, pl.ds(at, CHUNK), col : col + LANES] = high
                zl[j, pl.ds(at, CHUNK), col : col + LANES] = low

    def times(table, j, high, low):
        size = 2 * rows
        main = jnp.dot(table[j, 0:size], high, preferred_element_type=F32)
        main += jnp.dot(table[j, 0:size], low, preferred_element_type=F32)
        return main + jnp.dot(table[j, size : 2 * size], high, preferred_element_type=F32)

    @pl.loop(0, rows // CHUNK)
    def _(step):
        row = pl.multiple_of(step * CHUNK, CHUNK)
        for s in range(4):
            parts = [
                sig[s, pl.ds(row * blocks + b, CHUNK, stride=blocks)] for b in range(blocks)
            ]
            store_slots(parts, row, s * LANES)

    def products(data, first, second):
        real, imag = data[:rows], data[rows:]
        a_real, a_imag = real[:, :LANES], imag[:, :LANES]
        c_real, c_imag = real[:, LANES:], imag[:, LANES:]
        (f_real, f_imag), (s_real, s_imag) = first, second
        left = jnp.concatenate(
            [a_real * f_real - a_imag * f_imag, a_real * f_imag + a_imag * f_real], axis=0
        )
        right = jnp.concatenate(
            [c_real * s_real + c_imag * s_imag, c_imag * s_real - c_real * s_imag], axis=0
        )
        return jnp.concatenate([left, right], axis=1)

    def filter_spec(j, f):
        cols = slice(f * LANES, (f + 1) * LANES)
        return spec[j, 0:rows, cols], spec[j, rows : 2 * rows, cols]

    @pl.loop(0, blocks, unroll=blocks)
    def _(j):
        data = times(fwd_ref, j, zh[j], zl[j])
        spec[j] = data[:, 2 * LANES :]
        high, low = split_bf16(
            products(data[:, : 2 * LANES], filter_spec(j, 0), filter_spec(j, 1))
        )
        turned[j] = times(back_ref, j, high, low)

    def blocks_of(row, col):
        return odd_transform_back(
            [
                (
                    turned[j, pl.ds(row, CHUNK), col : col + LANES],
                    turned[j, pl.ds(rows + row, CHUNK), col : col + LANES],
                )
                for j in range(blocks)
            ]
        )

    @pl.loop(0, rows // CHUNK)
    def _(step):
        row = pl.multiple_of(step * CHUNK, CHUNK)
        first = blocks_of(row, 0)
        gated_grad = blocks_of(row, LANES)
        forward, backward = [], []
        for b in range(blocks):
            place = pl.ds(row * blocks + b, CHUNK, stride=blocks)
            gate_one = gate[place]
            cot[1, place] = (gated_grad[b] * first[b]).astype(BF16).astype(F32)
            forward.append(gate_one * first[b])
            backward.append(gate_one * gated_grad[b])
        store_slots(forward, row, 0)
        store_slots(backward, row, LANES)

    @pl.loop(0, blocks, unroll=blocks)
    def _(j):
        data = times(fwd_ref, j, zh[j, :, : 2 * LANES], zl[j, :, : 2 * LANES])
        high, low = split_bf16(products(data, filter_spec(j, 1), filter_spec(j, 0)))
        turned[j] = times(back_ref, j, high, low)

    @pl.loop(0, rows // CHUNK)
    def _(step):
        row = pl.multiple_of(step * CHUNK, CHUNK)
        second = blocks_of(row, 0)
        value_grad = blocks_of(row, LANES)
        for b in range(blocks):
            place = pl.ds(row * blocks + b, CHUNK, stride=blocks)
            conv[place] = second[b]
            cot[0, place] = value_grad[b].astype(BF16).astype(F32)

    for s in range(2):
        cot[s, total : total + halo] = shift_blocks(cot[s, 0:halo], blocks, -1)

    def finish(step, sums):
        base = pl.multiple_of(step * slab, slab)
        here = [cot[s, pl.ds(base, slab)] for s in range(2)]
        last = (grad[pl.ds(base, slab)] * conv[pl.ds(base, slab)]).astype(BF16).astype(F32)
        cot[2, pl.ds(base, slab)] = last
        here.append(last)
        for s in range(2):
            next_one = cot[s, pl.ds(base + blocks, slab)]
            next_two = cot[s, pl.ds(base + 2 * blocks, slab)]
            grads[s, pl.ds(base, slab)] = (
                weight(s, 0) * here[s] + weight(s, 1) * next_one + weight(s, 2) * next_two
            ).astype(BF16)
        added = []
        for s in range(3):
            for tap in range(TAPS):
                term = here[s] * raw[s, pl.ds(base + (TAPS - 1 - tap) * blocks, slab)]
                added.append(jnp.sum(term.reshape(slab // 8, 8, LANES), axis=0))
        return tuple(a + b for a, b in zip(sums, added))

    zeros = tuple(jnp.zeros((8, LANES), F32) for _ in range(3 * TAPS))
    sums = lax.fori_loop(0, total // slab, finish, zeros)
    cot[2, total : total + halo] = shift_blocks(cot[2, 0:halo], blocks, -1)
    scale = 1.0 / math.sqrt(total)
    tap_rows = [jnp.sum(part, axis=0, keepdims=True) * scale for part in sums]
    pad = jnp.zeros((TAP_ROWS - 3 * TAPS, LANES), F32)
    tap_block = jnp.concatenate(tap_rows + [pad], axis=0).astype(BF16)
    for k, by in enumerate(sending_order(partners)):
        start = pl.multiple_of((me ^ by) * slab, slab)
        outs[k][0:slab] = conv[pl.ds(start, slab)].astype(BF16)
        for s in range(2):
            at = (s + 1) * slab
            outs[k][at : at + slab] = grads[s, pl.ds(start, slab)]
        at = 3 * slab
        now, prev_one, prev_two = (raw[2, pl.ds(start + j * blocks, halo)] for j in (2, 1, 0))
        gate_two = weight(2, 0) * now + weight(2, 1) * prev_one + weight(2, 2) * prev_two
        first = gate_two.astype(BF16).astype(F32) * conv[pl.ds(start, halo)]
        outs[k][at : at + halo] = first.astype(BF16)
        at += halo
        begin = start + slab - halo
        now, next_one, next_two = (cot[2, pl.ds(begin + j * blocks, halo)] for j in range(TAPS))
        end = weight(2, 0) * now + weight(2, 1) * next_one + weight(2, 2) * next_two
        outs[k][at : at + halo] = end.astype(BF16)
        at += halo
        outs[k][at:] = tap_block


def home_kernel(blocks, partners, me_ref, *refs):
    msgs = refs[:partners]
    stream_ref, grad_ref, taps_ref = refs[partners : partners + 3]
    layer_ref, grads_ref, tap_ref = refs[partners + 3 :]
    me = me_ref[0]
    slab = stream_ref.shape[0]
    halo = (TAPS - 1) * blocks
    rest = slab - halo
    for k, by in enumerate(sending_order(partners)):
        lanes = pl.ds(pl.multiple_of((me ^ by) * LANES, LANES), LANES)
        msg = msgs[k]
        conv = msg[0:slab].astype(F32)
        tap = [taps_ref[2, j : j + 1, lanes] for j in range(TAPS)]
        stream = stream_ref[:, lanes].astype(F32)
        gate = tap[0] * stream[halo:] + tap[1] * stream[blocks : blocks + rest]
        gate = (gate + tap[2] * stream[:rest]).astype(BF16).astype(F32)
        layer_ref[0:halo, lanes] = msg[3 * slab : 3 * slab + halo]
        layer_ref[halo:slab, lanes] = (gate * conv[halo:]).astype(BF16)
        cot = (grad_ref[:, lanes].astype(F32) * conv).astype(BF16).astype(F32)
        last = tap[0] * cot[:rest] + tap[1] * cot[blocks : blocks + rest] + tap[2] * cot[halo:]
        grads_ref[0 : 2 * slab, lanes] = msg[slab : 3 * slab]
        grads_ref[2 * slab : 3 * slab - halo, lanes] = last.astype(BF16)
        grads_ref[3 * slab - halo : 3 * slab, lanes] = msg[3 * slab + halo : 3 * slab + 2 * halo]
        block = msg[3 * slab + 2 * halo :].astype(F32)
        for s in range(3):
            tap_ref[s, :, lanes] = block[s * TAPS : (s + 1) * TAPS]


def sending_order(count):
    far = [k for k in range(1, count) if k > 2]
    return [0] + far + [k for k in (2, 1) if k < count]


def traded(messages, count):
    out = [messages[0]]
    for k, message in zip(sending_order(count)[1:], messages[1:]):
        out.append(lax.ppermute(message, "seq", [(i, i ^ k) for i in range(count)]))
    return out


def whole_specs(count):
    return [pl.BlockSpec(memory_space=pltpu.VMEM) for _ in range(count)]


def in_hbm(array):
    return pltpu.with_memory_space_constraint(array, pltpu.HBM)


def shape(*dims, dtype=BF16):
    return jax.ShapeDtypeStruct(dims, dtype)


def core_call(place, arrived, tables, blocks):
    count = len(arrived)
    slab = arrived[0].shape[0] // 6
    total = slab * count
    rows = total // blocks
    halo = (TAPS - 1) * blocks
    scalar = pl.BlockSpec(memory_space=pltpu.SMEM)
    params = pltpu.CompilerParams(vmem_limit_bytes=VMEM_LIMIT)
    answer_rows = 3 * slab + 2 * halo + TAP_ROWS
    return pl.pallas_call(
        functools.partial(core_kernel, blocks, count),
        out_shape=[shape(answer_rows, LANES)] * count,
        in_specs=[scalar] + whole_specs(count + 3),
        out_specs=whole_specs(count),
        scratch_shapes=[
            pltpu.VMEM((3, halo + total, LANES), F32),
            pltpu.VMEM((4, total, LANES), F32),
            pltpu.VMEM((total, LANES), F32),
            pltpu.VMEM((total, LANES), F32),
            pltpu.VMEM((blocks, 2 * rows, 4 * LANES), BF16),
            pltpu.VMEM((blocks, 2 * rows, 4 * LANES), BF16),
            pltpu.VMEM((blocks, 2 * rows, 2 * LANES), F32),
            pltpu.VMEM((blocks, 2 * rows, 2 * LANES), F32),
            pltpu.VMEM((3, total + halo, LANES), F32),
            pltpu.VMEM((total, LANES), F32),
            pltpu.VMEM((2, total, LANES), BF16),
        ],
        compiler_params=params,
        name="core",
    )(place, *arrived, *tables)


def short_local(streams, short_taps, long_filters, out_grad):
    count = lax.axis_size("seq")
    me = lax.axis_index("seq").astype(jnp.int32)
    place = me[None]
    _, local_rows, blocks, channels = streams.shape
    slab = local_rows * blocks
    flat_streams = streams.reshape(3 * slab, channels)
    flat_filters = long_filters.reshape(2 * slab, channels)
    flat_grad = out_grad.reshape(slab, channels)
    scalar = pl.BlockSpec(memory_space=pltpu.SMEM)
    anywhere = pl.BlockSpec(memory_space=pl.ANY)
    params = pltpu.CompilerParams(vmem_limit_bytes=VMEM_LIMIT)

    messages = pl.pallas_call(
        pack_kernel,
        out_shape=[shape(6 * slab, LANES)] * count,
        in_specs=[scalar] + [anywhere] * 3,
        out_specs=whole_specs(count),
        scratch_shapes=[pltpu.SemaphoreType.DMA((count, 3))],
        compiler_params=params,
        name="pack",
    )(place, in_hbm(flat_streams), in_hbm(flat_filters), in_hbm(flat_grad))
    arrived = traded(messages, count)
    forward, back = transform_tables(blocks, local_rows * count)
    tables = pl.pallas_call(
        tables_kernel,
        out_shape=[
            shape(3, TAPS, LANES, dtype=F32),
            shape(*forward.shape),
            shape(*back.shape),
        ],
        in_specs=[scalar] + [anywhere] * 4,
        out_specs=whole_specs(3),
        scratch_shapes=[pltpu.SemaphoreType.DMA((3,))],
        compiler_params=params,
        name="tables",
    )(
        place,
        messages[0],
        in_hbm(short_taps),
        in_hbm(jnp.asarray(forward)),
        in_hbm(jnp.asarray(back)),
    )
    answers = core_call(place, arrived, tables, blocks)
    returned = traded(answers, count)

    layer_out, stream_grads, tap_grads = pl.pallas_call(
        functools.partial(home_kernel, blocks, count),
        out_shape=[
            shape(slab, channels),
            shape(3 * slab, channels),
            shape(3, TAPS, channels, dtype=F32),
        ],
        in_specs=[scalar] + whole_specs(count + 3),
        out_specs=whole_specs(3),
        compiler_params=params,
        name="home",
    )(place, *returned, flat_streams[2 * slab :], flat_grad, short_taps)
    return (
        layer_out.reshape(out_grad.shape),
        stream_grads.reshape(streams.shape),
        tap_grads,
    )


def shifted(value, axis, by):
    count = lax.axis_size(axis)
    return lax.ppermute(value, axis, [(i, (i + by) % count) for i in range(count)])


def complex_product(left_real, left_imag, right_real, right_imag):
    return (
        left_real * right_real - left_imag * right_imag,
        left_real * right_imag + left_imag * right_real,
    )


def conj_product(left_real, left_imag, right_real, right_imag):
    return (
        left_real * right_real + left_imag * right_imag,
        left_real * right_imag - left_imag * right_real,
    )


def long_local(streams, short_taps, long_filters, out_grad):
    seq_count = lax.axis_size("seq")
    seq_place = lax.axis_index("seq")
    local_rows = streams.shape[1]
    channels = streams.shape[3]
    block_rows = local_rows * seq_count
    full_length = 2 * block_rows * seq_count
    angle_unit = math.pi / full_length
    block_pos = jnp.arange(seq_count, dtype=jnp.int32)
    odd_slots = 2 * block_pos + 1
    local_index = seq_place * local_rows + jnp.arange(local_rows, dtype=jnp.int32)
    row_pos = jnp.arange(block_rows, dtype=jnp.int32)
    start_pos = block_pos[None, :, None] * block_rows + local_index[:, None, None]
    fwd_angle = (start_pos * odd_slots[None, None, :] % (2 * full_length)).astype(
        jnp.float32
    ) * angle_unit
    fwd_table = jnp.stack([jnp.cos(fwd_angle), -jnp.sin(fwd_angle)], axis=-1)
    inner_angle = (row_pos[:, None] * row_pos[None, :] % block_rows).astype(jnp.float32) * (
        2.0 * math.pi / block_rows
    )
    inner_cos = jnp.cos(inner_angle)
    inner_sin = jnp.sin(inner_angle)
    inner_table = jnp.stack(
        [jnp.stack([inner_cos, -inner_sin], axis=-1), jnp.stack([inner_sin, inner_cos], axis=-1)],
        axis=0,
    )
    back_num = (
        row_pos[None, :]
        * (4 * seq_count * row_pos[:, None] + 2 * seq_place + 1)
        % (2 * full_length)
    )
    back_angle = back_num.astype(jnp.float32) * angle_unit
    back_cos = jnp.cos(back_angle)
    back_sin = jnp.sin(back_angle)
    back_table = jnp.stack(
        [jnp.stack([back_cos, back_sin], axis=-1), jnp.stack([-back_sin, back_cos], axis=-1)],
        axis=0,
    )
    outer_angle = (block_pos[:, None] * odd_slots[None, :] % (4 * seq_count)).astype(
        jnp.float32
    ) * (math.pi / (2 * seq_count))
    outer_table = jnp.stack([jnp.cos(outer_angle).T, -jnp.sin(outer_angle).T], axis=0)

    def previous_rows(block):
        edge = shifted(block[:, -1:], "seq", 1)
        rolled = jnp.concatenate([jnp.zeros_like(edge[:, :, :1]), edge[:, :, :-1]], axis=2)
        edge = jnp.where(seq_place == 0, rolled, edge)
        return jnp.concatenate([edge, block[:, :-1]], axis=1)

    def next_rows(block):
        edge = shifted(block[:, :1], "seq", -1)
        rolled = jnp.concatenate([edge[:, :, 1:], jnp.zeros_like(edge[:, :, :1])], axis=2)
        edge = jnp.where(seq_place == seq_count - 1, rolled, edge)
        return jnp.concatenate([block[:, 1:], edge], axis=1)

    def spectra(signals):
        count = signals.shape[0]
        twisted = jnp.einsum("simc,imjr->srijc", signals, fwd_table, precision=HIGHEST_PRECISION)
        slotted = lax.all_to_all(twisted, "seq", split_axis=3, concat_axis=2, tiled=True)
        slotted = slotted.reshape(count, 2, block_rows, channels)
        spec = jnp.einsum("sric,rikq->sqkc", slotted, inner_table, precision=HIGHEST_PRECISION)
        return (spec[:, 0], spec[:, 1])

    def signals_back(real_spec, imag_spec):
        count = real_spec.shape[0]
        stacked = jnp.stack([real_spec, imag_spec], axis=1)
        turned = jnp.einsum("srkc,rkiq->sqic", stacked, back_table, precision=HIGHEST_PRECISION)
        turned = turned.reshape(count, 2, block_rows, 1, channels)
        parts = lax.all_to_all(turned, "seq", split_axis=2, concat_axis=3, tiled=True)
        rows_out = jnp.einsum("srijc,rjm->simc", parts, outer_table, precision=HIGHEST_PRECISION)
        return rows_out * (2.0 / full_length)

    def tap_weight(index):
        return short_taps[:, index][:, None, None, :]

    prev_one = previous_rows(streams)
    prev_two = previous_rows(prev_one)
    filtered = (
        tap_weight(0) * streams + tap_weight(1) * prev_one + tap_weight(2) * prev_two
    ).astype(jnp.bfloat16)
    value_stream = filtered[0].astype(jnp.float32)
    gate_one = filtered[1].astype(jnp.float32)
    gate_two = filtered[2].astype(jnp.float32)
    filters = long_filters.astype(jnp.float32)
    real_first, imag_first = spectra(jnp.stack([value_stream, filters[0]]))
    product_one = complex_product(real_first[0], imag_first[0], real_first[1], imag_first[1])
    first_conv = signals_back(product_one[0][None], product_one[1][None])[0]
    gated_first = gate_one * first_conv
    real_second, imag_second = spectra(jnp.stack([gated_first, filters[1]]))
    product_two = complex_product(real_second[0], imag_second[0], real_second[1], imag_second[1])
    second_conv = signals_back(product_two[0][None], product_two[1][None])[0]
    layer_out = (gate_two * second_conv).astype(jnp.bfloat16)
    cotangent = out_grad.astype(jnp.float32)
    back_two = cotangent * gate_two
    grad_two = cotangent * second_conv
    real_third, imag_third = spectra(back_two[None])
    filter_two_real, filter_two_imag = (real_second[1], imag_second[1])
    correlated_two = conj_product(filter_two_real, filter_two_imag, real_third[0], imag_third[0])
    grad_gated = signals_back(correlated_two[0][None], correlated_two[1][None])[0]
    grad_one = grad_gated * first_conv
    back_one = grad_gated * gate_one
    real_fourth, imag_fourth = spectra(back_one[None])
    filter_one_real, filter_one_imag = (real_first[1], imag_first[1])
    correlated_one = conj_product(filter_one_real, filter_one_imag, real_fourth[0], imag_fourth[0])
    grad_value = signals_back(correlated_one[0][None], correlated_one[1][None])[0]
    stream_cot = jnp.stack([grad_value, grad_one, grad_two]).astype(jnp.bfloat16)
    next_one = next_rows(stream_cot)
    next_two = next_rows(next_one)
    stream_grads = (
        tap_weight(0) * stream_cot + tap_weight(1) * next_one + tap_weight(2) * next_two
    ).astype(jnp.bfloat16)
    cot_float = stream_cot.astype(jnp.float32)
    tap_terms = jnp.stack(
        [
            jnp.sum(cot_float * streams, axis=(1, 2)),
            jnp.sum(cot_float * prev_one, axis=(1, 2)),
            jnp.sum(cot_float * prev_two, axis=(1, 2)),
        ],
        axis=1,
    )
    tap_total = lax.psum(tap_terms, "seq")
    return (layer_out, stream_grads, tap_total * (1.0 / math.sqrt(block_rows * seq_count)))


def local(streams, short_taps, long_filters, out_grad):
    count = lax.axis_size("seq")
    _, local_rows, blocks, channels = streams.shape
    rows = local_rows * count
    fits = (
        channels == LANES * count
        and count & (count - 1) == 0
        and blocks == 8
        and rows == LANES
        and local_rows >= TAPS - 1
    )
    work = short_local if fits else long_local
    return work(streams, short_taps, long_filters, out_grad)


def solution(mesh):
    in_specs = (
        P(None, "seq", "group", "tensor"),
        P(None, None, "tensor"),
        P(None, "seq", None, "tensor"),
        P("seq", "group", "tensor"),
    )
    out_specs = (
        P("seq", "group", "tensor"),
        P(None, "seq", "group", "tensor"),
        P("group", None, "tensor"),
    )
    return jax.shard_map(local, mesh=mesh, in_specs=in_specs, out_specs=out_specs, check_vma=False)
```

```python
import functools
import math

import jax
import jax.numpy as jnp
import numpy as np
from jax import lax
from jax.experimental import pallas as pl
from jax.experimental.pallas import tpu as pltpu
from jax.sharding import PartitionSpec as P

HIGHEST_PRECISION = lax.Precision.HIGHEST
BF16 = jnp.bfloat16
F32 = jnp.float32
LANES = 128
TAPS = 3
TAP_ROWS = 16
CHUNK = 16
VMEM_LIMIT = 40 * 1024 * 1024


def split_bf16(value):
    high = value.astype(BF16)
    return high, (value - high.astype(F32)).astype(BF16)


def odd_transform(parts):
    count = len(parts)
    if count == 1:
        return [(parts[0], None)]
    even = odd_transform(parts[0::2])
    odd = odd_transform(parts[1::2])
    low, high = [], []
    for j in range(count // 2):
        angle = math.pi * (2 * j + 1) / (2 * count)
        cos, sin = math.cos(angle), math.sin(angle)
        even_real, even_imag = even[j]
        odd_real, odd_imag = odd[j]
        if odd_imag is None:
            turn_real, turn_imag = odd_real * cos, odd_real * -sin
            low.append((even_real + turn_real, turn_imag))
            high.append((even_real - turn_real, turn_imag))
        else:
            turn_real = odd_real * cos + odd_imag * sin
            turn_imag = odd_imag * cos - odd_real * sin
            low.append((even_real + turn_real, even_imag + turn_imag))
            high.append((even_real - turn_real, turn_imag - even_imag))
    return low + high[::-1]


def odd_transform_back(slots):
    count = len(slots)
    if count == 1:
        return [slots[0][0]]
    even, odd = [], []
    for j in range(count // 2):
        angle = math.pi * (2 * j + 1) / (2 * count)
        cos, sin = math.cos(angle), math.sin(angle)
        low_real, low_imag = slots[j]
        high_real, high_imag = slots[count - 1 - j]
        diff_real = low_real - high_real
        sum_imag = low_imag + high_imag
        if count == 2:
            even.append((low_real + high_real, None))
            odd.append((diff_real * cos - sum_imag * sin, None))
        else:
            even.append((low_real + high_real, low_imag - high_imag))
            odd.append((diff_real * cos - sum_imag * sin, sum_imag * cos + diff_real * sin))
    even_out = odd_transform_back(even)
    odd_out = odd_transform_back(odd)
    return [part for pair in zip(even_out, odd_out) for part in pair]


def transform_tables(blocks, rows):
    length = blocks * rows
    slot = np.arange(blocks)[:, None, None]
    freq = np.arange(rows)[None, :, None]
    pos = np.arange(rows)[None, None, :]
    number = ((2 * slot + 1 + 4 * blocks * freq) * pos) % (4 * length)
    angle = number * (np.pi / (2 * length))
    cos, sin = np.cos(angle), np.sin(angle)
    forward = np.concatenate(
        [np.concatenate([cos, sin], axis=2), np.concatenate([-sin, cos], axis=2)], axis=1
    )
    back = np.swapaxes(forward, 1, 2) / length

    def halves(table):
        high = table.astype(BF16)
        low = (table - high.astype(np.float64)).astype(BF16)
        return np.concatenate([high, low], axis=1)

    return halves(forward), halves(back)


def shift_blocks(edge, blocks, by):
    rolled = pltpu.roll(edge, by % edge.shape[0], 0)
    block = lax.broadcasted_iota(jnp.int32, edge.shape, 0) % blocks
    empty = 0 if by > 0 else blocks - 1
    return jnp.where(block == empty, 0.0, rolled)


def run_copies(pairs, sems):
    copies = [
        pltpu.make_async_copy(source, target, sems.at[n])
        for n, (source, target) in enumerate(pairs)
    ]
    for copy in copies:
        copy.start()
    for copy in copies:
        copy.wait()


def pack_kernel(me_ref, streams_ref, filters_ref, grad_ref, *refs):
    outs, sems = refs[:-1], refs[-1]
    me = me_ref[0]
    pairs = []
    for by, out in zip(sending_order(len(outs)), outs):
        lanes = pl.ds(pl.multiple_of((me ^ by) * LANES, LANES), LANES)
        at = 0
        for source in (streams_ref, filters_ref, grad_ref):
            size = source.shape[0]
            pairs.append((source.at[:, lanes], out.at[pl.ds(at, size)]))
            at += size
    run_copies(pairs, sems)


def tables_kernel(me_ref, packed_ref, taps_ref, forward_ref, back_ref, *refs):
    del packed_ref
    outs, sems = refs[:-1], refs[-1]
    lanes = pl.ds(pl.multiple_of(me_ref[0] * LANES, LANES), LANES)
    sources = (taps_ref.at[:, :, lanes], forward_ref, back_ref)
    run_copies(zip(sources, outs), sems)


class Transforms:
    def __init__(self, rows, fwd_ref, back_ref, high, low):
        self.rows, self.fwd, self.back, self.high, self.low = rows, fwd_ref, back_ref, high, low
        self.blocks = fwd_ref.shape[0]

    def store(self, parts, row, col):
        for j, (real, imag) in enumerate(odd_transform(parts)):
            for at, value in ((row, real), (self.rows + row, imag)):
                high, low = split_bf16(value)
                self.high[j, pl.ds(at, CHUNK), col : col + LANES] = high
                self.low[j, pl.ds(at, CHUNK), col : col + LANES] = low

    def times(self, table, j, high, low):
        size = 2 * self.rows
        main = jnp.dot(table[j, 0:size], high, preferred_element_type=F32)
        main += jnp.dot(table[j, 0:size], low, preferred_element_type=F32)
        return main + jnp.dot(table[j, size : 2 * size], high, preferred_element_type=F32)

    def forward(self, j, begin, end):
        return self.times(self.fwd, j, self.high[j, :, begin:end], self.low[j, :, begin:end])

    def backward(self, j, data):
        return self.times(self.back, j, *split_bf16(data))

    def blocks_of(self, slots, row, col):
        return odd_transform_back(
            [
                (
                    slots[j, pl.ds(row, CHUNK), col : col + LANES],
                    slots[j, pl.ds(self.rows + row, CHUNK), col : col + LANES],
                )
                for j in range(self.blocks)
            ]
        )

    def each_slot(self, body):
        for j in range(self.blocks):
            body(j)

    def each_chunk(self, body):
        @pl.loop(0, self.rows // CHUNK, unroll=8)
        def _(step):
            body(pl.multiple_of(step * CHUNK, CHUNK))


def spread(blocks, row, block):
    return pl.ds(row * blocks + block, CHUNK, stride=blocks)


def product(left, right, conjugate=False):
    rows = left.shape[0] // 2
    a_real, a_imag, b_real, b_imag = left[:rows], left[rows:], right[:rows], right[rows:]
    if conjugate:
        real, imag = a_real * b_real + a_imag * b_imag, a_imag * b_real - a_real * b_imag
    else:
        real, imag = a_real * b_real - a_imag * b_imag, a_real * b_imag + a_imag * b_real
    return jnp.concatenate([real, imag], axis=0)


def filtered(raw, weights, s, at, blocks, size):
    now = weights[s, 0:1] * raw[pl.ds(at + 2 * blocks, size)]
    now = now + weights[s, 1:2] * raw[pl.ds(at + blocks, size)]
    return (now + weights[s, 2:3] * raw[pl.ds(at, size)]).astype(BF16).astype(F32)


def core_kernel(blocks, count, me_ref, *refs):
    weights, fwd_ref, back_ref = refs[:3]
    msgs, outs, scratch = refs[3 : 3 + count], refs[3 + count : 3 + 2 * count], refs[3 + 2 * count :]
    raw, sig, gate, grad, high, low, spec, turned, cot, conv, grads = scratch
    me = me_ref[0]
    total = sig.shape[1]
    rows = total // blocks
    slab = total // count
    halo = (TAPS - 1) * blocks

    def weight(stream, tap):
        return weights[stream, tap : tap + 1]

    for by, msg in zip(sending_order(count), msgs):
        start = pl.multiple_of((me ^ by) * slab, slab)
        for s in range(3):
            raw[s, pl.ds(halo + start, slab)] = msg[s * slab : (s + 1) * slab].astype(F32)
        for f in range(2):
            sig[f, pl.ds(start, slab)] = msg[(3 + f) * slab : (4 + f) * slab].astype(F32)
        grad[pl.ds(start, slab)] = msg[5 * slab : 6 * slab].astype(F32)
    for s in range(3):
        raw[s, 0:halo] = shift_blocks(raw[s, total : total + halo], blocks, 1)

    @pl.loop(0, total // slab)
    def _(step):
        base = pl.multiple_of(step * slab, slab)
        sig[2, pl.ds(base, slab)] = filtered(raw.at[0], weights, 0, base, blocks, slab)
        gate[pl.ds(base, slab)] = filtered(raw.at[1], weights, 1, base, blocks, slab)
        gate_two = filtered(raw.at[2], weights, 2, base, blocks, slab)
        sig[3, pl.ds(base, slab)] = gate_two * grad[pl.ds(base, slab)]

    work = Transforms(rows, fwd_ref, back_ref, high, low)

    def butterflies(row, signals):
        for s in signals:
            parts = [sig[s, spread(blocks, row, b)] for b in range(blocks)]
            work.store(parts, row, s * LANES)

    work.each_chunk(functools.partial(butterflies, signals=(0, 1)))
    steps = rows // CHUNK
    for j in range(max(blocks, steps)):
        if j < blocks:
            spec[j] = work.forward(j, 0, 2 * LANES)
        if j < steps:
            butterflies(j * CHUNK, (2, 3))

    def forward_data(j):
        turned[j] = work.forward(j, 2 * LANES, 4 * LANES)

    def first_products(j):
        data = turned[j]
        left = product(data[:, :LANES], spec[j, :, :LANES])
        right = product(data[:, LANES:], spec[j, :, LANES:], True)
        turned[j] = work.backward(j, jnp.concatenate([left, right], axis=1))

    work.each_slot(forward_data)
    work.each_slot(first_products)

    def gates(row):
        first = work.blocks_of(turned, row, 0)
        gated_grad = work.blocks_of(turned, row, LANES)
        forward, backward = [], []
        for b in range(blocks):
            here = spread(blocks, row, b)
            gate_one = gate[here]
            cot[1, here] = (gated_grad[b] * first[b]).astype(BF16).astype(F32)
            forward.append(gate_one * first[b])
            backward.append(gate_one * gated_grad[b])
        work.store(forward, row, 0)
        work.store(backward, row, LANES)

    work.each_chunk(gates)

    def convolve(j):
        data = work.forward(j, 0, 2 * LANES)
        left = product(data[:, :LANES], spec[j, :, LANES:])
        right = product(data[:, LANES:], spec[j, :, :LANES], True)
        turned[j] = work.backward(j, jnp.concatenate([left, right], axis=1))

    work.each_slot(convolve)

    def last(row):
        second = work.blocks_of(turned, row, 0)
        value_grad = work.blocks_of(turned, row, LANES)
        for b in range(blocks):
            here = spread(blocks, row, b)
            conv[here] = second[b]
            cot[0, here] = value_grad[b].astype(BF16).astype(F32)

    work.each_chunk(last)
    for s in range(2):
        cot[s, total : total + halo] = shift_blocks(cot[s, 0:halo], blocks, -1)

    def finish(step, sums):
        base = pl.multiple_of(step * slab, slab)
        here = [cot[s, pl.ds(base, slab)] for s in range(2)]
        last = (grad[pl.ds(base, slab)] * conv[pl.ds(base, slab)]).astype(BF16).astype(F32)
        cot[2, pl.ds(base, slab)] = last
        here.append(last)
        for s in range(2):
            next_one = cot[s, pl.ds(base + blocks, slab)]
            next_two = cot[s, pl.ds(base + 2 * blocks, slab)]
            grads[s, pl.ds(base, slab)] = (
                weight(s, 0) * here[s] + weight(s, 1) * next_one + weight(s, 2) * next_two
            ).astype(BF16)
        added = []
        for s in range(3):
            for tap in range(TAPS):
                term = here[s] * raw[s, pl.ds(base + (TAPS - 1 - tap) * blocks, slab)]
                added.append(jnp.sum(term.reshape(slab // 8, 8, LANES), axis=0))
        return tuple(a + b for a, b in zip(sums, added))

    zeros = tuple(jnp.zeros((8, LANES), F32) for _ in range(3 * TAPS))
    sums = lax.fori_loop(0, total // slab, finish, zeros)
    cot[2, total : total + halo] = shift_blocks(cot[2, 0:halo], blocks, -1)
    scale = 1.0 / math.sqrt(total)
    tap_rows = [jnp.sum(part, axis=0, keepdims=True) * scale for part in sums]
    pad = jnp.zeros((TAP_ROWS - 3 * TAPS, LANES), F32)
    tap_block = jnp.concatenate(tap_rows + [pad], axis=0).astype(BF16)
    for k, by in enumerate(sending_order(count)):
        start = pl.multiple_of((me ^ by) * slab, slab)
        outs[k][0:slab] = conv[pl.ds(start, slab)].astype(BF16)
        for s in range(2):
            at = (s + 1) * slab
            outs[k][at : at + slab] = grads[s, pl.ds(start, slab)]
        at = 3 * slab
        now, prev_one, prev_two = (raw[2, pl.ds(start + j * blocks, halo)] for j in (2, 1, 0))
        gate_two = weight(2, 0) * now + weight(2, 1) * prev_one + weight(2, 2) * prev_two
        first = gate_two.astype(BF16).astype(F32) * conv[pl.ds(start, halo)]
        outs[k][at : at + halo] = first.astype(BF16)
        at += halo
        begin = start + slab - halo
        now, next_one, next_two = (cot[2, pl.ds(begin + j * blocks, halo)] for j in range(TAPS))
        end = weight(2, 0) * now + weight(2, 1) * next_one + weight(2, 2) * next_two
        outs[k][at : at + halo] = end.astype(BF16)
        at += halo
        outs[k][at:] = tap_block


def home_kernel(blocks, partners, me_ref, *refs):
    msgs = refs[:partners]
    stream_ref, grad_ref, taps_ref = refs[partners : partners + 3]
    layer_ref, grads_ref, tap_ref = refs[partners + 3 :]
    me = me_ref[0]
    slab = stream_ref.shape[0]
    halo = (TAPS - 1) * blocks
    rest = slab - halo
    for k, by in enumerate(sending_order(partners)):
        lanes = pl.ds(pl.multiple_of((me ^ by) * LANES, LANES), LANES)
        msg = msgs[k]
        conv = msg[0:slab].astype(F32)
        tap = [taps_ref[2, j : j + 1, lanes] for j in range(TAPS)]
        stream = stream_ref[:, lanes].astype(F32)
        gate = tap[0] * stream[halo:] + tap[1] * stream[blocks : blocks + rest]
        gate = (gate + tap[2] * stream[:rest]).astype(BF16).astype(F32)
        layer_ref[0:halo, lanes] = msg[3 * slab : 3 * slab + halo]
        layer_ref[halo:slab, lanes] = (gate * conv[halo:]).astype(BF16)
        cot = (grad_ref[:, lanes].astype(F32) * conv).astype(BF16).astype(F32)
        last = tap[0] * cot[:rest] + tap[1] * cot[blocks : blocks + rest] + tap[2] * cot[halo:]
        grads_ref[0 : 2 * slab, lanes] = msg[slab : 3 * slab]
        grads_ref[2 * slab : 3 * slab - halo, lanes] = last.astype(BF16)
        grads_ref[3 * slab - halo : 3 * slab, lanes] = msg[3 * slab + halo : 3 * slab + 2 * halo]
        block = msg[3 * slab + 2 * halo :].astype(F32)
        for s in range(3):
            tap_ref[s, :, lanes] = block[s * TAPS : (s + 1) * TAPS]


def sending_order(count):
    far = [k for k in range(1, count) if k > 2]
    return [0] + far + [k for k in (2, 1) if k < count]


def everyone(messages):
    count = len(messages)
    out = [messages[0]]
    for by, message in zip(sending_order(count)[1:], messages[1:]):
        out.append(lax.ppermute(message, "seq", [(i, i ^ by) for i in range(count)]))
    return out


def whole_specs(count):
    return [pl.BlockSpec(memory_space=pltpu.VMEM) for _ in range(count)]


def in_hbm(array):
    return pltpu.with_memory_space_constraint(array, pltpu.HBM)


def shape(*dims, dtype=BF16):
    return jax.ShapeDtypeStruct(dims, dtype)


def call(kernel, name, out_shape, in_specs, scratch=()):
    return pl.pallas_call(
        kernel,
        out_shape=out_shape,
        in_specs=in_specs,
        out_specs=whole_specs(len(out_shape)),
        scratch_shapes=list(scratch),
        compiler_params=pltpu.CompilerParams(vmem_limit_bytes=VMEM_LIMIT),
        name=name,
    )


def core_call(place, tables, messages, blocks):
    count = len(messages)
    slab = messages[0].shape[0] // 6
    total = slab * count
    spectrum = (blocks, 2 * total // blocks)
    halo = (TAPS - 1) * blocks
    return call(
        functools.partial(core_kernel, blocks, count),
        "core",
        [shape(3 * slab + 2 * halo + TAP_ROWS, LANES)] * count,
        [pl.BlockSpec(memory_space=pltpu.SMEM)] + whole_specs(count + 3),
        [
            pltpu.VMEM((3, halo + total, LANES), F32),
            pltpu.VMEM((4, total, LANES), F32),
            pltpu.VMEM((total, LANES), F32),
            pltpu.VMEM((total, LANES), F32),
            pltpu.VMEM((*spectrum, 4 * LANES), BF16),
            pltpu.VMEM((*spectrum, 4 * LANES), BF16),
            pltpu.VMEM((*spectrum, 2 * LANES), F32),
            pltpu.VMEM((*spectrum, 2 * LANES), F32),
            pltpu.VMEM((3, total + halo, LANES), F32),
            pltpu.VMEM((total, LANES), F32),
            pltpu.VMEM((2, total, LANES), BF16),
        ],
    )(place, *tables, *messages)


def short_local(streams, short_taps, long_filters, out_grad):
    count = lax.axis_size("seq")
    place = lax.axis_index("seq").astype(jnp.int32)[None]
    _, local_rows, blocks, channels = streams.shape
    slab = local_rows * blocks
    flat_streams = streams.reshape(3 * slab, channels)
    flat_filters = long_filters.reshape(2 * slab, channels)
    flat_grad = out_grad.reshape(slab, channels)
    scalar = pl.BlockSpec(memory_space=pltpu.SMEM)
    anywhere = pl.BlockSpec(memory_space=pl.ANY)

    packed = call(
        pack_kernel,
        "pack",
        [shape(6 * slab, LANES)] * count,
        [scalar] + [anywhere] * 3,
        [pltpu.SemaphoreType.DMA((3 * count,))],
    )(place, in_hbm(flat_streams), in_hbm(flat_filters), in_hbm(flat_grad))
    messages = everyone(packed)
    forward, back = transform_tables(blocks, local_rows * count)
    tables = call(
        tables_kernel,
        "tables",
        [shape(3, TAPS, LANES, dtype=F32), shape(*forward.shape), shape(*back.shape)],
        [scalar] + [anywhere] * 4,
        [pltpu.SemaphoreType.DMA((3,))],
    )(
        place,
        packed[0],
        in_hbm(short_taps),
        in_hbm(jnp.asarray(forward)),
        in_hbm(jnp.asarray(back)),
    )
    answers = core_call(place, tables, messages, blocks)
    returned = everyone(answers)
    layer_out, stream_grads, tap_grads = call(
        functools.partial(home_kernel, blocks, count),
        "home",
        [
            shape(slab, channels),
            shape(3 * slab, channels),
            shape(3, TAPS, channels, dtype=F32),
        ],
        [scalar] + whole_specs(count + 3),
    )(place, *returned, flat_streams[2 * slab :], flat_grad, short_taps)
    return (
        layer_out.reshape(out_grad.shape),
        stream_grads.reshape(streams.shape),
        tap_grads,
    )


def shifted(value, axis, by):
    count = lax.axis_size(axis)
    return lax.ppermute(value, axis, [(i, (i + by) % count) for i in range(count)])


def complex_product(left_real, left_imag, right_real, right_imag):
    return (
        left_real * right_real - left_imag * right_imag,
        left_real * right_imag + left_imag * right_real,
    )


def conj_product(left_real, left_imag, right_real, right_imag):
    return (
        left_real * right_real + left_imag * right_imag,
        left_real * right_imag - left_imag * right_real,
    )


def long_local(streams, short_taps, long_filters, out_grad):
    seq_count = lax.axis_size("seq")
    seq_place = lax.axis_index("seq")
    local_rows = streams.shape[1]
    channels = streams.shape[3]
    block_rows = local_rows * seq_count
    full_length = 2 * block_rows * seq_count
    angle_unit = math.pi / full_length
    block_pos = jnp.arange(seq_count, dtype=jnp.int32)
    odd_slots = 2 * block_pos + 1
    local_index = seq_place * local_rows + jnp.arange(local_rows, dtype=jnp.int32)
    row_pos = jnp.arange(block_rows, dtype=jnp.int32)
    start_pos = block_pos[None, :, None] * block_rows + local_index[:, None, None]
    fwd_angle = (start_pos * odd_slots[None, None, :] % (2 * full_length)).astype(
        jnp.float32
    ) * angle_unit
    fwd_table = jnp.stack([jnp.cos(fwd_angle), -jnp.sin(fwd_angle)], axis=-1)
    inner_angle = (row_pos[:, None] * row_pos[None, :] % block_rows).astype(jnp.float32) * (
        2.0 * math.pi / block_rows
    )
    inner_cos = jnp.cos(inner_angle)
    inner_sin = jnp.sin(inner_angle)
    inner_table = jnp.stack(
        [jnp.stack([inner_cos, -inner_sin], axis=-1), jnp.stack([inner_sin, inner_cos], axis=-1)],
        axis=0,
    )
    back_num = (
        row_pos[None, :]
        * (4 * seq_count * row_pos[:, None] + 2 * seq_place + 1)
        % (2 * full_length)
    )
    back_angle = back_num.astype(jnp.float32) * angle_unit
    back_cos = jnp.cos(back_angle)
    back_sin = jnp.sin(back_angle)
    back_table = jnp.stack(
        [jnp.stack([back_cos, back_sin], axis=-1), jnp.stack([-back_sin, back_cos], axis=-1)],
        axis=0,
    )
    outer_angle = (block_pos[:, None] * odd_slots[None, :] % (4 * seq_count)).astype(
        jnp.float32
    ) * (math.pi / (2 * seq_count))
    outer_table = jnp.stack([jnp.cos(outer_angle).T, -jnp.sin(outer_angle).T], axis=0)

    def previous_rows(block):
        edge = shifted(block[:, -1:], "seq", 1)
        rolled = jnp.concatenate([jnp.zeros_like(edge[:, :, :1]), edge[:, :, :-1]], axis=2)
        edge = jnp.where(seq_place == 0, rolled, edge)
        return jnp.concatenate([edge, block[:, :-1]], axis=1)

    def next_rows(block):
        edge = shifted(block[:, :1], "seq", -1)
        rolled = jnp.concatenate([edge[:, :, 1:], jnp.zeros_like(edge[:, :, :1])], axis=2)
        edge = jnp.where(seq_place == seq_count - 1, rolled, edge)
        return jnp.concatenate([block[:, 1:], edge], axis=1)

    def spectra(signals):
        count = signals.shape[0]
        twisted = jnp.einsum("simc,imjr->srijc", signals, fwd_table, precision=HIGHEST_PRECISION)
        slotted = lax.all_to_all(twisted, "seq", split_axis=3, concat_axis=2, tiled=True)
        slotted = slotted.reshape(count, 2, block_rows, channels)
        spec = jnp.einsum("sric,rikq->sqkc", slotted, inner_table, precision=HIGHEST_PRECISION)
        return (spec[:, 0], spec[:, 1])

    def signals_back(real_spec, imag_spec):
        count = real_spec.shape[0]
        stacked = jnp.stack([real_spec, imag_spec], axis=1)
        turned = jnp.einsum("srkc,rkiq->sqic", stacked, back_table, precision=HIGHEST_PRECISION)
        turned = turned.reshape(count, 2, block_rows, 1, channels)
        parts = lax.all_to_all(turned, "seq", split_axis=2, concat_axis=3, tiled=True)
        rows_out = jnp.einsum("srijc,rjm->simc", parts, outer_table, precision=HIGHEST_PRECISION)
        return rows_out * (2.0 / full_length)

    def tap_weight(index):
        return short_taps[:, index][:, None, None, :]

    prev_one = previous_rows(streams)
    prev_two = previous_rows(prev_one)
    filtered = (
        tap_weight(0) * streams + tap_weight(1) * prev_one + tap_weight(2) * prev_two
    ).astype(jnp.bfloat16)
    value_stream = filtered[0].astype(jnp.float32)
    gate_one = filtered[1].astype(jnp.float32)
    gate_two = filtered[2].astype(jnp.float32)
    filters = long_filters.astype(jnp.float32)
    real_first, imag_first = spectra(jnp.stack([value_stream, filters[0]]))
    product_one = complex_product(real_first[0], imag_first[0], real_first[1], imag_first[1])
    first_conv = signals_back(product_one[0][None], product_one[1][None])[0]
    gated_first = gate_one * first_conv
    real_second, imag_second = spectra(jnp.stack([gated_first, filters[1]]))
    product_two = complex_product(real_second[0], imag_second[0], real_second[1], imag_second[1])
    second_conv = signals_back(product_two[0][None], product_two[1][None])[0]
    layer_out = (gate_two * second_conv).astype(jnp.bfloat16)
    cotangent = out_grad.astype(jnp.float32)
    back_two = cotangent * gate_two
    grad_two = cotangent * second_conv
    real_third, imag_third = spectra(back_two[None])
    filter_two_real, filter_two_imag = (real_second[1], imag_second[1])
    correlated_two = conj_product(filter_two_real, filter_two_imag, real_third[0], imag_third[0])
    grad_gated = signals_back(correlated_two[0][None], correlated_two[1][None])[0]
    grad_one = grad_gated * first_conv
    back_one = grad_gated * gate_one
    real_fourth, imag_fourth = spectra(back_one[None])
    filter_one_real, filter_one_imag = (real_first[1], imag_first[1])
    correlated_one = conj_product(filter_one_real, filter_one_imag, real_fourth[0], imag_fourth[0])
    grad_value = signals_back(correlated_one[0][None], correlated_one[1][None])[0]
    stream_cot = jnp.stack([grad_value, grad_one, grad_two]).astype(jnp.bfloat16)
    next_one = next_rows(stream_cot)
    next_two = next_rows(next_one)
    stream_grads = (
        tap_weight(0) * stream_cot + tap_weight(1) * next_one + tap_weight(2) * next_two
    ).astype(jnp.bfloat16)
    cot_float = stream_cot.astype(jnp.float32)
    tap_terms = jnp.stack(
        [
            jnp.sum(cot_float * streams, axis=(1, 2)),
            jnp.sum(cot_float * prev_one, axis=(1, 2)),
            jnp.sum(cot_float * prev_two, axis=(1, 2)),
        ],
        axis=1,
    )
    tap_total = lax.psum(tap_terms, "seq")
    return (layer_out, stream_grads, tap_total * (1.0 / math.sqrt(block_rows * seq_count)))


def local(streams, short_taps, long_filters, out_grad):
    count = lax.axis_size("seq")
    _, local_rows, blocks, channels = streams.shape
    rows = local_rows * count
    fits = (
        channels == LANES * count
        and count & (count - 1) == 0
        and blocks == 8
        and rows == LANES
        and local_rows >= TAPS - 1
    )
    work = short_local if fits else long_local
    return work(streams, short_taps, long_filters, out_grad)


def solution(mesh):
    in_specs = (
        P(None, "seq", "group", "tensor"),
        P(None, None, "tensor"),
        P(None, "seq", None, "tensor"),
        P("seq", "group", "tensor"),
    )
    out_specs = (
        P("seq", "group", "tensor"),
        P(None, "seq", "group", "tensor"),
        P("group", None, "tensor"),
    )
    return jax.shard_map(local, mesh=mesh, in_specs=in_specs, out_specs=out_specs, check_vma=False)
```

```python
import functools
import math

import jax
import jax.numpy as jnp
import numpy as np
from jax import lax
from jax.experimental import pallas as pl
from jax.experimental.pallas import tpu as pltpu
from jax.sharding import PartitionSpec as P

HIGHEST_PRECISION = lax.Precision.HIGHEST
BF16 = jnp.bfloat16
F32 = jnp.float32
LANES = 128
TAPS = 3
TAP_ROWS = 16
CHUNK = 16
VMEM_LIMIT = 40 * 1024 * 1024


def split_bf16(value):
    high = value.astype(BF16)
    return high, (value - high.astype(F32)).astype(BF16)


def odd_transform(parts):
    count = len(parts)
    if count == 1:
        return [(parts[0], None)]
    even = odd_transform(parts[0::2])
    odd = odd_transform(parts[1::2])
    low, high = [], []
    for j in range(count // 2):
        angle = math.pi * (2 * j + 1) / (2 * count)
        cos, sin = math.cos(angle), math.sin(angle)
        even_real, even_imag = even[j]
        odd_real, odd_imag = odd[j]
        if odd_imag is None:
            turn_real, turn_imag = odd_real * cos, odd_real * -sin
            low.append((even_real + turn_real, turn_imag))
            high.append((even_real - turn_real, turn_imag))
        else:
            turn_real = odd_real * cos + odd_imag * sin
            turn_imag = odd_imag * cos - odd_real * sin
            low.append((even_real + turn_real, even_imag + turn_imag))
            high.append((even_real - turn_real, turn_imag - even_imag))
    return low + high[::-1]


def odd_transform_back(slots):
    count = len(slots)
    if count == 1:
        return [slots[0][0]]
    even, odd = [], []
    for j in range(count // 2):
        angle = math.pi * (2 * j + 1) / (2 * count)
        cos, sin = math.cos(angle), math.sin(angle)
        low_real, low_imag = slots[j]
        high_real, high_imag = slots[count - 1 - j]
        diff_real = low_real - high_real
        sum_imag = low_imag + high_imag
        if count == 2:
            even.append((low_real + high_real, None))
            odd.append((diff_real * cos - sum_imag * sin, None))
        else:
            even.append((low_real + high_real, low_imag - high_imag))
            odd.append((diff_real * cos - sum_imag * sin, sum_imag * cos + diff_real * sin))
    even_out = odd_transform_back(even)
    odd_out = odd_transform_back(odd)
    return [part for pair in zip(even_out, odd_out) for part in pair]


def transform_tables(blocks, rows):
    length = blocks * rows
    slot = np.arange(blocks)[:, None, None]
    freq = np.arange(rows)[None, :, None]
    pos = np.arange(rows)[None, None, :]
    number = ((2 * slot + 1 + 4 * blocks * freq) * pos) % (4 * length)
    angle = number * (np.pi / (2 * length))
    cos, sin = np.cos(angle), np.sin(angle)
    forward = np.concatenate(
        [np.concatenate([cos, sin], axis=2), np.concatenate([-sin, cos], axis=2)], axis=1
    )
    back = np.swapaxes(forward, 1, 2) / length

    def halves(table):
        high = table.astype(BF16)
        low = (table - high.astype(np.float64)).astype(BF16)
        return np.concatenate([high, low], axis=1)

    return halves(forward), halves(back)


def shift_blocks(edge, blocks, by):
    rolled = pltpu.roll(edge, by % edge.shape[0], 0)
    block = lax.broadcasted_iota(jnp.int32, edge.shape, 0) % blocks
    empty = 0 if by > 0 else blocks - 1
    return jnp.where(block == empty, 0.0, rolled)


def run_copies(pairs, sems):
    copies = [
        pltpu.make_async_copy(source, target, sems.at[n])
        for n, (source, target) in enumerate(pairs)
    ]
    for copy in copies:
        copy.start()
    for copy in copies:
        copy.wait()


def pack_kernel(me_ref, group_ref, streams_ref, filters_ref, grad_ref, *refs):
    outs, sems = refs[:-1], refs[-1]
    me, group = me_ref[0], group_ref[0]
    slab = grad_ref.shape[0]
    pairs = []
    for by, out in zip(asking_order(len(outs)), outs):
        lanes = pl.ds(pl.multiple_of((me ^ by) * LANES, LANES), LANES)
        filters = pl.ds(0, 2 * slab)
        if out.shape[0] == 5 * slab:
            filters = pl.ds(pl.multiple_of(group * slab, slab), slab)
        at = 0
        for source in (
            streams_ref.at[:, lanes],
            grad_ref.at[:, lanes],
            filters_ref.at[filters, lanes],
        ):
            size = source.shape[0]
            pairs.append((source, out.at[pl.ds(at, size)]))
            at += size
    run_copies(pairs, sems)


def swap_kernel(*refs):
    out = refs[-1]
    slab = out.shape[0] // (len(refs) - 1)
    for n, msg in enumerate(refs[:-1]):
        out[n * slab : (n + 1) * slab] = msg[4 * slab : 5 * slab]


def tables_kernel(me_ref, packed_ref, taps_ref, forward_ref, back_ref, *refs):
    del packed_ref
    outs, sems = refs[:-1], refs[-1]
    lanes = pl.ds(pl.multiple_of(me_ref[0] * LANES, LANES), LANES)
    sources = (taps_ref.at[:, :, lanes], forward_ref, back_ref)
    run_copies(zip(sources, outs), sems)


class Transforms:
    def __init__(self, rows, fwd_ref, back_ref, high, low):
        self.rows, self.fwd, self.back, self.high, self.low = rows, fwd_ref, back_ref, high, low
        self.blocks = fwd_ref.shape[0]

    def store(self, parts, row, col):
        for j, (real, imag) in enumerate(odd_transform(parts)):
            for at, value in ((row, real), (self.rows + row, imag)):
                high, low = split_bf16(value)
                self.high[j, pl.ds(at, CHUNK), col : col + LANES] = high
                self.low[j, pl.ds(at, CHUNK), col : col + LANES] = low

    def times(self, table, j, high, low):
        size = 2 * self.rows
        main = jnp.dot(table[j, 0:size], high, preferred_element_type=F32)
        main += jnp.dot(table[j, 0:size], low, preferred_element_type=F32)
        return main + jnp.dot(table[j, size : 2 * size], high, preferred_element_type=F32)

    def forward(self, j, begin, end):
        return self.times(self.fwd, j, self.high[j, :, begin:end], self.low[j, :, begin:end])

    def backward(self, j, data):
        return self.times(self.back, j, *split_bf16(data))

    def blocks_of(self, slots, row, col):
        return odd_transform_back(
            [
                (
                    slots[j, pl.ds(row, CHUNK), col : col + LANES],
                    slots[j, pl.ds(self.rows + row, CHUNK), col : col + LANES],
                )
                for j in range(self.blocks)
            ]
        )

    def each_slot(self, body):
        for j in range(self.blocks):
            body(j)

    def each_chunk(self, body):
        @pl.loop(0, self.rows // CHUNK, unroll=8)
        def _(step):
            body(pl.multiple_of(step * CHUNK, CHUNK))


def spread(blocks, row, block):
    return pl.ds(row * blocks + block, CHUNK, stride=blocks)


def product(left, right, conjugate=False):
    rows = left.shape[0] // 2
    a_real, a_imag, b_real, b_imag = left[:rows], left[rows:], right[:rows], right[rows:]
    if conjugate:
        real, imag = a_real * b_real + a_imag * b_imag, a_imag * b_real - a_real * b_imag
    else:
        real, imag = a_real * b_real - a_imag * b_imag, a_real * b_imag + a_imag * b_real
    return jnp.concatenate([real, imag], axis=0)


def filtered(raw, weights, s, at, blocks, size):
    now = weights[s, 0:1] * raw[pl.ds(at + 2 * blocks, size)]
    now = now + weights[s, 1:2] * raw[pl.ds(at + blocks, size)]
    return (now + weights[s, 2:3] * raw[pl.ds(at, size)]).astype(BF16).astype(F32)


def core_kernel(blocks, count, me_ref, group_ref, *refs):
    weights, fwd_ref, back_ref = refs[:3]
    msgs, swapped, refs = refs[3 : 3 + count], refs[3 + count], refs[4 + count :]
    outs, scratch = refs[:count], refs[count:]
    raw, sig, gate, grad, high, low, spec, turned, cot, conv, grads = scratch
    me, group = me_ref[0], group_ref[0]
    total = sig.shape[1]
    rows = total // blocks
    slab = total // count
    halo = (TAPS - 1) * blocks

    def weight(stream, tap):
        return weights[stream, tap : tap + 1]

    taken = 0
    for by, msg in zip(asking_order(count), msgs):
        start = pl.multiple_of((me ^ by) * slab, slab)
        for s in range(3):
            raw[s, pl.ds(halo + start, slab)] = msg[s * slab : (s + 1) * slab].astype(F32)
        grad[pl.ds(start, slab)] = msg[3 * slab : 4 * slab].astype(F32)
        if msg.shape[0] == 5 * slab:
            sig[group, pl.ds(start, slab)] = msg[4 * slab :].astype(F32)
            other = swapped[taken * slab : (taken + 1) * slab]
            sig[1 - group, pl.ds(start, slab)] = other.astype(F32)
            taken += 1
        else:
            for f in range(2):
                sig[f, pl.ds(start, slab)] = msg[(4 + f) * slab : (5 + f) * slab].astype(F32)
    for s in range(3):
        raw[s, 0:halo] = shift_blocks(raw[s, total : total + halo], blocks, 1)

    @pl.loop(0, total // slab)
    def _(step):
        base = pl.multiple_of(step * slab, slab)
        sig[2, pl.ds(base, slab)] = filtered(raw.at[0], weights, 0, base, blocks, slab)
        gate[pl.ds(base, slab)] = filtered(raw.at[1], weights, 1, base, blocks, slab)
        gate_two = filtered(raw.at[2], weights, 2, base, blocks, slab)
        sig[3, pl.ds(base, slab)] = gate_two * grad[pl.ds(base, slab)]

    work = Transforms(rows, fwd_ref, back_ref, high, low)

    def butterflies(row, signals):
        for s in signals:
            parts = [sig[s, spread(blocks, row, b)] for b in range(blocks)]
            work.store(parts, row, s * LANES)

    work.each_chunk(functools.partial(butterflies, signals=(0, 1)))
    steps = rows // CHUNK
    for j in range(max(blocks, steps)):
        if j < blocks:
            spec[j] = work.forward(j, 0, 2 * LANES)
        if j < steps:
            butterflies(j * CHUNK, (2, 3))

    def forward_data(j):
        turned[j] = work.forward(j, 2 * LANES, 4 * LANES)

    def first_products(j):
        data = turned[j]
        left = product(data[:, :LANES], spec[j, :, :LANES])
        right = product(data[:, LANES:], spec[j, :, LANES:], True)
        turned[j] = work.backward(j, jnp.concatenate([left, right], axis=1))

    work.each_slot(forward_data)
    work.each_slot(first_products)

    def gates(row):
        first = work.blocks_of(turned, row, 0)
        gated_grad = work.blocks_of(turned, row, LANES)
        forward, backward = [], []
        for b in range(blocks):
            here = spread(blocks, row, b)
            gate_one = gate[here]
            cot[1, here] = (gated_grad[b] * first[b]).astype(BF16).astype(F32)
            forward.append(gate_one * first[b])
            backward.append(gate_one * gated_grad[b])
        work.store(forward, row, 0)
        work.store(backward, row, LANES)

    work.each_chunk(gates)

    def convolve(j):
        data = work.forward(j, 0, 2 * LANES)
        left = product(data[:, :LANES], spec[j, :, LANES:])
        right = product(data[:, LANES:], spec[j, :, :LANES], True)
        turned[j] = work.backward(j, jnp.concatenate([left, right], axis=1))

    work.each_slot(convolve)

    def last(row):
        second = work.blocks_of(turned, row, 0)
        value_grad = work.blocks_of(turned, row, LANES)
        for b in range(blocks):
            here = spread(blocks, row, b)
            conv[here] = second[b]
            cot[0, here] = value_grad[b].astype(BF16).astype(F32)

    work.each_chunk(last)
    for s in range(2):
        cot[s, total : total + halo] = shift_blocks(cot[s, 0:halo], blocks, -1)

    def finish(step, sums):
        base = pl.multiple_of(step * slab, slab)
        here = [cot[s, pl.ds(base, slab)] for s in range(2)]
        last = (grad[pl.ds(base, slab)] * conv[pl.ds(base, slab)]).astype(BF16).astype(F32)
        cot[2, pl.ds(base, slab)] = last
        here.append(last)
        for s in range(2):
            next_one = cot[s, pl.ds(base + blocks, slab)]
            next_two = cot[s, pl.ds(base + 2 * blocks, slab)]
            grads[s, pl.ds(base, slab)] = (
                weight(s, 0) * here[s] + weight(s, 1) * next_one + weight(s, 2) * next_two
            ).astype(BF16)
        added = []
        for s in range(3):
            for tap in range(TAPS):
                term = here[s] * raw[s, pl.ds(base + (TAPS - 1 - tap) * blocks, slab)]
                added.append(jnp.sum(term.reshape(slab // 8, 8, LANES), axis=0))
        return tuple(a + b for a, b in zip(sums, added))

    zeros = tuple(jnp.zeros((8, LANES), F32) for _ in range(3 * TAPS))
    sums = lax.fori_loop(0, total // slab, finish, zeros)
    cot[2, total : total + halo] = shift_blocks(cot[2, 0:halo], blocks, -1)
    scale = 1.0 / math.sqrt(total)
    tap_rows = [jnp.sum(part, axis=0, keepdims=True) * scale for part in sums]
    pad = jnp.zeros((TAP_ROWS - 3 * TAPS, LANES), F32)
    tap_block = jnp.concatenate(tap_rows + [pad], axis=0).astype(BF16)
    for k, by in enumerate(answering_order(count)):
        start = pl.multiple_of((me ^ by) * slab, slab)
        outs[k][0:slab] = conv[pl.ds(start, slab)].astype(BF16)
        for s in range(2):
            at = (s + 1) * slab
            outs[k][at : at + slab] = grads[s, pl.ds(start, slab)]
        at = 3 * slab
        now, prev_one, prev_two = (raw[2, pl.ds(start + j * blocks, halo)] for j in (2, 1, 0))
        gate_two = weight(2, 0) * now + weight(2, 1) * prev_one + weight(2, 2) * prev_two
        first = gate_two.astype(BF16).astype(F32) * conv[pl.ds(start, halo)]
        outs[k][at : at + halo] = first.astype(BF16)
        at += halo
        begin = start + slab - halo
        now, next_one, next_two = (cot[2, pl.ds(begin + j * blocks, halo)] for j in range(TAPS))
        end = weight(2, 0) * now + weight(2, 1) * next_one + weight(2, 2) * next_two
        outs[k][at : at + halo] = end.astype(BF16)
        at += halo
        outs[k][at:] = tap_block


def home_kernel(blocks, partners, me_ref, *refs):
    msgs = refs[:partners]
    stream_ref, grad_ref, taps_ref = refs[partners : partners + 3]
    layer_ref, grads_ref, tap_ref = refs[partners + 3 :]
    me = me_ref[0]
    slab = stream_ref.shape[0]
    halo = (TAPS - 1) * blocks
    rest = slab - halo
    for k, by in enumerate(answering_order(partners)):
        lanes = pl.ds(pl.multiple_of((me ^ by) * LANES, LANES), LANES)
        msg = msgs[k]
        conv = msg[0:slab].astype(F32)
        tap = [taps_ref[2, j : j + 1, lanes] for j in range(TAPS)]
        stream = stream_ref[:, lanes].astype(F32)
        gate = tap[0] * stream[halo:] + tap[1] * stream[blocks : blocks + rest]
        gate = (gate + tap[2] * stream[:rest]).astype(BF16).astype(F32)
        layer_ref[0:halo, lanes] = msg[3 * slab : 3 * slab + halo]
        layer_ref[halo:slab, lanes] = (gate * conv[halo:]).astype(BF16)
        cot = (grad_ref[:, lanes].astype(F32) * conv).astype(BF16).astype(F32)
        last = tap[0] * cot[:rest] + tap[1] * cot[blocks : blocks + rest] + tap[2] * cot[halo:]
        grads_ref[0 : 2 * slab, lanes] = msg[slab : 3 * slab]
        grads_ref[2 * slab : 3 * slab - halo, lanes] = last.astype(BF16)
        grads_ref[3 * slab - halo : 3 * slab, lanes] = msg[3 * slab + halo : 3 * slab + 2 * halo]
        block = msg[3 * slab + 2 * halo :].astype(F32)
        for s in range(3):
            tap_ref[s, :, lanes] = block[s * TAPS : (s + 1) * TAPS]


def asking_order(count):
    half = count // 2
    near, far = list(range(half - 1, 0, -1)), list(range(half, count))
    return [0, *far[:1], *near[:1], *far[1:], *near[1:]]


def answering_order(count):
    half = count // 2
    near, far = list(range(half - 1, 0, -1)), list(range(half, count))
    return [0, *near[2:], *near[1:2], *far[:1], *near[:1], *far[1:]]


def filters_once(count, groups):
    return [count // 2, count // 2 + 1, count // 2 + 2] if groups == 2 else []


def everyone(messages, order):
    count = len(messages)
    out = [messages[0]]
    for by, message in zip(order[1:], messages[1:]):
        out.append(lax.ppermute(message, "seq", [(i, i ^ by) for i in range(count)]))
    return out


def whole_specs(count):
    return [pl.BlockSpec(memory_space=pltpu.VMEM) for _ in range(count)]


def in_hbm(array):
    return pltpu.with_memory_space_constraint(array, pltpu.HBM)


def shape(*dims, dtype=BF16):
    return jax.ShapeDtypeStruct(dims, dtype)


def call(kernel, name, out_shape, in_specs, scratch=()):
    return pl.pallas_call(
        kernel,
        out_shape=out_shape,
        in_specs=in_specs,
        out_specs=whole_specs(len(out_shape)),
        scratch_shapes=list(scratch),
        compiler_params=pltpu.CompilerParams(vmem_limit_bytes=VMEM_LIMIT),
        name=name,
    )


def core_call(place, group, tables, messages, swapped, blocks):
    count = len(messages)
    slab = messages[0].shape[0] // 6
    total = slab * count
    spectrum = (blocks, 2 * total // blocks)
    halo = (TAPS - 1) * blocks
    return call(
        functools.partial(core_kernel, blocks, count),
        "core",
        [shape(3 * slab + 2 * halo + TAP_ROWS, LANES)] * count,
        [pl.BlockSpec(memory_space=pltpu.SMEM)] * 2 + whole_specs(count + 4),
        [
            pltpu.VMEM((3, halo + total, LANES), F32),
            pltpu.VMEM((4, total, LANES), F32),
            pltpu.VMEM((total, LANES), F32),
            pltpu.VMEM((total, LANES), F32),
            pltpu.VMEM((*spectrum, 4 * LANES), BF16),
            pltpu.VMEM((*spectrum, 4 * LANES), BF16),
            pltpu.VMEM((*spectrum, 2 * LANES), F32),
            pltpu.VMEM((*spectrum, 2 * LANES), F32),
            pltpu.VMEM((3, total + halo, LANES), F32),
            pltpu.VMEM((total, LANES), F32),
            pltpu.VMEM((2, total, LANES), BF16),
        ],
    )(place, group, *tables, *messages, swapped)


def short_local(streams, short_taps, long_filters, out_grad):
    count = lax.axis_size("seq")
    groups = lax.axis_size("group")
    place = lax.axis_index("seq").astype(jnp.int32)[None]
    group = lax.axis_index("group").astype(jnp.int32)[None]
    order = asking_order(count)
    once = filters_once(count, groups)
    _, local_rows, blocks, channels = streams.shape
    slab = local_rows * blocks
    flat_streams = streams.reshape(3 * slab, channels)
    flat_filters = long_filters.reshape(2 * slab, channels)
    flat_grad = out_grad.reshape(slab, channels)
    scalar = pl.BlockSpec(memory_space=pltpu.SMEM)
    anywhere = pl.BlockSpec(memory_space=pl.ANY)

    packed = call(
        pack_kernel,
        "pack",
        [shape((5 if by in once else 6) * slab, LANES) for by in order],
        [scalar] * 2 + [anywhere] * 3,
        [pltpu.SemaphoreType.DMA((3 * count,))],
    )(place, group, in_hbm(flat_streams), in_hbm(flat_filters), in_hbm(flat_grad))
    messages = everyone(packed, order)
    swapped = jnp.zeros((16, LANES), BF16)
    if once:
        halves = [message for by, message in zip(order, messages) if by in once]
        (mine,) = call(
            swap_kernel, "swap", [shape(len(once) * slab, LANES)], whole_specs(len(once))
        )(*halves)
        swapped = lax.ppermute(mine, "group", [(0, 1), (1, 0)])
    forward, back = transform_tables(blocks, local_rows * count)
    tables = call(
        tables_kernel,
        "tables",
        [shape(3, TAPS, LANES, dtype=F32), shape(*forward.shape), shape(*back.shape)],
        [scalar] + [anywhere] * 4,
        [pltpu.SemaphoreType.DMA((3,))],
    )(
        place,
        packed[0],
        in_hbm(short_taps),
        in_hbm(jnp.asarray(forward)),
        in_hbm(jnp.asarray(back)),
    )
    answers = core_call(place, group, tables, messages, swapped, blocks)
    returned = everyone(answers, answering_order(count))
    layer_out, stream_grads, tap_grads = call(
        functools.partial(home_kernel, blocks, count),
        "home",
        [
            shape(slab, channels),
            shape(3 * slab, channels),
            shape(3, TAPS, channels, dtype=F32),
        ],
        [scalar] + whole_specs(count + 3),
    )(place, *returned, flat_streams[2 * slab :], flat_grad, short_taps)
    return (
        layer_out.reshape(out_grad.shape),
        stream_grads.reshape(streams.shape),
        tap_grads,
    )


def shifted(value, axis, by):
    count = lax.axis_size(axis)
    return lax.ppermute(value, axis, [(i, (i + by) % count) for i in range(count)])


def complex_product(left_real, left_imag, right_real, right_imag):
    return (
        left_real * right_real - left_imag * right_imag,
        left_real * right_imag + left_imag * right_real,
    )


def conj_product(left_real, left_imag, right_real, right_imag):
    return (
        left_real * right_real + left_imag * right_imag,
        left_real * right_imag - left_imag * right_real,
    )


def long_local(streams, short_taps, long_filters, out_grad):
    seq_count = lax.axis_size("seq")
    seq_place = lax.axis_index("seq")
    local_rows = streams.shape[1]
    channels = streams.shape[3]
    block_rows = local_rows * seq_count
    full_length = 2 * block_rows * seq_count
    angle_unit = math.pi / full_length
    block_pos = jnp.arange(seq_count, dtype=jnp.int32)
    odd_slots = 2 * block_pos + 1
    local_index = seq_place * local_rows + jnp.arange(local_rows, dtype=jnp.int32)
    row_pos = jnp.arange(block_rows, dtype=jnp.int32)
    start_pos = block_pos[None, :, None] * block_rows + local_index[:, None, None]
    fwd_angle = (start_pos * odd_slots[None, None, :] % (2 * full_length)).astype(
        jnp.float32
    ) * angle_unit
    fwd_table = jnp.stack([jnp.cos(fwd_angle), -jnp.sin(fwd_angle)], axis=-1)
    inner_angle = (row_pos[:, None] * row_pos[None, :] % block_rows).astype(jnp.float32) * (
        2.0 * math.pi / block_rows
    )
    inner_cos = jnp.cos(inner_angle)
    inner_sin = jnp.sin(inner_angle)
    inner_table = jnp.stack(
        [jnp.stack([inner_cos, -inner_sin], axis=-1), jnp.stack([inner_sin, inner_cos], axis=-1)],
        axis=0,
    )
    back_num = (
        row_pos[None, :]
        * (4 * seq_count * row_pos[:, None] + 2 * seq_place + 1)
        % (2 * full_length)
    )
    back_angle = back_num.astype(jnp.float32) * angle_unit
    back_cos = jnp.cos(back_angle)
    back_sin = jnp.sin(back_angle)
    back_table = jnp.stack(
        [jnp.stack([back_cos, back_sin], axis=-1), jnp.stack([-back_sin, back_cos], axis=-1)],
        axis=0,
    )
    outer_angle = (block_pos[:, None] * odd_slots[None, :] % (4 * seq_count)).astype(
        jnp.float32
    ) * (math.pi / (2 * seq_count))
    outer_table = jnp.stack([jnp.cos(outer_angle).T, -jnp.sin(outer_angle).T], axis=0)

    def previous_rows(block):
        edge = shifted(block[:, -1:], "seq", 1)
        rolled = jnp.concatenate([jnp.zeros_like(edge[:, :, :1]), edge[:, :, :-1]], axis=2)
        edge = jnp.where(seq_place == 0, rolled, edge)
        return jnp.concatenate([edge, block[:, :-1]], axis=1)

    def next_rows(block):
        edge = shifted(block[:, :1], "seq", -1)
        rolled = jnp.concatenate([edge[:, :, 1:], jnp.zeros_like(edge[:, :, :1])], axis=2)
        edge = jnp.where(seq_place == seq_count - 1, rolled, edge)
        return jnp.concatenate([block[:, 1:], edge], axis=1)

    def spectra(signals):
        count = signals.shape[0]
        twisted = jnp.einsum("simc,imjr->srijc", signals, fwd_table, precision=HIGHEST_PRECISION)
        slotted = lax.all_to_all(twisted, "seq", split_axis=3, concat_axis=2, tiled=True)
        slotted = slotted.reshape(count, 2, block_rows, channels)
        spec = jnp.einsum("sric,rikq->sqkc", slotted, inner_table, precision=HIGHEST_PRECISION)
        return (spec[:, 0], spec[:, 1])

    def signals_back(real_spec, imag_spec):
        count = real_spec.shape[0]
        stacked = jnp.stack([real_spec, imag_spec], axis=1)
        turned = jnp.einsum("srkc,rkiq->sqic", stacked, back_table, precision=HIGHEST_PRECISION)
        turned = turned.reshape(count, 2, block_rows, 1, channels)
        parts = lax.all_to_all(turned, "seq", split_axis=2, concat_axis=3, tiled=True)
        rows_out = jnp.einsum("srijc,rjm->simc", parts, outer_table, precision=HIGHEST_PRECISION)
        return rows_out * (2.0 / full_length)

    def tap_weight(index):
        return short_taps[:, index][:, None, None, :]

    prev_one = previous_rows(streams)
    prev_two = previous_rows(prev_one)
    filtered = (
        tap_weight(0) * streams + tap_weight(1) * prev_one + tap_weight(2) * prev_two
    ).astype(jnp.bfloat16)
    value_stream = filtered[0].astype(jnp.float32)
    gate_one = filtered[1].astype(jnp.float32)
    gate_two = filtered[2].astype(jnp.float32)
    filters = long_filters.astype(jnp.float32)
    real_first, imag_first = spectra(jnp.stack([value_stream, filters[0]]))
    product_one = complex_product(real_first[0], imag_first[0], real_first[1], imag_first[1])
    first_conv = signals_back(product_one[0][None], product_one[1][None])[0]
    gated_first = gate_one * first_conv
    real_second, imag_second = spectra(jnp.stack([gated_first, filters[1]]))
    product_two = complex_product(real_second[0], imag_second[0], real_second[1], imag_second[1])
    second_conv = signals_back(product_two[0][None], product_two[1][None])[0]
    layer_out = (gate_two * second_conv).astype(jnp.bfloat16)
    cotangent = out_grad.astype(jnp.float32)
    back_two = cotangent * gate_two
    grad_two = cotangent * second_conv
    real_third, imag_third = spectra(back_two[None])
    filter_two_real, filter_two_imag = (real_second[1], imag_second[1])
    correlated_two = conj_product(filter_two_real, filter_two_imag, real_third[0], imag_third[0])
    grad_gated = signals_back(correlated_two[0][None], correlated_two[1][None])[0]
    grad_one = grad_gated * first_conv
    back_one = grad_gated * gate_one
    real_fourth, imag_fourth = spectra(back_one[None])
    filter_one_real, filter_one_imag = (real_first[1], imag_first[1])
    correlated_one = conj_product(filter_one_real, filter_one_imag, real_fourth[0], imag_fourth[0])
    grad_value = signals_back(correlated_one[0][None], correlated_one[1][None])[0]
    stream_cot = jnp.stack([grad_value, grad_one, grad_two]).astype(jnp.bfloat16)
    next_one = next_rows(stream_cot)
    next_two = next_rows(next_one)
    stream_grads = (
        tap_weight(0) * stream_cot + tap_weight(1) * next_one + tap_weight(2) * next_two
    ).astype(jnp.bfloat16)
    cot_float = stream_cot.astype(jnp.float32)
    tap_terms = jnp.stack(
        [
            jnp.sum(cot_float * streams, axis=(1, 2)),
            jnp.sum(cot_float * prev_one, axis=(1, 2)),
            jnp.sum(cot_float * prev_two, axis=(1, 2)),
        ],
        axis=1,
    )
    tap_total = lax.psum(tap_terms, "seq")
    return (layer_out, stream_grads, tap_total * (1.0 / math.sqrt(block_rows * seq_count)))


def local(streams, short_taps, long_filters, out_grad):
    count = lax.axis_size("seq")
    _, local_rows, blocks, channels = streams.shape
    rows = local_rows * count
    fits = (
        channels == LANES * count
        and count & (count - 1) == 0
        and blocks == 8
        and rows == LANES
        and local_rows >= TAPS - 1
    )
    work = short_local if fits else long_local
    return work(streams, short_taps, long_filters, out_grad)


def solution(mesh):
    in_specs = (
        P(None, "seq", "group", "tensor"),
        P(None, None, "tensor"),
        P(None, "seq", None, "tensor"),
        P("seq", "group", "tensor"),
    )
    out_specs = (
        P("seq", "group", "tensor"),
        P(None, "seq", "group", "tensor"),
        P("group", None, "tensor"),
    )
    return jax.shard_map(local, mesh=mesh, in_specs=in_specs, out_specs=out_specs, check_vma=False)
```

```python
import functools
import math

import jax
import jax.numpy as jnp
import numpy as np
from jax import lax
from jax.experimental import pallas as pl
from jax.experimental.pallas import tpu as pltpu
from jax.sharding import PartitionSpec as P

HIGHEST_PRECISION = lax.Precision.HIGHEST
BF16 = jnp.bfloat16
F32 = jnp.float32
LANES = 128
TAPS = 3
TAP_ROWS = 16
CHUNK = 16
VMEM_LIMIT = 40 * 1024 * 1024


def split_bf16(value):
    high = value.astype(BF16)
    return high, (value - high.astype(F32)).astype(BF16)


def odd_transform(parts):
    count = len(parts)
    if count == 1:
        return [(parts[0], None)]
    even = odd_transform(parts[0::2])
    odd = odd_transform(parts[1::2])
    low, high = [], []
    for j in range(count // 2):
        angle = math.pi * (2 * j + 1) / (2 * count)
        cos, sin = math.cos(angle), math.sin(angle)
        even_real, even_imag = even[j]
        odd_real, odd_imag = odd[j]
        if odd_imag is None:
            turn_real, turn_imag = odd_real * cos, odd_real * -sin
            low.append((even_real + turn_real, turn_imag))
            high.append((even_real - turn_real, turn_imag))
        else:
            turn_real = odd_real * cos + odd_imag * sin
            turn_imag = odd_imag * cos - odd_real * sin
            low.append((even_real + turn_real, even_imag + turn_imag))
            high.append((even_real - turn_real, turn_imag - even_imag))
    return low + high[::-1]


def odd_transform_back(slots):
    count = len(slots)
    if count == 1:
        return [slots[0][0]]
    even, odd = [], []
    for j in range(count // 2):
        angle = math.pi * (2 * j + 1) / (2 * count)
        cos, sin = math.cos(angle), math.sin(angle)
        low_real, low_imag = slots[j]
        high_real, high_imag = slots[count - 1 - j]
        diff_real = low_real - high_real
        sum_imag = low_imag + high_imag
        if count == 2:
            even.append((low_real + high_real, None))
            odd.append((diff_real * cos - sum_imag * sin, None))
        else:
            even.append((low_real + high_real, low_imag - high_imag))
            odd.append((diff_real * cos - sum_imag * sin, sum_imag * cos + diff_real * sin))
    even_out = odd_transform_back(even)
    odd_out = odd_transform_back(odd)
    return [part for pair in zip(even_out, odd_out) for part in pair]


def transform_tables(blocks, rows):
    length = blocks * rows
    slot = np.arange(blocks)[:, None, None]
    freq = np.arange(rows)[None, :, None]
    pos = np.arange(rows)[None, None, :]
    number = ((2 * slot + 1 + 4 * blocks * freq) * pos) % (4 * length)
    angle = number * (np.pi / (2 * length))
    cos, sin = np.cos(angle), np.sin(angle)
    forward = np.concatenate(
        [np.concatenate([cos, sin], axis=2), np.concatenate([-sin, cos], axis=2)], axis=1
    )
    back = np.swapaxes(forward, 1, 2) / length

    def halves(table):
        high = table.astype(BF16)
        low = (table - high.astype(np.float64)).astype(BF16)
        return np.concatenate([high, low], axis=1)

    return halves(forward), halves(back)


def shift_blocks(edge, blocks, by):
    rolled = pltpu.roll(edge, by % edge.shape[0], 0)
    block = lax.broadcasted_iota(jnp.int32, edge.shape, 0) % blocks
    empty = 0 if by > 0 else blocks - 1
    return jnp.where(block == empty, 0.0, rolled)


def run_copies(pairs, sems):
    copies = [
        pltpu.make_async_copy(source, target, sems.at[n])
        for n, (source, target) in enumerate(pairs)
    ]
    for copy in copies:
        copy.start()
    for copy in copies:
        copy.wait()


def pack_kernel(me_ref, group_ref, streams_ref, filters_ref, grad_ref, *refs):
    outs, sems = refs[:-1], refs[-1]
    me, group = me_ref[0], group_ref[0]
    slab = grad_ref.shape[0]
    pairs = []
    for by, out in zip(asking_order(len(outs)), outs):
        lanes = pl.ds(pl.multiple_of((me ^ by) * LANES, LANES), LANES)
        filters = pl.ds(0, 2 * slab)
        if out.shape[0] == 5 * slab:
            filters = pl.ds(pl.multiple_of(group * slab, slab), slab)
        at = 0
        for source in (
            streams_ref.at[:, lanes],
            grad_ref.at[:, lanes],
            filters_ref.at[filters, lanes],
        ):
            size = source.shape[0]
            pairs.append((source, out.at[pl.ds(at, size)]))
            at += size
    run_copies(pairs, sems)


def swap_kernel(*refs):
    out = refs[-1]
    slab = out.shape[0] // (len(refs) - 1)
    for n, msg in enumerate(refs[:-1]):
        out[n * slab : (n + 1) * slab] = msg[4 * slab : 5 * slab]


def tables_kernel(me_ref, packed_ref, taps_ref, forward_ref, back_ref, *refs):
    del packed_ref
    outs, sems = refs[:-1], refs[-1]
    lanes = pl.ds(pl.multiple_of(me_ref[0] * LANES, LANES), LANES)
    sources = (taps_ref.at[:, :, lanes], forward_ref, back_ref)
    run_copies(zip(sources, outs), sems)


class Transforms:
    def __init__(self, rows, fwd_ref, back_ref, high, low):
        self.rows, self.fwd, self.back, self.high, self.low = rows, fwd_ref, back_ref, high, low
        self.blocks = fwd_ref.shape[0]

    def store(self, parts, row, col):
        for j, (real, imag) in enumerate(odd_transform(parts)):
            for at, value in ((row, real), (self.rows + row, imag)):
                high, low = split_bf16(value)
                self.high[j, pl.ds(at, CHUNK), col : col + LANES] = high
                self.low[j, pl.ds(at, CHUNK), col : col + LANES] = low

    def times(self, table, j, high, low):
        size = 2 * self.rows
        main = jnp.dot(table[j, 0:size], high, preferred_element_type=F32)
        main += jnp.dot(table[j, 0:size], low, preferred_element_type=F32)
        return main + jnp.dot(table[j, size : 2 * size], high, preferred_element_type=F32)

    def forward(self, j, begin, end):
        return self.times(self.fwd, j, self.high[j, :, begin:end], self.low[j, :, begin:end])

    def backward(self, j, data):
        return self.times(self.back, j, *split_bf16(data))

    def blocks_of(self, slots, row, col):
        return odd_transform_back(
            [
                (
                    slots[j, pl.ds(row, CHUNK), col : col + LANES],
                    slots[j, pl.ds(self.rows + row, CHUNK), col : col + LANES],
                )
                for j in range(self.blocks)
            ]
        )

    def each_slot(self, body):
        for j in range(self.blocks):
            body(j)

    def each_chunk(self, body):
        @pl.loop(0, self.rows // CHUNK, unroll=8)
        def _(step):
            body(pl.multiple_of(step * CHUNK, CHUNK))


def spread(blocks, row, block):
    return pl.ds(row * blocks + block, CHUNK, stride=blocks)


def product(left, right, conjugate=False):
    rows = left.shape[0] // 2
    a_real, a_imag, b_real, b_imag = left[:rows], left[rows:], right[:rows], right[rows:]
    if conjugate:
        real, imag = a_real * b_real + a_imag * b_imag, a_imag * b_real - a_real * b_imag
    else:
        real, imag = a_real * b_real - a_imag * b_imag, a_real * b_imag + a_imag * b_real
    return jnp.concatenate([real, imag], axis=0)


def filtered(raw, weights, s, at, blocks, size):
    now = weights[s, 0:1] * raw[pl.ds(at + 2 * blocks, size)]
    now = now + weights[s, 1:2] * raw[pl.ds(at + blocks, size)]
    return (now + weights[s, 2:3] * raw[pl.ds(at, size)]).astype(BF16).astype(F32)


def core_kernel(blocks, count, me_ref, group_ref, *refs):
    weights, fwd_ref, back_ref = refs[:3]
    msgs, swapped, refs = refs[3 : 3 + count], refs[3 + count], refs[4 + count :]
    outs, scratch = refs[:count], refs[count:]
    raw, sig, gate, grad, high, low, spec, turned, cot, conv, grads = scratch
    me, group = me_ref[0], group_ref[0]
    total = sig.shape[1]
    rows = total // blocks
    slab = total // count
    halo = (TAPS - 1) * blocks

    def weight(stream, tap):
        return weights[stream, tap : tap + 1]

    taken = 0
    for by, msg in zip(asking_order(count), msgs):
        start = pl.multiple_of((me ^ by) * slab, slab)
        for s in range(3):
            raw[s, pl.ds(halo + start, slab)] = msg[s * slab : (s + 1) * slab].astype(F32)
        grad[pl.ds(start, slab)] = msg[3 * slab : 4 * slab].astype(F32)
        if msg.shape[0] == 5 * slab:
            sig[group, pl.ds(start, slab)] = msg[4 * slab :].astype(F32)
            other = swapped[taken * slab : (taken + 1) * slab]
            sig[1 - group, pl.ds(start, slab)] = other.astype(F32)
            taken += 1
        else:
            for f in range(2):
                sig[f, pl.ds(start, slab)] = msg[(4 + f) * slab : (5 + f) * slab].astype(F32)
    for s in range(3):
        raw[s, 0:halo] = shift_blocks(raw[s, total : total + halo], blocks, 1)

    @pl.loop(0, total // slab)
    def _(step):
        base = pl.multiple_of(step * slab, slab)
        sig[2, pl.ds(base, slab)] = filtered(raw.at[0], weights, 0, base, blocks, slab)
        gate[pl.ds(base, slab)] = filtered(raw.at[1], weights, 1, base, blocks, slab)
        gate_two = filtered(raw.at[2], weights, 2, base, blocks, slab)
        sig[3, pl.ds(base, slab)] = gate_two * grad[pl.ds(base, slab)]

    work = Transforms(rows, fwd_ref, back_ref, high, low)

    def butterflies(row, signals):
        for s in signals:
            parts = [sig[s, spread(blocks, row, b)] for b in range(blocks)]
            work.store(parts, row, s * LANES)

    work.each_chunk(functools.partial(butterflies, signals=(0, 1)))
    steps = rows // CHUNK
    for j in range(max(blocks, steps)):
        if j < blocks:
            spec[j] = work.forward(j, 0, 2 * LANES)
        if j < steps:
            butterflies(j * CHUNK, (2, 3))

    def forward_data(j):
        turned[j] = work.forward(j, 2 * LANES, 4 * LANES)

    def first_products(j):
        data = turned[j]
        left = product(data[:, :LANES], spec[j, :, :LANES])
        right = product(data[:, LANES:], spec[j, :, LANES:], True)
        turned[j] = work.backward(j, jnp.concatenate([left, right], axis=1))

    work.each_slot(forward_data)
    work.each_slot(first_products)

    def gates(row):
        first = work.blocks_of(turned, row, 0)
        gated_grad = work.blocks_of(turned, row, LANES)
        forward, backward = [], []
        for b in range(blocks):
            here = spread(blocks, row, b)
            gate_one = gate[here]
            cot[1, here] = (gated_grad[b] * first[b]).astype(BF16).astype(F32)
            forward.append(gate_one * first[b])
            backward.append(gate_one * gated_grad[b])
        work.store(forward, row, 0)
        work.store(backward, row, LANES)

    work.each_chunk(gates)

    def convolve(j):
        data = work.forward(j, 0, 2 * LANES)
        left = product(data[:, :LANES], spec[j, :, LANES:])
        right = product(data[:, LANES:], spec[j, :, :LANES], True)
        turned[j] = work.backward(j, jnp.concatenate([left, right], axis=1))

    work.each_slot(convolve)

    def last(row):
        second = work.blocks_of(turned, row, 0)
        value_grad = work.blocks_of(turned, row, LANES)
        for b in range(blocks):
            here = spread(blocks, row, b)
            conv[here] = second[b]
            cot[0, here] = value_grad[b].astype(BF16).astype(F32)

    work.each_chunk(last)
    for s in range(2):
        cot[s, total : total + halo] = shift_blocks(cot[s, 0:halo], blocks, -1)

    def finish(step, sums):
        base = pl.multiple_of(step * slab, slab)
        here = [cot[s, pl.ds(base, slab)] for s in range(2)]
        last = (grad[pl.ds(base, slab)] * conv[pl.ds(base, slab)]).astype(BF16).astype(F32)
        cot[2, pl.ds(base, slab)] = last
        here.append(last)
        for s in range(2):
            next_one = cot[s, pl.ds(base + blocks, slab)]
            next_two = cot[s, pl.ds(base + 2 * blocks, slab)]
            grads[s, pl.ds(base, slab)] = (
                weight(s, 0) * here[s] + weight(s, 1) * next_one + weight(s, 2) * next_two
            ).astype(BF16)
        added = []
        for s in range(3):
            for tap in range(TAPS):
                term = here[s] * raw[s, pl.ds(base + (TAPS - 1 - tap) * blocks, slab)]
                added.append(jnp.sum(term.reshape(slab // 8, 8, LANES), axis=0))
        return tuple(a + b for a, b in zip(sums, added))

    zeros = tuple(jnp.zeros((8, LANES), F32) for _ in range(3 * TAPS))
    sums = lax.fori_loop(0, total // slab, finish, zeros)
    cot[2, total : total + halo] = shift_blocks(cot[2, 0:halo], blocks, -1)
    scale = 1.0 / math.sqrt(total)
    tap_rows = [jnp.sum(part, axis=0, keepdims=True) * scale for part in sums]
    pad = jnp.zeros((TAP_ROWS - 3 * TAPS, LANES), F32)
    tap_block = jnp.concatenate(tap_rows + [pad], axis=0).astype(BF16)
    for k, by in enumerate(answering_order(count)):
        start = pl.multiple_of((me ^ by) * slab, slab)
        outs[k][0:slab] = conv[pl.ds(start, slab)].astype(BF16)
        for s in range(2):
            at = (s + 1) * slab
            outs[k][at : at + slab] = grads[s, pl.ds(start, slab)]
        at = 3 * slab
        now, prev_one, prev_two = (raw[2, pl.ds(start + j * blocks, halo)] for j in (2, 1, 0))
        gate_two = weight(2, 0) * now + weight(2, 1) * prev_one + weight(2, 2) * prev_two
        first = gate_two.astype(BF16).astype(F32) * conv[pl.ds(start, halo)]
        outs[k][at : at + halo] = first.astype(BF16)
        at += halo
        begin = start + slab - halo
        now, next_one, next_two = (cot[2, pl.ds(begin + j * blocks, halo)] for j in range(TAPS))
        end = weight(2, 0) * now + weight(2, 1) * next_one + weight(2, 2) * next_two
        outs[k][at : at + halo] = end.astype(BF16)
        at += halo
        outs[k][at:] = tap_block


def home_kernel(blocks, partners, me_ref, *refs):
    msgs = refs[:partners]
    stream_ref, grad_ref, taps_ref = refs[partners : partners + 3]
    layer_ref, grads_ref, tap_ref = refs[partners + 3 :]
    me = me_ref[0]
    slab = stream_ref.shape[0]
    halo = (TAPS - 1) * blocks
    rest = slab - halo
    for k, by in enumerate(answering_order(partners)):
        lanes = pl.ds(pl.multiple_of((me ^ by) * LANES, LANES), LANES)
        msg = msgs[k]
        conv = msg[0:slab].astype(F32)
        tap = [taps_ref[2, j : j + 1, lanes] for j in range(TAPS)]
        stream = stream_ref[:, lanes].astype(F32)
        gate = tap[0] * stream[halo:] + tap[1] * stream[blocks : blocks + rest]
        gate = (gate + tap[2] * stream[:rest]).astype(BF16).astype(F32)
        layer_ref[0:halo, lanes] = msg[3 * slab : 3 * slab + halo]
        layer_ref[halo:slab, lanes] = (gate * conv[halo:]).astype(BF16)
        cot = (grad_ref[:, lanes].astype(F32) * conv).astype(BF16).astype(F32)
        last = tap[0] * cot[:rest] + tap[1] * cot[blocks : blocks + rest] + tap[2] * cot[halo:]
        grads_ref[0 : 2 * slab, lanes] = msg[slab : 3 * slab]
        grads_ref[2 * slab : 3 * slab - halo, lanes] = last.astype(BF16)
        grads_ref[3 * slab - halo : 3 * slab, lanes] = msg[3 * slab + halo : 3 * slab + 2 * halo]
        block = msg[3 * slab + 2 * halo :].astype(F32)
        for s in range(3):
            tap_ref[s, :, lanes] = block[s * TAPS : (s + 1) * TAPS]


def asking_order(count):
    return [0, 4, 3, 2, 5, 6, 7, 1] if count == 8 else list(range(count))


def answering_order(count):
    return [0, 1, 2, 4, 3, 5, 7, 6] if count == 8 else list(range(count))


def filters_once(count, groups):
    return list(range(count // 2, count - 1)) if groups == 2 else []


def everyone(messages, order):
    count = len(messages)
    out = [messages[0]]
    for by, message in zip(order[1:], messages[1:]):
        out.append(lax.ppermute(message, "seq", [(i, i ^ by) for i in range(count)]))
    return out


def whole_specs(count):
    return [pl.BlockSpec(memory_space=pltpu.VMEM) for _ in range(count)]


def in_hbm(array):
    return pltpu.with_memory_space_constraint(array, pltpu.HBM)


def shape(*dims, dtype=BF16):
    return jax.ShapeDtypeStruct(dims, dtype)


def call(kernel, name, out_shape, in_specs, scratch=()):
    return pl.pallas_call(
        kernel,
        out_shape=out_shape,
        in_specs=in_specs,
        out_specs=whole_specs(len(out_shape)),
        scratch_shapes=list(scratch),
        compiler_params=pltpu.CompilerParams(vmem_limit_bytes=VMEM_LIMIT),
        name=name,
    )


def core_call(place, group, tables, messages, swapped, blocks):
    count = len(messages)
    slab = messages[0].shape[0] // 6
    total = slab * count
    spectrum = (blocks, 2 * total // blocks)
    halo = (TAPS - 1) * blocks
    return call(
        functools.partial(core_kernel, blocks, count),
        "core",
        [shape(3 * slab + 2 * halo + TAP_ROWS, LANES)] * count,
        [pl.BlockSpec(memory_space=pltpu.SMEM)] * 2 + whole_specs(count + 4),
        [
            pltpu.VMEM((3, halo + total, LANES), F32),
            pltpu.VMEM((4, total, LANES), F32),
            pltpu.VMEM((total, LANES), F32),
            pltpu.VMEM((total, LANES), F32),
            pltpu.VMEM((*spectrum, 4 * LANES), BF16),
            pltpu.VMEM((*spectrum, 4 * LANES), BF16),
            pltpu.VMEM((*spectrum, 2 * LANES), F32),
            pltpu.VMEM((*spectrum, 2 * LANES), F32),
            pltpu.VMEM((3, total + halo, LANES), F32),
            pltpu.VMEM((total, LANES), F32),
            pltpu.VMEM((2, total, LANES), BF16),
        ],
    )(place, group, *tables, *messages, swapped)


def short_local(streams, short_taps, long_filters, out_grad):
    count = lax.axis_size("seq")
    groups = lax.axis_size("group")
    place = lax.axis_index("seq").astype(jnp.int32)[None]
    group = lax.axis_index("group").astype(jnp.int32)[None]
    order = asking_order(count)
    once = filters_once(count, groups)
    _, local_rows, blocks, channels = streams.shape
    slab = local_rows * blocks
    flat_streams = streams.reshape(3 * slab, channels)
    flat_filters = long_filters.reshape(2 * slab, channels)
    flat_grad = out_grad.reshape(slab, channels)
    scalar = pl.BlockSpec(memory_space=pltpu.SMEM)
    anywhere = pl.BlockSpec(memory_space=pl.ANY)

    packed = call(
        pack_kernel,
        "pack",
        [shape((5 if by in once else 6) * slab, LANES) for by in order],
        [scalar] * 2 + [anywhere] * 3,
        [pltpu.SemaphoreType.DMA((3 * count,))],
    )(place, group, in_hbm(flat_streams), in_hbm(flat_filters), in_hbm(flat_grad))
    messages = everyone(packed, order)
    swapped = jnp.zeros((16, LANES), BF16)
    if once:
        halves = [message for by, message in zip(order, messages) if by in once]
        (mine,) = call(
            swap_kernel, "swap", [shape(len(once) * slab, LANES)], whole_specs(len(once))
        )(*halves)
        swapped = lax.ppermute(mine, "group", [(0, 1), (1, 0)])
    forward, back = transform_tables(blocks, local_rows * count)
    tables = call(
        tables_kernel,
        "tables",
        [shape(3, TAPS, LANES, dtype=F32), shape(*forward.shape), shape(*back.shape)],
        [scalar] + [anywhere] * 4,
        [pltpu.SemaphoreType.DMA((3,))],
    )(
        place,
        packed[0],
        in_hbm(short_taps),
        in_hbm(jnp.asarray(forward)),
        in_hbm(jnp.asarray(back)),
    )
    answers = core_call(place, group, tables, messages, swapped, blocks)
    returned = everyone(answers, answering_order(count))
    layer_out, stream_grads, tap_grads = call(
        functools.partial(home_kernel, blocks, count),
        "home",
        [
            shape(slab, channels),
            shape(3 * slab, channels),
            shape(3, TAPS, channels, dtype=F32),
        ],
        [scalar] + whole_specs(count + 3),
    )(place, *returned, flat_streams[2 * slab :], flat_grad, short_taps)
    return (
        layer_out.reshape(out_grad.shape),
        stream_grads.reshape(streams.shape),
        tap_grads,
    )


def shifted(value, axis, by):
    count = lax.axis_size(axis)
    return lax.ppermute(value, axis, [(i, (i + by) % count) for i in range(count)])


def complex_product(left_real, left_imag, right_real, right_imag):
    return (
        left_real * right_real - left_imag * right_imag,
        left_real * right_imag + left_imag * right_real,
    )


def conj_product(left_real, left_imag, right_real, right_imag):
    return (
        left_real * right_real + left_imag * right_imag,
        left_real * right_imag - left_imag * right_real,
    )


def long_local(streams, short_taps, long_filters, out_grad):
    seq_count = lax.axis_size("seq")
    seq_place = lax.axis_index("seq")
    local_rows = streams.shape[1]
    channels = streams.shape[3]
    block_rows = local_rows * seq_count
    full_length = 2 * block_rows * seq_count
    angle_unit = math.pi / full_length
    block_pos = jnp.arange(seq_count, dtype=jnp.int32)
    odd_slots = 2 * block_pos + 1
    local_index = seq_place * local_rows + jnp.arange(local_rows, dtype=jnp.int32)
    row_pos = jnp.arange(block_rows, dtype=jnp.int32)
    start_pos = block_pos[None, :, None] * block_rows + local_index[:, None, None]
    fwd_angle = (start_pos * odd_slots[None, None, :] % (2 * full_length)).astype(
        jnp.float32
    ) * angle_unit
    fwd_table = jnp.stack([jnp.cos(fwd_angle), -jnp.sin(fwd_angle)], axis=-1)
    inner_angle = (row_pos[:, None] * row_pos[None, :] % block_rows).astype(jnp.float32) * (
        2.0 * math.pi / block_rows
    )
    inner_cos = jnp.cos(inner_angle)
    inner_sin = jnp.sin(inner_angle)
    inner_table = jnp.stack(
        [jnp.stack([inner_cos, -inner_sin], axis=-1), jnp.stack([inner_sin, inner_cos], axis=-1)],
        axis=0,
    )
    back_num = (
        row_pos[None, :]
        * (4 * seq_count * row_pos[:, None] + 2 * seq_place + 1)
        % (2 * full_length)
    )
    back_angle = back_num.astype(jnp.float32) * angle_unit
    back_cos = jnp.cos(back_angle)
    back_sin = jnp.sin(back_angle)
    back_table = jnp.stack(
        [jnp.stack([back_cos, back_sin], axis=-1), jnp.stack([-back_sin, back_cos], axis=-1)],
        axis=0,
    )
    outer_angle = (block_pos[:, None] * odd_slots[None, :] % (4 * seq_count)).astype(
        jnp.float32
    ) * (math.pi / (2 * seq_count))
    outer_table = jnp.stack([jnp.cos(outer_angle).T, -jnp.sin(outer_angle).T], axis=0)

    def previous_rows(block):
        edge = shifted(block[:, -1:], "seq", 1)
        rolled = jnp.concatenate([jnp.zeros_like(edge[:, :, :1]), edge[:, :, :-1]], axis=2)
        edge = jnp.where(seq_place == 0, rolled, edge)
        return jnp.concatenate([edge, block[:, :-1]], axis=1)

    def next_rows(block):
        edge = shifted(block[:, :1], "seq", -1)
        rolled = jnp.concatenate([edge[:, :, 1:], jnp.zeros_like(edge[:, :, :1])], axis=2)
        edge = jnp.where(seq_place == seq_count - 1, rolled, edge)
        return jnp.concatenate([block[:, 1:], edge], axis=1)

    def spectra(signals):
        count = signals.shape[0]
        twisted = jnp.einsum("simc,imjr->srijc", signals, fwd_table, precision=HIGHEST_PRECISION)
        slotted = lax.all_to_all(twisted, "seq", split_axis=3, concat_axis=2, tiled=True)
        slotted = slotted.reshape(count, 2, block_rows, channels)
        spec = jnp.einsum("sric,rikq->sqkc", slotted, inner_table, precision=HIGHEST_PRECISION)
        return (spec[:, 0], spec[:, 1])

    def signals_back(real_spec, imag_spec):
        count = real_spec.shape[0]
        stacked = jnp.stack([real_spec, imag_spec], axis=1)
        turned = jnp.einsum("srkc,rkiq->sqic", stacked, back_table, precision=HIGHEST_PRECISION)
        turned = turned.reshape(count, 2, block_rows, 1, channels)
        parts = lax.all_to_all(turned, "seq", split_axis=2, concat_axis=3, tiled=True)
        rows_out = jnp.einsum("srijc,rjm->simc", parts, outer_table, precision=HIGHEST_PRECISION)
        return rows_out * (2.0 / full_length)

    def tap_weight(index):
        return short_taps[:, index][:, None, None, :]

    prev_one = previous_rows(streams)
    prev_two = previous_rows(prev_one)
    filtered = (
        tap_weight(0) * streams + tap_weight(1) * prev_one + tap_weight(2) * prev_two
    ).astype(jnp.bfloat16)
    value_stream = filtered[0].astype(jnp.float32)
    gate_one = filtered[1].astype(jnp.float32)
    gate_two = filtered[2].astype(jnp.float32)
    filters = long_filters.astype(jnp.float32)
    real_first, imag_first = spectra(jnp.stack([value_stream, filters[0]]))
    product_one = complex_product(real_first[0], imag_first[0], real_first[1], imag_first[1])
    first_conv = signals_back(product_one[0][None], product_one[1][None])[0]
    gated_first = gate_one * first_conv
    real_second, imag_second = spectra(jnp.stack([gated_first, filters[1]]))
    product_two = complex_product(real_second[0], imag_second[0], real_second[1], imag_second[1])
    second_conv = signals_back(product_two[0][None], product_two[1][None])[0]
    layer_out = (gate_two * second_conv).astype(jnp.bfloat16)
    cotangent = out_grad.astype(jnp.float32)
    back_two = cotangent * gate_two
    grad_two = cotangent * second_conv
    real_third, imag_third = spectra(back_two[None])
    filter_two_real, filter_two_imag = (real_second[1], imag_second[1])
    correlated_two = conj_product(filter_two_real, filter_two_imag, real_third[0], imag_third[0])
    grad_gated = signals_back(correlated_two[0][None], correlated_two[1][None])[0]
    grad_one = grad_gated * first_conv
    back_one = grad_gated * gate_one
    real_fourth, imag_fourth = spectra(back_one[None])
    filter_one_real, filter_one_imag = (real_first[1], imag_first[1])
    correlated_one = conj_product(filter_one_real, filter_one_imag, real_fourth[0], imag_fourth[0])
    grad_value = signals_back(correlated_one[0][None], correlated_one[1][None])[0]
    stream_cot = jnp.stack([grad_value, grad_one, grad_two]).astype(jnp.bfloat16)
    next_one = next_rows(stream_cot)
    next_two = next_rows(next_one)
    stream_grads = (
        tap_weight(0) * stream_cot + tap_weight(1) * next_one + tap_weight(2) * next_two
    ).astype(jnp.bfloat16)
    cot_float = stream_cot.astype(jnp.float32)
    tap_terms = jnp.stack(
        [
            jnp.sum(cot_float * streams, axis=(1, 2)),
            jnp.sum(cot_float * prev_one, axis=(1, 2)),
            jnp.sum(cot_float * prev_two, axis=(1, 2)),
        ],
        axis=1,
    )
    tap_total = lax.psum(tap_terms, "seq")
    return (layer_out, stream_grads, tap_total * (1.0 / math.sqrt(block_rows * seq_count)))


def local(streams, short_taps, long_filters, out_grad):
    count = lax.axis_size("seq")
    _, local_rows, blocks, channels = streams.shape
    rows = local_rows * count
    fits = (
        channels == LANES * count
        and count & (count - 1) == 0
        and blocks == 8
        and rows == LANES
        and local_rows >= TAPS - 1
    )
    work = short_local if fits else long_local
    return work(streams, short_taps, long_filters, out_grad)


def solution(mesh):
    in_specs = (
        P(None, "seq", "group", "tensor"),
        P(None, None, "tensor"),
        P(None, "seq", None, "tensor"),
        P("seq", "group", "tensor"),
    )
    out_specs = (
        P("seq", "group", "tensor"),
        P(None, "seq", "group", "tensor"),
        P("group", None, "tensor"),
    )
    return jax.shard_map(local, mesh=mesh, in_specs=in_specs, out_specs=out_specs, check_vma=False)
```

```python
import functools
import math

import jax
import jax.numpy as jnp
import numpy as np
from jax import lax
from jax.experimental import pallas as pl
from jax.experimental.pallas import tpu as pltpu
from jax.sharding import PartitionSpec as P

HIGHEST_PRECISION = lax.Precision.HIGHEST
BF16 = jnp.bfloat16
F32 = jnp.float32
LANES = 128
TAPS = 3
TAP_ROWS = 16
CHUNK = 16
VMEM_LIMIT = 40 * 1024 * 1024


def split_bf16(value):
    high = value.astype(BF16)
    return high, (value - high.astype(F32)).astype(BF16)


def odd_transform(parts):
    count = len(parts)
    if count == 1:
        return [(parts[0], None)]
    even = odd_transform(parts[0::2])
    odd = odd_transform(parts[1::2])
    low, high = [], []
    for j in range(count // 2):
        angle = math.pi * (2 * j + 1) / (2 * count)
        cos, sin = math.cos(angle), math.sin(angle)
        even_real, even_imag = even[j]
        odd_real, odd_imag = odd[j]
        if odd_imag is None:
            turn_real, turn_imag = odd_real * cos, odd_real * -sin
            low.append((even_real + turn_real, turn_imag))
            high.append((even_real - turn_real, turn_imag))
        else:
            turn_real = odd_real * cos + odd_imag * sin
            turn_imag = odd_imag * cos - odd_real * sin
            low.append((even_real + turn_real, even_imag + turn_imag))
            high.append((even_real - turn_real, turn_imag - even_imag))
    return low + high[::-1]


def odd_transform_back(slots):
    count = len(slots)
    if count == 1:
        return [slots[0][0]]
    even, odd = [], []
    for j in range(count // 2):
        angle = math.pi * (2 * j + 1) / (2 * count)
        cos, sin = math.cos(angle), math.sin(angle)
        low_real, low_imag = slots[j]
        high_real, high_imag = slots[count - 1 - j]
        diff_real = low_real - high_real
        sum_imag = low_imag + high_imag
        if count == 2:
            even.append((low_real + high_real, None))
            odd.append((diff_real * cos - sum_imag * sin, None))
        else:
            even.append((low_real + high_real, low_imag - high_imag))
            odd.append((diff_real * cos - sum_imag * sin, sum_imag * cos + diff_real * sin))
    even_out = odd_transform_back(even)
    odd_out = odd_transform_back(odd)
    return [part for pair in zip(even_out, odd_out) for part in pair]


def transform_tables(blocks, rows):
    length = blocks * rows
    slot = np.arange(blocks)[:, None, None]
    freq = np.arange(rows)[None, :, None]
    pos = np.arange(rows)[None, None, :]
    number = ((2 * slot + 1 + 4 * blocks * freq) * pos) % (4 * length)
    angle = number * (np.pi / (2 * length))
    cos, sin = np.cos(angle), np.sin(angle)
    forward = np.concatenate(
        [np.concatenate([cos, sin], axis=2), np.concatenate([-sin, cos], axis=2)], axis=1
    )
    back = np.swapaxes(forward, 1, 2) / length

    def halves(table):
        high = table.astype(BF16)
        low = (table - high.astype(np.float64)).astype(BF16)
        return np.concatenate([high, low], axis=1)

    return halves(forward), halves(back)


def shift_blocks(edge, blocks, by):
    rolled = pltpu.roll(edge, by % edge.shape[0], 0)
    block = lax.broadcasted_iota(jnp.int32, edge.shape, 0) % blocks
    empty = 0 if by > 0 else blocks - 1
    return jnp.where(block == empty, 0.0, rolled)


def run_copies(pairs, sems):
    copies = [
        pltpu.make_async_copy(source, target, sems.at[n])
        for n, (source, target) in enumerate(pairs)
    ]
    for copy in copies:
        copy.start()
    for copy in copies:
        copy.wait()


def message_pairs(out, lanes, group, streams_ref, filters_ref, grad_ref):
    slab = grad_ref.shape[0]
    filters = pl.ds(0, 2 * slab)
    if out.shape[0] == 5 * slab:
        filters = pl.ds(pl.multiple_of(group * slab, slab), slab)
    sources = (
        streams_ref.at[:, lanes],
        grad_ref.at[:, lanes],
        filters_ref.at[filters, lanes],
    )
    at, pairs = 0, []
    for source in sources:
        size = source.shape[0]
        pairs.append((source, out.at[pl.ds(at, size)]))
        at += size
    return pairs


def pack_kernel(me_ref, group_ref, streams_ref, filters_ref, grad_ref, *refs):
    outs, sems = refs[:-1], refs[-1]
    me, group = me_ref[0], group_ref[0]
    pairs = []
    for by, out in zip(asking_order(len(outs) + 1)[1:], outs):
        lanes = pl.ds(pl.multiple_of((me ^ by) * LANES, LANES), LANES)
        pairs += message_pairs(out, lanes, group, streams_ref, filters_ref, grad_ref)
    run_copies(pairs, sems)


def swap_kernel(*refs):
    out = refs[-1]
    slab = out.shape[0] // (len(refs) - 1)
    for n, msg in enumerate(refs[:-1]):
        out[n * slab : (n + 1) * slab] = msg[4 * slab : 5 * slab]


def tables_kernel(me_ref, packed_ref, taps_ref, forward_ref, back_ref, *refs):
    del packed_ref
    arrays, outs, sems = refs[:3], refs[3:-1], refs[-1]
    lanes = pl.ds(pl.multiple_of(me_ref[0] * LANES, LANES), LANES)
    sources = (taps_ref.at[:, :, lanes], forward_ref, back_ref)
    pairs = list(zip(sources, outs)) + message_pairs(outs[3], lanes, None, *arrays)
    run_copies(pairs, sems)


class Transforms:
    def __init__(self, rows, fwd_ref, back_ref, high, low):
        self.rows, self.fwd, self.back, self.high, self.low = rows, fwd_ref, back_ref, high, low
        self.blocks = fwd_ref.shape[0]

    def store(self, parts, row, col):
        for j, (real, imag) in enumerate(odd_transform(parts)):
            for at, value in ((row, real), (self.rows + row, imag)):
                high, low = split_bf16(value)
                self.high[j, pl.ds(at, CHUNK), col : col + LANES] = high
                self.low[j, pl.ds(at, CHUNK), col : col + LANES] = low

    def times(self, table, j, high, low):
        size = 2 * self.rows
        main = jnp.dot(table[j, 0:size], high, preferred_element_type=F32)
        main += jnp.dot(table[j, 0:size], low, preferred_element_type=F32)
        return main + jnp.dot(table[j, size : 2 * size], high, preferred_element_type=F32)

    def forward(self, j, begin, end):
        return self.times(self.fwd, j, self.high[j, :, begin:end], self.low[j, :, begin:end])

    def backward(self, j, data):
        return self.times(self.back, j, *split_bf16(data))

    def blocks_of(self, slots, row, col):
        return odd_transform_back(
            [
                (
                    slots[j, pl.ds(row, CHUNK), col : col + LANES],
                    slots[j, pl.ds(self.rows + row, CHUNK), col : col + LANES],
                )
                for j in range(self.blocks)
            ]
        )

    def each_slot(self, body):
        for j in range(self.blocks):
            body(j)

    def each_chunk(self, body):
        @pl.loop(0, self.rows // CHUNK, unroll=8)
        def _(step):
            body(pl.multiple_of(step * CHUNK, CHUNK))


def spread(blocks, row, block):
    return pl.ds(row * blocks + block, CHUNK, stride=blocks)


def product(left, right, conjugate=False):
    rows = left.shape[0] // 2
    a_real, a_imag, b_real, b_imag = left[:rows], left[rows:], right[:rows], right[rows:]
    if conjugate:
        real, imag = a_real * b_real + a_imag * b_imag, a_imag * b_real - a_real * b_imag
    else:
        real, imag = a_real * b_real - a_imag * b_imag, a_real * b_imag + a_imag * b_real
    return jnp.concatenate([real, imag], axis=0)


def filtered(raw, weights, s, at, blocks, size):
    now = weights[s, 0:1] * raw[pl.ds(at + 2 * blocks, size)]
    now = now + weights[s, 1:2] * raw[pl.ds(at + blocks, size)]
    return (now + weights[s, 2:3] * raw[pl.ds(at, size)]).astype(BF16).astype(F32)


def core_kernel(blocks, count, me_ref, group_ref, *refs):
    weights, fwd_ref, back_ref = refs[:3]
    msgs, swapped, refs = refs[3 : 3 + count], refs[3 + count], refs[4 + count :]
    outs, scratch = refs[:count], refs[count:]
    raw, sig, gate, grad, high, low, spec, turned, cot, conv, grads = scratch
    me, group = me_ref[0], group_ref[0]
    total = sig.shape[1]
    rows = total // blocks
    slab = total // count
    halo = (TAPS - 1) * blocks

    def weight(stream, tap):
        return weights[stream, tap : tap + 1]

    taken = 0
    for by, msg in zip(asking_order(count), msgs):
        start = pl.multiple_of((me ^ by) * slab, slab)
        for s in range(3):
            raw[s, pl.ds(halo + start, slab)] = msg[s * slab : (s + 1) * slab].astype(F32)
        grad[pl.ds(start, slab)] = msg[3 * slab : 4 * slab].astype(F32)
        if msg.shape[0] == 5 * slab:
            sig[group, pl.ds(start, slab)] = msg[4 * slab :].astype(F32)
            other = swapped[taken * slab : (taken + 1) * slab]
            sig[1 - group, pl.ds(start, slab)] = other.astype(F32)
            taken += 1
        else:
            for f in range(2):
                sig[f, pl.ds(start, slab)] = msg[(4 + f) * slab : (5 + f) * slab].astype(F32)
    for s in range(3):
        raw[s, 0:halo] = shift_blocks(raw[s, total : total + halo], blocks, 1)

    @pl.loop(0, total // slab)
    def _(step):
        base = pl.multiple_of(step * slab, slab)
        sig[2, pl.ds(base, slab)] = filtered(raw.at[0], weights, 0, base, blocks, slab)
        gate[pl.ds(base, slab)] = filtered(raw.at[1], weights, 1, base, blocks, slab)
        gate_two = filtered(raw.at[2], weights, 2, base, blocks, slab)
        sig[3, pl.ds(base, slab)] = gate_two * grad[pl.ds(base, slab)]

    work = Transforms(rows, fwd_ref, back_ref, high, low)

    def butterflies(row, signals):
        for s in signals:
            parts = [sig[s, spread(blocks, row, b)] for b in range(blocks)]
            work.store(parts, row, s * LANES)

    work.each_chunk(functools.partial(butterflies, signals=(0, 1)))
    steps = rows // CHUNK
    for j in range(max(blocks, steps)):
        if j < blocks:
            spec[j] = work.forward(j, 0, 2 * LANES)
        if j < steps:
            butterflies(j * CHUNK, (2, 3))

    def first_products(j):
        data = work.forward(j, 2 * LANES, 4 * LANES)
        left = product(data[:, :LANES], spec[j, :, :LANES])
        right = product(data[:, LANES:], spec[j, :, LANES:], True)
        turned[j] = work.backward(j, jnp.concatenate([left, right], axis=1))

    work.each_slot(first_products)

    def gates(row):
        first = work.blocks_of(turned, row, 0)
        gated_grad = work.blocks_of(turned, row, LANES)
        forward, backward = [], []
        for b in range(blocks):
            here = spread(blocks, row, b)
            gate_one = gate[here]
            cot[1, here] = (gated_grad[b] * first[b]).astype(BF16).astype(F32)
            forward.append(gate_one * first[b])
            backward.append(gate_one * gated_grad[b])
        work.store(forward, row, 0)
        work.store(backward, row, LANES)

    work.each_chunk(gates)

    def convolve(j):
        data = work.forward(j, 0, 2 * LANES)
        left = product(data[:, :LANES], spec[j, :, LANES:])
        right = product(data[:, LANES:], spec[j, :, :LANES], True)
        turned[j] = work.backward(j, jnp.concatenate([left, right], axis=1))

    work.each_slot(convolve)

    def last(row):
        second = work.blocks_of(turned, row, 0)
        value_grad = work.blocks_of(turned, row, LANES)
        for b in range(blocks):
            here = spread(blocks, row, b)
            conv[here] = second[b]
            cot[0, here] = value_grad[b].astype(BF16).astype(F32)

    work.each_chunk(last)
    for s in range(2):
        cot[s, total : total + halo] = shift_blocks(cot[s, 0:halo], blocks, -1)

    def finish(step, sums):
        base = pl.multiple_of(step * slab, slab)
        here = [cot[s, pl.ds(base, slab)] for s in range(2)]
        last = (grad[pl.ds(base, slab)] * conv[pl.ds(base, slab)]).astype(BF16).astype(F32)
        cot[2, pl.ds(base, slab)] = last
        here.append(last)
        for s in range(2):
            next_one = cot[s, pl.ds(base + blocks, slab)]
            next_two = cot[s, pl.ds(base + 2 * blocks, slab)]
            grads[s, pl.ds(base, slab)] = (
                weight(s, 0) * here[s] + weight(s, 1) * next_one + weight(s, 2) * next_two
            ).astype(BF16)
        added = []
        for s in range(3):
            for tap in range(TAPS):
                term = here[s] * raw[s, pl.ds(base + (TAPS - 1 - tap) * blocks, slab)]
                added.append(jnp.sum(term.reshape(slab // 8, 8, LANES), axis=0))
        return tuple(a + b for a, b in zip(sums, added))

    zeros = tuple(jnp.zeros((8, LANES), F32) for _ in range(3 * TAPS))
    sums = lax.fori_loop(0, total // slab, finish, zeros)
    cot[2, total : total + halo] = shift_blocks(cot[2, 0:halo], blocks, -1)
    scale = 1.0 / math.sqrt(total)
    tap_rows = [jnp.sum(part, axis=0, keepdims=True) * scale for part in sums]
    pad = jnp.zeros((TAP_ROWS - 3 * TAPS, LANES), F32)
    tap_block = jnp.concatenate(tap_rows + [pad], axis=0).astype(BF16)
    for k, by in enumerate(answering_order(count)):
        start = pl.multiple_of((me ^ by) * slab, slab)
        outs[k][0:slab] = conv[pl.ds(start, slab)].astype(BF16)
        for s in range(2):
            at = (s + 1) * slab
            outs[k][at : at + slab] = grads[s, pl.ds(start, slab)]
        at = 3 * slab
        now, prev_one, prev_two = (raw[2, pl.ds(start + j * blocks, halo)] for j in (2, 1, 0))
        gate_two = weight(2, 0) * now + weight(2, 1) * prev_one + weight(2, 2) * prev_two
        first = gate_two.astype(BF16).astype(F32) * conv[pl.ds(start, halo)]
        outs[k][at : at + halo] = first.astype(BF16)
        at += halo
        begin = start + slab - halo
        now, next_one, next_two = (cot[2, pl.ds(begin + j * blocks, halo)] for j in range(TAPS))
        end = weight(2, 0) * now + weight(2, 1) * next_one + weight(2, 2) * next_two
        outs[k][at : at + halo] = end.astype(BF16)
        at += halo
        outs[k][at:] = tap_block


def home_kernel(blocks, partners, me_ref, *refs):
    msgs = refs[:partners]
    stream_ref, grad_ref, taps_ref = refs[partners : partners + 3]
    layer_ref, grads_ref, tap_ref = refs[partners + 3 :]
    me = me_ref[0]
    slab = stream_ref.shape[0]
    halo = (TAPS - 1) * blocks
    rest = slab - halo
    for k, by in enumerate(answering_order(partners)):
        lanes = pl.ds(pl.multiple_of((me ^ by) * LANES, LANES), LANES)
        msg = msgs[k]
        conv = msg[0:slab].astype(F32)
        tap = [taps_ref[2, j : j + 1, lanes] for j in range(TAPS)]
        stream = stream_ref[:, lanes].astype(F32)
        gate = tap[0] * stream[halo:] + tap[1] * stream[blocks : blocks + rest]
        gate = (gate + tap[2] * stream[:rest]).astype(BF16).astype(F32)
        layer_ref[0:halo, lanes] = msg[3 * slab : 3 * slab + halo]
        layer_ref[halo:slab, lanes] = (gate * conv[halo:]).astype(BF16)
        cot = (grad_ref[:, lanes].astype(F32) * conv).astype(BF16).astype(F32)
        last = tap[0] * cot[:rest] + tap[1] * cot[blocks : blocks + rest] + tap[2] * cot[halo:]
        grads_ref[0 : 2 * slab, lanes] = msg[slab : 3 * slab]
        grads_ref[2 * slab : 3 * slab - halo, lanes] = last.astype(BF16)
        grads_ref[3 * slab - halo : 3 * slab, lanes] = msg[3 * slab + halo : 3 * slab + 2 * halo]
        block = msg[3 * slab + 2 * halo :].astype(F32)
        for s in range(3):
            tap_ref[s, :, lanes] = block[s * TAPS : (s + 1) * TAPS]


def asking_order(count):
    return [0, 4, 3, 2, 5, 6, 7, 1] if count == 8 else list(range(count))


def answering_order(count):
    return [0, 1, 2, 4, 3, 5, 7, 6] if count == 8 else list(range(count))


def filters_once(count, groups):
    return list(range(count // 2, count - 1)) if groups == 2 else []


def everyone(messages, order):
    count = len(messages)
    out = [messages[0]]
    for by, message in zip(order[1:], messages[1:]):
        out.append(lax.ppermute(message, "seq", [(i, i ^ by) for i in range(count)]))
    return out


def whole_specs(count):
    return [pl.BlockSpec(memory_space=pltpu.VMEM) for _ in range(count)]


def in_hbm(array):
    return pltpu.with_memory_space_constraint(array, pltpu.HBM)


def shape(*dims, dtype=BF16):
    return jax.ShapeDtypeStruct(dims, dtype)


def call(kernel, name, out_shape, in_specs, scratch=()):
    return pl.pallas_call(
        kernel,
        out_shape=out_shape,
        in_specs=in_specs,
        out_specs=whole_specs(len(out_shape)),
        scratch_shapes=list(scratch),
        compiler_params=pltpu.CompilerParams(vmem_limit_bytes=VMEM_LIMIT),
        name=name,
    )


def core_call(place, group, tables, messages, swapped, blocks):
    count = len(messages)
    slab = messages[0].shape[0] // 6
    total = slab * count
    spectrum = (blocks, 2 * total // blocks)
    halo = (TAPS - 1) * blocks
    return call(
        functools.partial(core_kernel, blocks, count),
        "core",
        [shape(3 * slab + 2 * halo + TAP_ROWS, LANES)] * count,
        [pl.BlockSpec(memory_space=pltpu.SMEM)] * 2 + whole_specs(count + 4),
        [
            pltpu.VMEM((3, halo + total, LANES), F32),
            pltpu.VMEM((4, total, LANES), F32),
            pltpu.VMEM((total, LANES), F32),
            pltpu.VMEM((total, LANES), F32),
            pltpu.VMEM((*spectrum, 4 * LANES), BF16),
            pltpu.VMEM((*spectrum, 4 * LANES), BF16),
            pltpu.VMEM((*spectrum, 2 * LANES), F32),
            pltpu.VMEM((*spectrum, 2 * LANES), F32),
            pltpu.VMEM((3, total + halo, LANES), F32),
            pltpu.VMEM((total, LANES), F32),
            pltpu.VMEM((2, total, LANES), BF16),
        ],
    )(place, group, *tables, *messages, swapped)


def short_local(streams, short_taps, long_filters, out_grad):
    count = lax.axis_size("seq")
    groups = lax.axis_size("group")
    place = lax.axis_index("seq").astype(jnp.int32)[None]
    group = lax.axis_index("group").astype(jnp.int32)[None]
    order = asking_order(count)
    once = filters_once(count, groups)
    _, local_rows, blocks, channels = streams.shape
    slab = local_rows * blocks
    flat_streams = streams.reshape(3 * slab, channels)
    flat_filters = long_filters.reshape(2 * slab, channels)
    flat_grad = out_grad.reshape(slab, channels)
    scalar = pl.BlockSpec(memory_space=pltpu.SMEM)
    anywhere = pl.BlockSpec(memory_space=pl.ANY)

    packed = call(
        pack_kernel,
        "pack",
        [shape((5 if by in once else 6) * slab, LANES) for by in order[1:]],
        [scalar] * 2 + [anywhere] * 3,
        [pltpu.SemaphoreType.DMA((3 * (count - 1),))],
    )(place, group, in_hbm(flat_streams), in_hbm(flat_filters), in_hbm(flat_grad))
    forward, back = transform_tables(blocks, local_rows * count)
    *tables, own = call(
        tables_kernel,
        "tables",
        [shape(3, TAPS, LANES, dtype=F32), shape(*forward.shape), shape(*back.shape)]
        + [shape(6 * slab, LANES)],
        [scalar] + [anywhere] * 7,
        [pltpu.SemaphoreType.DMA((6,))],
    )(
        place,
        packed[0],
        in_hbm(short_taps),
        in_hbm(jnp.asarray(forward)),
        in_hbm(jnp.asarray(back)),
        in_hbm(flat_streams),
        in_hbm(flat_filters),
        in_hbm(flat_grad),
    )
    messages = everyone([own, *packed], order)
    swapped = jnp.zeros((16, LANES), BF16)
    if once:
        halves = [message for by, message in zip(order, messages) if by in once]
        (mine,) = call(
            swap_kernel, "swap", [shape(len(once) * slab, LANES)], whole_specs(len(once))
        )(*halves)
        swapped = lax.ppermute(mine, "group", [(0, 1), (1, 0)])
    answers = core_call(place, group, tables, messages, swapped, blocks)
    returned = everyone(answers, answering_order(count))
    layer_out, stream_grads, tap_grads = call(
        functools.partial(home_kernel, blocks, count),
        "home",
        [
            shape(slab, channels),
            shape(3 * slab, channels),
            shape(3, TAPS, channels, dtype=F32),
        ],
        [scalar] + whole_specs(count + 3),
    )(place, *returned, flat_streams[2 * slab :], flat_grad, short_taps)
    return (
        layer_out.reshape(out_grad.shape),
        stream_grads.reshape(streams.shape),
        tap_grads,
    )


def shifted(value, axis, by):
    count = lax.axis_size(axis)
    return lax.ppermute(value, axis, [(i, (i + by) % count) for i in range(count)])


def complex_product(left_real, left_imag, right_real, right_imag):
    return (
        left_real * right_real - left_imag * right_imag,
        left_real * right_imag + left_imag * right_real,
    )


def conj_product(left_real, left_imag, right_real, right_imag):
    return (
        left_real * right_real + left_imag * right_imag,
        left_real * right_imag - left_imag * right_real,
    )


def long_local(streams, short_taps, long_filters, out_grad):
    seq_count = lax.axis_size("seq")
    seq_place = lax.axis_index("seq")
    local_rows = streams.shape[1]
    channels = streams.shape[3]
    block_rows = local_rows * seq_count
    full_length = 2 * block_rows * seq_count
    angle_unit = math.pi / full_length
    block_pos = jnp.arange(seq_count, dtype=jnp.int32)
    odd_slots = 2 * block_pos + 1
    local_index = seq_place * local_rows + jnp.arange(local_rows, dtype=jnp.int32)
    row_pos = jnp.arange(block_rows, dtype=jnp.int32)
    start_pos = block_pos[None, :, None] * block_rows + local_index[:, None, None]
    fwd_angle = (start_pos * odd_slots[None, None, :] % (2 * full_length)).astype(
        jnp.float32
    ) * angle_unit
    fwd_table = jnp.stack([jnp.cos(fwd_angle), -jnp.sin(fwd_angle)], axis=-1)
    inner_angle = (row_pos[:, None] * row_pos[None, :] % block_rows).astype(jnp.float32) * (
        2.0 * math.pi / block_rows
    )
    inner_cos = jnp.cos(inner_angle)
    inner_sin = jnp.sin(inner_angle)
    inner_table = jnp.stack(
        [jnp.stack([inner_cos, -inner_sin], axis=-1), jnp.stack([inner_sin, inner_cos], axis=-1)],
        axis=0,
    )
    back_num = (
        row_pos[None, :]
        * (4 * seq_count * row_pos[:, None] + 2 * seq_place + 1)
        % (2 * full_length)
    )
    back_angle = back_num.astype(jnp.float32) * angle_unit
    back_cos = jnp.cos(back_angle)
    back_sin = jnp.sin(back_angle)
    back_table = jnp.stack(
        [jnp.stack([back_cos, back_sin], axis=-1), jnp.stack([-back_sin, back_cos], axis=-1)],
        axis=0,
    )
    outer_angle = (block_pos[:, None] * odd_slots[None, :] % (4 * seq_count)).astype(
        jnp.float32
    ) * (math.pi / (2 * seq_count))
    outer_table = jnp.stack([jnp.cos(outer_angle).T, -jnp.sin(outer_angle).T], axis=0)

    def previous_rows(block):
        edge = shifted(block[:, -1:], "seq", 1)
        rolled = jnp.concatenate([jnp.zeros_like(edge[:, :, :1]), edge[:, :, :-1]], axis=2)
        edge = jnp.where(seq_place == 0, rolled, edge)
        return jnp.concatenate([edge, block[:, :-1]], axis=1)

    def next_rows(block):
        edge = shifted(block[:, :1], "seq", -1)
        rolled = jnp.concatenate([edge[:, :, 1:], jnp.zeros_like(edge[:, :, :1])], axis=2)
        edge = jnp.where(seq_place == seq_count - 1, rolled, edge)
        return jnp.concatenate([block[:, 1:], edge], axis=1)

    def spectra(signals):
        count = signals.shape[0]
        twisted = jnp.einsum("simc,imjr->srijc", signals, fwd_table, precision=HIGHEST_PRECISION)
        slotted = lax.all_to_all(twisted, "seq", split_axis=3, concat_axis=2, tiled=True)
        slotted = slotted.reshape(count, 2, block_rows, channels)
        spec = jnp.einsum("sric,rikq->sqkc", slotted, inner_table, precision=HIGHEST_PRECISION)
        return (spec[:, 0], spec[:, 1])

    def signals_back(real_spec, imag_spec):
        count = real_spec.shape[0]
        stacked = jnp.stack([real_spec, imag_spec], axis=1)
        turned = jnp.einsum("srkc,rkiq->sqic", stacked, back_table, precision=HIGHEST_PRECISION)
        turned = turned.reshape(count, 2, block_rows, 1, channels)
        parts = lax.all_to_all(turned, "seq", split_axis=2, concat_axis=3, tiled=True)
        rows_out = jnp.einsum("srijc,rjm->simc", parts, outer_table, precision=HIGHEST_PRECISION)
        return rows_out * (2.0 / full_length)

    def tap_weight(index):
        return short_taps[:, index][:, None, None, :]

    prev_one = previous_rows(streams)
    prev_two = previous_rows(prev_one)
    filtered = (
        tap_weight(0) * streams + tap_weight(1) * prev_one + tap_weight(2) * prev_two
    ).astype(jnp.bfloat16)
    value_stream = filtered[0].astype(jnp.float32)
    gate_one = filtered[1].astype(jnp.float32)
    gate_two = filtered[2].astype(jnp.float32)
    filters = long_filters.astype(jnp.float32)
    real_first, imag_first = spectra(jnp.stack([value_stream, filters[0]]))
    product_one = complex_product(real_first[0], imag_first[0], real_first[1], imag_first[1])
    first_conv = signals_back(product_one[0][None], product_one[1][None])[0]
    gated_first = gate_one * first_conv
    real_second, imag_second = spectra(jnp.stack([gated_first, filters[1]]))
    product_two = complex_product(real_second[0], imag_second[0], real_second[1], imag_second[1])
    second_conv = signals_back(product_two[0][None], product_two[1][None])[0]
    layer_out = (gate_two * second_conv).astype(jnp.bfloat16)
    cotangent = out_grad.astype(jnp.float32)
    back_two = cotangent * gate_two
    grad_two = cotangent * second_conv
    real_third, imag_third = spectra(back_two[None])
    filter_two_real, filter_two_imag = (real_second[1], imag_second[1])
    correlated_two = conj_product(filter_two_real, filter_two_imag, real_third[0], imag_third[0])
    grad_gated = signals_back(correlated_two[0][None], correlated_two[1][None])[0]
    grad_one = grad_gated * first_conv
    back_one = grad_gated * gate_one
    real_fourth, imag_fourth = spectra(back_one[None])
    filter_one_real, filter_one_imag = (real_first[1], imag_first[1])
    correlated_one = conj_product(filter_one_real, filter_one_imag, real_fourth[0], imag_fourth[0])
    grad_value = signals_back(correlated_one[0][None], correlated_one[1][None])[0]
    stream_cot = jnp.stack([grad_value, grad_one, grad_two]).astype(jnp.bfloat16)
    next_one = next_rows(stream_cot)
    next_two = next_rows(next_one)
    stream_grads = (
        tap_weight(0) * stream_cot + tap_weight(1) * next_one + tap_weight(2) * next_two
    ).astype(jnp.bfloat16)
    cot_float = stream_cot.astype(jnp.float32)
    tap_terms = jnp.stack(
        [
            jnp.sum(cot_float * streams, axis=(1, 2)),
            jnp.sum(cot_float * prev_one, axis=(1, 2)),
            jnp.sum(cot_float * prev_two, axis=(1, 2)),
        ],
        axis=1,
    )
    tap_total = lax.psum(tap_terms, "seq")
    return (layer_out, stream_grads, tap_total * (1.0 / math.sqrt(block_rows * seq_count)))


def local(streams, short_taps, long_filters, out_grad):
    count = lax.axis_size("seq")
    _, local_rows, blocks, channels = streams.shape
    rows = local_rows * count
    fits = (
        channels == LANES * count
        and count & (count - 1) == 0
        and blocks == 8
        and rows == LANES
        and local_rows >= TAPS - 1
    )
    work = short_local if fits else long_local
    return work(streams, short_taps, long_filters, out_grad)


def solution(mesh):
    in_specs = (
        P(None, "seq", "group", "tensor"),
        P(None, None, "tensor"),
        P(None, "seq", None, "tensor"),
        P("seq", "group", "tensor"),
    )
    out_specs = (
        P("seq", "group", "tensor"),
        P(None, "seq", "group", "tensor"),
        P("group", None, "tensor"),
    )
    return jax.shard_map(local, mesh=mesh, in_specs=in_specs, out_specs=out_specs, check_vma=False)
```
